32 devices in a mesh: seq: 8 (over y, x, core), mp: 4 (over z).
Axes of the slice: x: 2, y: 2, z: 4, core: 2. Of those that a mesh axis runs over, the one named last changes fastest.
Arguments:
- tokens: float32 [8192, 2, 2048], P(('seq', 'mp')), may hold values from -6 to 6
- norm1_gain: float32 [2048], replicated, may hold values from 0.5 to 1.5
- w_mix_in: bfloat16 [2048, 4, 2048], P(None, None, 'mp'), may hold values from -0.125 to 0.125
- forget_gap: float32 [16, 128], P('mp'), may hold values from 0.00012207031 to 0.1
- group_gain: float32 [16, 128], P('mp'), may hold values from 0.5 to 1.5
- w_mix_out: bfloat16 [16, 128, 2048], replicated, may hold values from -0.125 to 0.125
- norm2_gain: float32 [2048], replicated, may hold values from 0.5 to 1.5
- w_gate_up: bfloat16 [2048, 2, 5632], P(None, None, 'mp'), may hold values from -0.125 to 0.125
- w_down: bfloat16 [5632, 2048], P('mp'), may hold values from -0.078125 to 0.078125
- doc_lengths: int32 [2, 4], replicated, may hold values from 1 to 7169, 8192 in all within a row
- out_cotangent: float32 [8192, 2, 2048], P('seq'), may hold values from -6 to 6
Outputs:
- layer_out: float32 [8192, 2, 2048], P(('seq', 'mp'))
- tokens_grad: float32 [8192, 2, 2048], P(('seq', 'mp'))
- norm1_gain_grad: float32 [2048], P(('seq', 'mp'))
- w_mix_in_grad: float32 [2048, 4, 2048], P('seq', None, 'mp')
- forget_gap_grad: float32 [16, 128], P('mp', 'seq')
- group_gain_grad: float32 [16, 128], P('mp', 'seq')
- w_mix_out_grad: float32 [16, 128, 2048], P('mp', 'seq')
- norm2_gain_grad: float32 [2048], P(('seq', 'mp'))
- w_gate_up_grad: float32 [2048, 2, 5632], P('seq', None, 'mp')
- w_down_grad: float32 [5632, 2048], P('mp', 'seq')
The draws below stay inside these ranges and needn't reach their ends.
Inputs may be any that keep to these rules, and one draw needn't show every extreme that they name: `doc_lengths`: in each pack the 4 lengths add up to 8192, and the longest is exactly 7169.
All inputs are finite; a program needn't handle non-finite values.
Results may differ from the reference program's by a relative error of at most 0.025.
The reference program's roundings to bfloat16 on the way count: a program that leaves them out, or rounds other values in their place, can miss the bound.
Values may be sent and summed in bfloat16 or wider, within the bound.
A program may use at most 384 MiB of HBM per device.

```python
import math
import jax
import jax.numpy as jnp
import numpy as np
from jax import lax

D = 2048
HEADS = 16
HD = 128
FF = 5632
BLOCK = 128
PACKS = 2
DOCS = 4
RUN = 1024
SPAN = 8192


def draw_forget_gap(key, part):
    key = jax.random.fold_in(key, 11)
    shift_key, jitter_key = jax.random.split(key)
    shifts = jax.random.randint(shift_key, (HEADS, 1), 0, HD)
    strata = (jnp.arange(HD, dtype=jnp.int32)[None, :] + shifts) % HD
    jitter = jax.random.uniform(jitter_key, (HEADS, HD), jnp.float32, 0.02, 0.98)
    fraction = (strata.astype(jnp.float32) + jitter) / HD
    low_log = jnp.log(1.0 / SPAN)
    high_log = jnp.log(0.1)
    return jnp.exp(low_log + fraction * (high_log - low_log)).astype(jnp.float32)


def shard_levels(key, shape, cuts, least, high):
    factor_of = 1.0
    for axis_at, shards_of in cuts:
        draws = jax.random.uniform(jax.random.fold_in(jax.random.fold_in(key, 6), axis_at), (shards_of,), jnp.float32, least / len(cuts), high / len(cuts))
        factor_of = factor_of * jnp.repeat(jnp.exp(draws), shape[axis_at] // shards_of).reshape((-1,) + (1,) * (len(shape) - 1 - axis_at))
    return factor_of


def split_up(amount, total, limit, lean):
    weights = [(1 << 20) // math.isqrt(standing ** lean) + 1 for standing in range(2, amount + 1)]
    rest, counts = total - limit - (amount - 1), [1] * (amount - 1)
    while rest > 0:
        free = [i for i in range(amount - 1) if counts[i] < limit]
        whole, budget = sum([weights[i] for i in free]), rest
        for i in free:
            more = min(limit - counts[i], max(1, budget * weights[i] // whole), rest)
            counts[i] = counts[i] + more
            rest = rest - more
    return np.array([limit] + counts)


def uneven(stream_key, count, total, most, slope):
    if count == 2:
        one = jax.random.randint(stream_key, (), max(1, total - most), min(most, total - 1) + 1)
        return jnp.stack([one, total - one])
    sizes = jnp.asarray(split_up(count, total, most, slope), jnp.int32)
    twos = (count - 1) // 2
    donor, receiver = sizes[1:1 + 2 * twos:2], sizes[2:2 + 2 * twos:2]
    margin = jnp.minimum(donor - 1, most - receiver)
    moved = jax.random.randint(jax.random.fold_in(stream_key, 1), (twos,), 0, 1 << 20) % (margin + 1)
    sizes = sizes.at[1:1 + 2 * twos:2].set(donor - moved).at[2:2 + 2 * twos:2].set(receiver + moved)
    return sizes[jax.random.permutation(jax.random.fold_in(stream_key, 2), count)]


def scatter_about(stream_key, extent, width, reach, shards=(), kind=jnp.bfloat16):
    drawn = width * jax.random.normal(stream_key, extent, jnp.float32)
    if shards:
        drawn = drawn * shard_levels(stream_key, extent, shards, -0.22, 0.18)
    return jnp.clip(drawn, -reach, reach).astype(kind)


def setup_inputs(seed: int = 0) -> dict:
    key_of = jax.random.split(jax.random.key(seed), 12)
    return {
        "tokens": scatter_about(key_of[0], (SPAN, PACKS, D), 1.0, 6.0, ((0, 32),), jnp.float32),
        "norm1_gain": jnp.clip(1.0 + 0.1 * jax.random.normal(key_of[1], (D,), jnp.float32), 0.5, 1.5),
        "w_mix_in": scatter_about(key_of[2], (D, 4, HEADS * HD), D ** -0.5, 0.125, ((2, 4),)),
        "forget_gap": draw_forget_gap(jax.random.fold_in(key_of[11], 71), 0),
        "group_gain": jnp.clip(1.0 + 0.1 * jax.random.normal(key_of[4], (HEADS, HD), jnp.float32), 0.5, 1.5),
        "w_mix_out": scatter_about(key_of[5], (HEADS, HD, D), (HEADS * HD) ** -0.5, 0.125),
        "norm2_gain": jnp.clip(1.0 + 0.1 * jax.random.normal(key_of[6], (D,), jnp.float32), 0.5, 1.5),
        "w_gate_up": scatter_about(key_of[7], (D, 2, FF), D ** -0.5, 0.125, ((2, 4),)),
        "w_down": scatter_about(key_of[8], (FF, D), FF ** -0.5, 0.078125, ((0, 4),)),
        "doc_lengths": jax.vmap(lambda own: uneven(own, DOCS, SPAN, SPAN - RUN + 1, 1))(jax.random.split(key_of[9], PACKS)).reshape((PACKS, DOCS)).astype(jnp.int32),
        "out_cotangent": scatter_about(key_of[10], (SPAN, PACKS, D), 1.0, 6.0, ((0, 8),), jnp.float32),
    }


EPSILON = 1e-06
PRECISE = lax.Precision.HIGHEST

@jax.custom_vjp
def low(v):
    return lax.optimization_barrier(v.astype(jnp.bfloat16)).astype(jnp.float32)

@jax.custom_vjp
def low_back(v):
    return v

def low_keep(v):
    return (low(v), None)

def low_pass(kept, grad):
    return (grad,)

def back_keep(v):
    return (v, None)

def back_low(kept, grad):
    return (low(grad),)
low.defvjp(low_keep, low_pass)
low_back.defvjp(back_keep, back_low)

def norm_rows(signal, gain_vec):
    scaling = lax.rsqrt(lax.optimization_barrier(jnp.mean(signal * signal, axis=-1, keepdims=True)) + EPSILON)
    return signal * scaling * gain_vec

def doc_index(doc_lengths, positions):
    doc_ends = jnp.cumsum(doc_lengths, axis=1).astype(jnp.int32)
    return lax.optimization_barrier(jnp.sum((positions[:, None, None] >= doc_ends[None, :, :]).astype(jnp.int32), axis=2))

def block_step(state_now, element):
    queries, key_vec, values_in, log_forget, doc_ids, previous = element
    length = queries.shape[0]
    row_index = lax.broadcasted_iota(jnp.int32, (length, length), 0)
    col_index = lax.broadcasted_iota(jnp.int32, (length, length), 1)
    cumulated = jnp.cumsum(log_forget, axis=0)
    last_sum = cumulated[-1]
    q_tilde = queries * jnp.exp(cumulated)
    k_tilde = key_vec * jnp.exp(-cumulated)
    at_end = (doc_ids == doc_ids[-1][None, :]).astype(jnp.float32)[:, :, None, None]
    k_hat = key_vec * jnp.exp(last_sum[None] - cumulated) * at_end
    same_doc = doc_ids[:, None, :] == doc_ids[None, :, :]
    visible = jnp.transpose(same_doc & (row_index >= col_index)[:, :, None], (2, 0, 1))[:, None]
    scores = jnp.einsum('ishk,jshk->shij', q_tilde, k_tilde, precision=PRECISE)
    mixing = jnp.where(visible, scores, 0.0)
    inside = jnp.einsum('shij,jshv->ishv', mixing, values_in, precision=PRECISE)
    enters = (doc_ids == previous[None, :]).astype(jnp.float32)[:, :, None, None]
    carried = jnp.einsum('ishk,shkv->ishv', q_tilde * enters, state_now, precision=PRECISE)
    local_sum = jnp.einsum('jshk,jshv->shkv', k_hat, values_in, precision=PRECISE)
    alive_end = (doc_ids[-1] == previous).astype(jnp.float32)[:, None, None]
    decays = jnp.exp(last_sum) * alive_end
    return (decays[..., None] * state_now + local_sum, inside + carried)

def recurrence(queries, key_vec, values_in, log_forget, doc_ids):
    span_len, pack_count, head_count, head_size = queries.shape
    blocks = span_len // BLOCK

    def to_blocks(array_in):
        return array_in.reshape((blocks, BLOCK) + array_in.shape[1:])
    id_blocks = doc_ids.reshape(blocks, BLOCK, pack_count)
    previous = jnp.concatenate([jnp.full((1, pack_count), -1, jnp.int32), id_blocks[:-1, -1]], axis=0)
    initial = jnp.zeros((pack_count, head_count, head_size, head_size), queries.dtype)
    final_state, outputs = lax.scan(jax.checkpoint(block_step), initial, (to_blocks(queries), to_blocks(key_vec), to_blocks(values_in), to_blocks(log_forget), id_blocks, previous))
    return outputs.reshape(span_len, pack_count, head_count, head_size)

def layer(tokens, norm1_gain, w_mix_in, forget_gap, group_gain, w_mix_out, norm2_gain, w_gate_up, w_down, doc_ids):
    channels = HEADS * HD
    shape_heads = (SPAN, PACKS, HEADS, HD)
    normed = low(norm_rows(tokens, norm1_gain))
    projected = jnp.einsum('tsd,dkc->tskc', normed, w_mix_in, precision=PRECISE)
    queries = low(low_back(projected[:, :, 0]))
    forget_in = low_back(projected[:, :, 1])
    values_in = low(low_back(projected[:, :, 2]))
    gate_in = low_back(projected[:, :, 3])
    gap_gate = forget_gap.reshape(channels) * jax.nn.sigmoid(-forget_in)
    key_vec = low(gap_gate)
    log_forget = jnp.log1p(-gap_gate)
    mixed = recurrence(queries.reshape(shape_heads), key_vec.reshape(shape_heads), values_in.reshape(shape_heads), log_forget.reshape(shape_heads), doc_ids)
    gated_out = mixed * jax.nn.silu(gate_in.reshape(shape_heads))
    heads_out = low(low_back(norm_rows(gated_out, group_gain))).reshape(SPAN, PACKS, channels)
    mix_out = low_back(jnp.einsum('tsc,cd->tsd', heads_out, w_mix_out.reshape(channels, D), precision=PRECISE))
    hidden = tokens + mix_out
    normed_two = low(norm_rows(hidden, norm2_gain))
    gate_up = jnp.einsum('tsd,dkf->tskf', normed_two, w_gate_up, precision=PRECISE)
    activation = low(jax.nn.silu(low_back(gate_up[:, :, 0])) * low_back(gate_up[:, :, 1]))
    ffn_out = low_back(jnp.einsum('tsf,fd->tsd', activation, w_down, precision=PRECISE))
    return hidden + ffn_out

def reference(tokens, norm1_gain, w_mix_in, forget_gap, group_gain, w_mix_out, norm2_gain, w_gate_up, w_down, doc_lengths, out_cotangent):
    doc_ids = doc_index(doc_lengths, jnp.arange(SPAN, dtype=jnp.int32))
    floats = tuple((array_in.astype(jnp.float32) for array_in in (tokens, norm1_gain, w_mix_in, forget_gap, group_gain, w_mix_out, norm2_gain, w_gate_up, w_down)))

    def apply_layer(*inputs):
        return layer(*inputs, doc_ids)
    layer_out, pullback = jax.vjp(apply_layer, *floats)
    gradients = pullback(out_cotangent.astype(jnp.float32))
    return (layer_out, gradients[0], gradients[1], gradients[2], gradients[3], gradients[4], gradients[5], gradients[6], gradients[7], gradients[8])
```

```python
import functools

import jax
import jax.numpy as jnp
from jax import lax
from jax.experimental import pallas as pl
from jax.experimental.pallas import tpu as pltpu
from jax.sharding import PartitionSpec as P

BLOCK = 128


EPSILON = 1e-06
PRECISE = lax.Precision.HIGHEST


def entering(x, axis, combine, identity, reverse):
    length, index = (lax.axis_size(axis), lax.axis_index(axis))
    everything = jax.tree.map(
        lambda part, kind: lax.all_gather(part.astype(kind), axis), x, (jnp.bfloat16, jnp.bfloat16)
    )
    start = jax.tree.map(
        lambda part, zero: jnp.broadcast_to(jnp.asarray(zero, part.dtype), part.shape), x, identity
    )

    def turn(k, before):
        at = length - 1 - k if reverse else k
        reached = at > index if reverse else at < index
        new = combine(
            before, jax.tree.map(lambda part, own: part[at].astype(own.dtype), everything, x)
        )
        return jax.tree.map(lambda a, b: jnp.where(reached, a, b), new, before)

    return lax.fori_loop(0, length, turn, start)


def rounded(signal):
    return lax.optimization_barrier(signal.astype(jnp.bfloat16)).astype(jnp.float32)


def rms_scale(signal):
    return lax.rsqrt(jnp.mean(signal * signal, axis=-1, keepdims=True) + EPSILON)


def rms_back(gradient, signal, scaling, gain_vec):
    weighted = gradient * gain_vec
    inner_sum = jnp.mean(weighted * signal, axis=-1, keepdims=True)
    return scaling * weighted - signal * (scaling * scaling * scaling) * inner_sum


def silu_slope(signal):
    sigma_val = jax.nn.sigmoid(signal)
    return sigma_val * (1.0 + signal * (1.0 - sigma_val))


def doc_index(doc_lengths, positions):
    doc_ends = jnp.stack(
        [jnp.sum(doc_lengths[:, : k + 1], axis=1) for k in range(doc_lengths.shape[1])], axis=1
    )
    return jnp.sum((positions[:, None, None] >= doc_ends[None, :, :]).astype(jnp.int32), axis=2)


def chain_combine(earlier, later_part):
    return (earlier[0] * later_part[0], later_part[0][..., None] * earlier[1] + later_part[1])


def block_tables(log_forget, doc_ids, previous):
    length = log_forget.shape[1]
    row_index = lax.broadcasted_iota(jnp.int32, (length, length), 0)
    col_index = lax.broadcasted_iota(jnp.int32, (length, length), 1)
    lower_ones = (row_index >= col_index).astype(jnp.float32)
    cumulated = jnp.einsum("ij,njshk->nishk", lower_ones, log_forget, precision=PRECISE)
    last_sum = cumulated[:, -1]
    same_doc = doc_ids[:, :, None, :] == doc_ids[:, None, :, :]
    visible = jnp.transpose(same_doc & (row_index >= col_index)[None, :, :, None], (0, 3, 1, 2))[
        :, :, None
    ]
    enters = (doc_ids == previous[:, None, :]).astype(jnp.float32)[..., None, None]
    at_end = (doc_ids == doc_ids[:, -1:, :]).astype(jnp.float32)[..., None, None]
    alive_end = (doc_ids[:, -1] == previous).astype(jnp.float32)[..., None, None]
    decays = jnp.exp(last_sum) * alive_end
    return (lower_ones, cumulated, last_sum, visible, enters, at_end, decays)


def block_factors(queries, key_vec, cumulated, last_sum, at_end):
    q_tilde = queries * jnp.exp(cumulated)
    k_tilde = key_vec * jnp.exp(-cumulated)
    k_hat = key_vec * jnp.exp(last_sum[:, None] - cumulated) * at_end
    return (q_tilde, k_tilde, k_hat)


def recur_forward(queries, key_vec, values_in, log_forget, doc_ids, previous):
    lower_ones, cumulated, last_sum, visible, enters, at_end, decays = block_tables(
        log_forget, doc_ids, previous
    )
    q_tilde, k_tilde, k_hat = block_factors(queries, key_vec, cumulated, last_sum, at_end)
    scores = jnp.einsum("nishk,njshk->nshij", q_tilde, k_tilde, precision=PRECISE)
    mixing = jnp.where(visible, scores, 0.0)
    inside = jnp.einsum("nshij,njshv->nishv", mixing, values_in, precision=PRECISE)
    local_sum = jnp.einsum("njshk,njshv->nshkv", k_hat, values_in, precision=PRECISE)

    def advance(carried, element):
        state_now, product = carried
        factor, addend = element
        return ((factor[..., None] * state_now + addend, product * factor), (state_now, product))

    zero_state = jnp.zeros(local_sum.shape[1:], jnp.float32)
    unit_decay = jnp.ones(decays.shape[1:], jnp.float32)
    (run_state, run_decay), (prefix_state, prefix_decay) = lax.scan(
        advance, (zero_state, unit_decay), (decays, local_sum)
    )
    incoming = entering(
        (run_decay, run_state), "seq", chain_combine, (unit_decay, zero_state), False
    )[1]
    start_state = prefix_state + prefix_decay[..., None] * incoming[None]
    carried_in = jnp.einsum("nishk,nshkv->nishv", q_tilde * enters, start_state, precision=PRECISE)
    return (inside + carried_in, start_state)


def recur_backward(
    queries, key_vec, values_in, log_forget, doc_ids, previous, start_state, grad_out
):
    lower_ones, cumulated, last_sum, visible, enters, at_end, decays = block_tables(
        log_forget, doc_ids, previous
    )
    q_tilde, k_tilde, k_hat = block_factors(queries, key_vec, cumulated, last_sum, at_end)
    scores = jnp.einsum("nishk,njshk->nshij", q_tilde, k_tilde, precision=PRECISE)
    mixing = jnp.where(visible, scores, 0.0)
    own_term = jnp.einsum("nishk,nishv->nshkv", q_tilde * enters, grad_out, precision=PRECISE)

    def retreat(carried, element):
        running, product = carried
        factor, addend = element
        return ((addend + factor[..., None] * running, product * factor), (running, product))

    zero_state = jnp.zeros(own_term.shape[1:], jnp.float32)
    unit_decay = jnp.ones(decays.shape[1:], jnp.float32)
    (run_grad, run_decay), (after_sum, after_decay) = lax.scan(
        retreat, (zero_state, unit_decay), (decays, own_term), reverse=True
    )
    outgoing = entering(
        (run_decay, run_grad), "seq", chain_combine, (unit_decay, zero_state), True
    )[1]
    next_grad = after_sum + after_decay[..., None] * outgoing[None]
    grad_mixing = jnp.where(
        visible, jnp.einsum("nishv,njshv->nshij", grad_out, values_in, precision=PRECISE), 0.0
    )
    grad_qt = jnp.einsum("nshij,njshk->nishk", grad_mixing, k_tilde, precision=PRECISE)
    grad_qt = grad_qt + jnp.einsum(
        "nishv,nshkv->nishk", grad_out * enters, start_state, precision=PRECISE
    )
    grad_kt = jnp.einsum("nshij,nishk->njshk", grad_mixing, q_tilde, precision=PRECISE)
    grad_values = jnp.einsum("nshij,nishv->njshv", mixing, grad_out, precision=PRECISE)
    grad_values = grad_values + jnp.einsum(
        "njshk,nshkv->njshv", k_hat, next_grad, precision=PRECISE
    )
    grad_khat = jnp.einsum("njshv,nshkv->njshk", values_in, next_grad, precision=PRECISE) * at_end
    grad_decay = jnp.sum(next_grad * start_state, axis=-1)
    grad_queries = grad_qt * jnp.exp(cumulated)
    grad_keys = grad_kt * jnp.exp(-cumulated) + grad_khat * jnp.exp(last_sum[:, None] - cumulated)
    grad_cum = grad_qt * q_tilde - grad_kt * k_tilde - grad_khat * k_hat
    grad_last = jnp.sum(grad_khat * k_hat, axis=1) + grad_decay * decays
    grad_log = (
        jnp.einsum("it,nishk->ntshk", lower_ones, grad_cum, precision=PRECISE) + grad_last[:, None]
    )
    return (grad_queries, grad_keys, grad_values, grad_log)


def generic_device(
    tokens,
    norm1_gain,
    w_mix_in,
    forget_gap,
    group_gain,
    w_mix_out,
    norm2_gain,
    w_gate_up,
    w_down,
    doc_lengths,
    out_cotangent,
):
    mp_count = lax.axis_size("mp")
    rows_dev, pack_count, model_width = tokens.shape
    run_length = rows_dev * mp_count
    blocks = run_length // BLOCK
    local_heads, head_size = forget_gap.shape
    local_chans = local_heads * head_size
    local_ff = w_gate_up.shape[2]
    mp_index = lax.axis_index("mp")
    run_start = lax.axis_index("seq") * run_length
    positions = run_start - 1 + jnp.arange(run_length + 1, dtype=jnp.int32)
    all_ids = doc_index(doc_lengths, positions)
    doc_ids = all_ids[1:].reshape(blocks, BLOCK, pack_count)
    previous = all_ids[0:run_length:BLOCK]
    shape_blocks = (blocks, BLOCK, pack_count, local_heads, head_size)
    shape_heads = (run_length, pack_count, local_heads, head_size)
    shape_flat = (run_length, pack_count, local_chans)
    scale_one = rms_scale(tokens)
    normed = (tokens * scale_one * norm1_gain).astype(jnp.bfloat16)
    in_flat = w_mix_in.reshape(model_width, 4 * local_chans)
    shard_rows = lax.all_gather(normed, "mp", axis=0, tiled=True)
    normed_all = shard_rows
    projected = jnp.einsum("tsd,dc->tsc", shard_rows, in_flat, preferred_element_type=jnp.float32)
    pre_query = projected[..., :local_chans]
    pre_forget = projected[..., local_chans : 2 * local_chans]
    pre_value = projected[..., 2 * local_chans : 3 * local_chans]
    pre_gate = projected[..., 3 * local_chans :]
    open_gate = jax.nn.sigmoid(-pre_forget)
    gap_gate = forget_gap.reshape(local_chans) * open_gate
    queries = rounded(pre_query).reshape(shape_blocks)
    key_vec = rounded(gap_gate).reshape(shape_blocks)
    values_in = rounded(pre_value).reshape(shape_blocks)
    log_forget = jnp.log1p(-gap_gate).reshape(shape_blocks)
    mixed, start_state = recur_forward(queries, key_vec, values_in, log_forget, doc_ids, previous)
    mixed = mixed.reshape(shape_flat)
    gate_act = jax.nn.silu(pre_gate)
    gated_four = (mixed * gate_act).reshape(shape_heads)
    scale_group = rms_scale(gated_four)
    heads_out = (gated_four * scale_group * group_gain).astype(jnp.bfloat16).reshape(shape_flat)
    heads_tok = lax.all_to_all(heads_out, "mp", split_axis=0, concat_axis=2, tiled=True)
    out_flat = w_mix_out.reshape(-1, model_width)
    hidden = tokens + jnp.einsum(
        "tsc,cd->tsd", heads_tok, out_flat, preferred_element_type=jnp.float32
    )
    scale_two = rms_scale(hidden)
    normed_two = (hidden * scale_two * norm2_gain).astype(jnp.bfloat16)
    ffn_flat = w_gate_up.reshape(model_width, 2 * local_ff)
    shard_rows = lax.all_gather(normed_two, "mp", axis=0, tiled=True)
    gate_up = jnp.einsum("tsd,dc->tsc", shard_rows, ffn_flat, preferred_element_type=jnp.float32)
    pre_gate_two = gate_up[..., :local_ff]
    pre_up = gate_up[..., local_ff:]
    silu_two = jax.nn.silu(pre_gate_two)
    activation = (silu_two * pre_up).astype(jnp.bfloat16)
    partial_value = activation
    ffn_sum = lax.psum_scatter(
        jnp.einsum("tsf,fd->tsd", partial_value, w_down, preferred_element_type=jnp.float32).astype(
            jnp.bfloat16
        ),
        "mp",
        scatter_dimension=0,
        tiled=True,
    ).astype(jnp.float32)
    layer_out = hidden + ffn_sum
    cot_low = out_cotangent.astype(jnp.bfloat16)
    cot_own = lax.dynamic_slice_in_dim(out_cotangent, mp_index * rows_dev, rows_dev, 0)
    down_part = jnp.einsum("tsf,tsd->fd", activation, cot_low, preferred_element_type=jnp.float32)
    grad_act = jnp.einsum("tsd,fd->tsf", cot_low, w_down, preferred_element_type=jnp.float32)
    grad_gate_two = grad_act * pre_up * silu_slope(pre_gate_two)
    grad_up = grad_act * silu_two
    grad_gate_up = jnp.concatenate([grad_gate_two, grad_up], axis=-1).astype(jnp.bfloat16)
    gate_up_part = jnp.einsum(
        "tsd,tsc->dc", shard_rows, grad_gate_up, preferred_element_type=jnp.float32
    )
    gate_up_part = gate_up_part.reshape(model_width, 2, local_ff)
    partial_value = grad_gate_up
    grad_normed_two = lax.psum_scatter(
        jnp.einsum(
            "tsc,dc->tsd", partial_value, ffn_flat, preferred_element_type=jnp.float32
        ).astype(jnp.bfloat16),
        "mp",
        scatter_dimension=0,
        tiled=True,
    ).astype(jnp.float32)
    norm2_part = jnp.sum(grad_normed_two * hidden * scale_two, axis=(0, 1))
    grad_hidden = cot_own + rms_back(grad_normed_two, hidden, scale_two, norm2_gain)
    grad_mix = grad_hidden.astype(jnp.bfloat16)
    out_part = jnp.einsum("tsc,tsd->cd", heads_tok, grad_mix, preferred_element_type=jnp.float32)
    grad_tok = jnp.einsum(
        "tsd,cd->tsc", grad_mix, out_flat, preferred_element_type=jnp.float32
    ).astype(jnp.bfloat16)
    grad_heads = lax.all_to_all(grad_tok, "mp", split_axis=2, concat_axis=0, tiled=True).astype(
        jnp.float32
    )
    grad_four = grad_heads.reshape(shape_heads)
    group_part = jnp.sum(grad_four * gated_four * scale_group, axis=(0, 1))
    grad_gated = rms_back(grad_four, gated_four, scale_group, group_gain).reshape(shape_flat)
    grad_mixed = grad_gated * gate_act
    grad_gate_in = grad_gated * mixed * silu_slope(pre_gate)
    grad_queries, grad_keys, grad_values, grad_log = recur_backward(
        queries,
        key_vec,
        values_in,
        log_forget,
        doc_ids,
        previous,
        start_state,
        grad_mixed.reshape(shape_blocks),
    )
    grad_gap = grad_keys.reshape(shape_flat) - grad_log.reshape(shape_flat) / (1.0 - gap_gate)
    gap_part = jnp.sum(grad_gap * open_gate, axis=(0, 1)).reshape(local_heads, head_size)
    grad_forget_in = -grad_gap * gap_gate * (1.0 - open_gate)
    grad_projected = jnp.concatenate(
        [
            grad_queries.reshape(shape_flat),
            grad_forget_in,
            grad_values.reshape(shape_flat),
            grad_gate_in,
        ],
        axis=-1,
    ).astype(jnp.bfloat16)
    mix_in_part = jnp.einsum(
        "tsd,tsc->dc", normed_all, grad_projected, preferred_element_type=jnp.float32
    )
    mix_in_part = mix_in_part.reshape(model_width, 4, local_chans)
    partial_value = grad_projected
    grad_normed = lax.psum_scatter(
        jnp.einsum(
            "tsc,dc->tsd", partial_value, in_flat, preferred_element_type=jnp.float32
        ).astype(jnp.bfloat16),
        "mp",
        scatter_dimension=0,
        tiled=True,
    ).astype(jnp.float32)
    norm1_part = jnp.sum(grad_normed * tokens * scale_one, axis=(0, 1))
    tokens_grad = grad_hidden + rms_back(grad_normed, tokens, scale_one, norm1_gain)
    seq_count = lax.axis_size("seq")
    arranged = out_part.reshape(
        mp_count, local_heads, seq_count, head_size // seq_count, model_width
    )
    arranged = jnp.transpose(arranged, (2, 0, 1, 3, 4)).reshape(
        seq_count * mp_count * local_heads, head_size // seq_count, model_width
    )
    mix_in_grad, gate_up_grad, down_grad, group_grad, gap_grad = (
        lax.psum_scatter(
            mix_in_part.astype(jnp.bfloat16), "seq", scatter_dimension=0, tiled=True
        ).astype(jnp.float32),
        lax.psum_scatter(
            gate_up_part.astype(jnp.bfloat16), "seq", scatter_dimension=0, tiled=True
        ).astype(jnp.float32),
        lax.psum_scatter(
            down_part.astype(jnp.bfloat16), "seq", scatter_dimension=1, tiled=True
        ).astype(jnp.float32),
        lax.psum_scatter(
            group_part.astype(jnp.bfloat16), "seq", scatter_dimension=1, tiled=True
        ).astype(jnp.float32),
        lax.psum_scatter(
            gap_part.astype(jnp.bfloat16), "seq", scatter_dimension=1, tiled=True
        ).astype(jnp.float32),
    )
    mix_out_grad, norm1_grad, norm2_grad = (
        lax.psum_scatter(arranged, ("seq", "mp"), scatter_dimension=0, tiled=True),
        lax.psum_scatter(norm1_part, ("seq", "mp"), scatter_dimension=0, tiled=True),
        lax.psum_scatter(norm2_part, ("seq", "mp"), scatter_dimension=0, tiled=True),
    )
    return (
        layer_out,
        tokens_grad,
        norm1_grad,
        mix_in_grad,
        gap_grad,
        group_grad,
        mix_out_grad,
        norm2_grad,
        gate_up_grad,
        down_grad,
    )


F32 = jnp.float32
BF16 = jnp.bfloat16


def mm(a, b, dims=((1,), (0,))):
    return lax.dot_general(a, b, (dims, ((), ())), preferred_element_type=F32)


NN, NT, TN = ((1,), (0,)), ((1,), (1,)), ((0,), (0,))


def split_two(value):
    high = value.astype(BF16)
    return high, (value - high.astype(F32)).astype(BF16)


def triangle(length, upper):
    row = lax.broadcasted_iota(jnp.int32, (length, length), 0)
    col = lax.broadcasted_iota(jnp.int32, (length, length), 1)
    return jnp.where((row <= col) if upper else (row >= col), 1.0, 0.0).astype(BF16)


def ids_of(lens, pack, positions):
    total, ids = 0, jnp.zeros_like(positions)
    for k in range(lens.shape[1]):
        total = total + lens[pack, k]
        ids = ids + jnp.where(positions >= total, 1, 0)
    return ids


def block_docs(lens, pack, base, length):
    col = ids_of(lens, pack, base + lax.broadcasted_iota(jnp.int32, (length, 1), 0))
    row = ids_of(lens, pack, base + lax.broadcasted_iota(jnp.int32, (1, length), 1))
    last = ids_of(lens, pack, base + length - 1 + jnp.zeros((1, 1), jnp.int32))
    before = ids_of(lens, pack, base - 1 + jnp.zeros((1, 1), jnp.int32))
    return col, row, last, before


def gates(pre_forget, gap):
    open_gate = jax.nn.sigmoid(-pre_forget)
    gap_gate = gap * open_gate
    return open_gate, gap_gate, gap_gate.astype(BF16).astype(F32), jnp.log1p(-gap_gate)


def mm_split(a, b, dims=((1,), (0,))):
    (a_high, a_low), (b_high, b_low) = split_two(a), split_two(b)
    return mm(a_high, b_high, dims) + mm(a_high, b_low, dims) + mm(a_low, b_high, dims)


def running_sum(ones, value):
    high, low = split_two(value)
    return mm(ones, high) + mm(ones, low)


def states_kernel(lens, start, gap, pf, pv, state_out, decay_out):
    step = pl.program_id(0)
    length = pf.shape[2]
    heads = state_out.shape[1]

    @pl.when(step == 0)
    def _():
        state_out[...] = jnp.zeros_like(state_out)
        decay_out[...] = jnp.ones_like(decay_out)

    base = start[0] + step * length
    ones = triangle(length, False)
    for p in range(pf.shape[1]):
        col, _, last_id, before = block_docs(lens, p, base, length)
        _, _, key, log_forget = gates(pf[0, p], gap[...])
        cum = running_sum(ones, log_forget)
        last = cum[length - 1 :]
        khat = (key * jnp.where(col == last_id, jnp.exp(last - cum), 0.0)).astype(BF16)
        decay = jnp.where(last_id == before, jnp.exp(last), 0.0)
        decay_out[p] = decay_out[p] * decay
        for h in range(heads):
            at = slice(h * 128, h * 128 + 128)
            values = pv[0, p, :, at].astype(BF16)
            state_out[p, h] = state_out[p, h] * decay[:, at] + mm(values, khat[:, at], TN)


def entering_state(where_ref, states, decays, place, reverse):
    count = states.shape[0]
    for p in range(states.shape[1]):
        for h in range(states.shape[2]):
            at = slice(h * 128, h * 128 + 128)
            now = jnp.zeros(states.shape[3:], F32)
            for k in range(count):
                s = count - 1 - k if reverse else k
                reached = (s > place) if reverse else (s < place)
                new = decays[s, p, :, at] * now + states[s, p, h].astype(F32)
                now = jnp.where(reached, new, now)
            where_ref[p, h] = now


def forward_kernel(
    lens, start, gap, gain, proj, states, decays, heads_out, mixed_out, kept, state
):
    step = pl.program_id(0)
    length = proj.shape[2]
    heads = state.shape[1]
    width = heads * 128

    @pl.when(step == 0)
    def _():
        entering_state(state, states, decays, start[1], False)

    base = start[0] + step * length
    ones = triangle(length, False)
    row_index = lax.broadcasted_iota(jnp.int32, (length, length), 0)
    col_index = lax.broadcasted_iota(jnp.int32, (length, length), 1)
    for p in range(proj.shape[1]):
        col, row, last_id, before = block_docs(lens, p, base, length)
        _, _, key, log_forget = gates(proj[0, p, :, width : 2 * width], gap[...])
        cum = running_sum(ones, log_forget)
        last = cum[length - 1 :]
        khat = (key * jnp.where(col == last_id, jnp.exp(last - cum), 0.0)).astype(BF16)
        decay = jnp.where(last_id == before, jnp.exp(last), 0.0)
        qt = proj[0, p, :, :width].astype(BF16).astype(F32) * jnp.exp(cum)
        qe = jnp.where(col == before, qt, 0.0)
        kt = key * jnp.exp(-cum)
        visible = (col == row) & (row_index >= col_index)
        for h in range(heads):
            at = slice(h * 128, h * 128 + 128)
            values = proj[0, p, :, 2 * width + h * 128 : 2 * width + h * 128 + 128].astype(BF16)
            gate = proj[0, p, :, 3 * width + h * 128 : 3 * width + h * 128 + 128]
            now = state[p, h]
            kept[0, p, h] = now
            mixing = jnp.where(visible, mm_split(qt[:, at], kt[:, at], NT), 0.0).astype(BF16)
            mixed = mm(mixing, values) + mm_split(qe[:, at], now, NT)
            state[p, h] = now * decay[:, at] + mm(values, khat[:, at], TN)
            mixed_out[0, p, :, at] = mixed
            gated = mixed * (gate * jax.nn.sigmoid(gate))
            scale = lax.rsqrt(jnp.mean(gated * gated, axis=-1, keepdims=True) + EPSILON)
            heads_out[0, p, :, at] = (gated * scale * gain[:, at]).astype(BF16)


def gate_back_kernel(
    lens, start, gap, gain, proj, mixed_in, grad_heads, grad_out, grad_gate, group_part, state
):
    step = pl.program_id(0)
    length = proj.shape[2]
    heads = state.shape[1]
    width = heads * 128

    @pl.when(step == 0)
    def _():
        state[...] = jnp.zeros_like(state)
        group_part[...] = jnp.zeros_like(group_part)

    base = start[0] + (pl.num_programs(0) - 1 - step) * length
    ones = triangle(length, False)
    for p in range(proj.shape[1]):
        col, _, last_id, before = block_docs(lens, p, base, length)
        _, _, _, log_forget = gates(proj[0, p, :, width : 2 * width], gap[...])
        cum = running_sum(ones, log_forget)
        decay = jnp.where(last_id == before, jnp.exp(cum[length - 1 :]), 0.0)
        qt = proj[0, p, :, :width].astype(BF16).astype(F32) * jnp.exp(cum)
        qe = jnp.where(col == before, qt, 0.0).astype(BF16)
        for h in range(heads):
            at = slice(h * 128, h * 128 + 128)
            gate = proj[0, p, :, 3 * width + h * 128 : 3 * width + h * 128 + 128]
            mixed = mixed_in[0, p, :, at]
            incoming = grad_heads[0, p, :, at].astype(F32)
            sigma = jax.nn.sigmoid(gate)
            act = gate * sigma
            gated = mixed * act
            scale = lax.rsqrt(jnp.mean(gated * gated, axis=-1, keepdims=True) + EPSILON)
            group_part[:, at] += jnp.sum(incoming * gated * scale, axis=0, keepdims=True)
            weighted = incoming * gain[:, at]
            inner = jnp.mean(weighted * gated, axis=-1, keepdims=True)
            grad_gated = scale * weighted - gated * (scale * scale * scale) * inner
            grad = grad_gated * act
            grad_out[0, p, :, at] = grad
            slope = sigma * (1.0 + gate * (1.0 - sigma))
            grad_gate[0, p, :, at] = (grad_gated * mixed * slope).astype(BF16)
            high, low = split_two(grad)
            own = mm(high, qe[:, at], TN) + mm(low, qe[:, at], TN)
            state[p, h] = state[p, h] * decay[:, at] + own


def backward_kernel(
    lens, start, gap, proj, grad_out, grad_gate, kept, states, decays, grad_proj, gap_part, state
):
    step = pl.program_id(0)
    length = proj.shape[2]
    heads = state.shape[1]
    width = heads * 128

    @pl.when(step == 0)
    def _():
        entering_state(state, states, decays, start[1], True)
        gap_part[...] = jnp.zeros_like(gap_part)

    base = start[0] + (pl.num_programs(0) - 1 - step) * length
    ones = triangle(length, False)
    ones_up = triangle(length, True)
    row_index = lax.broadcasted_iota(jnp.int32, (length, length), 0)
    col_index = lax.broadcasted_iota(jnp.int32, (length, length), 1)
    for p in range(proj.shape[1]):
        col, row, last_id, before = block_docs(lens, p, base, length)
        open_gate, gap_gate, key, log_forget = gates(proj[0, p, :, width : 2 * width], gap[...])
        cum = running_sum(ones, log_forget)
        last = cum[length - 1 :]
        ecum = jnp.exp(cum)
        encum = jnp.exp(-cum)
        tail = jnp.where(col == last_id, jnp.exp(last - cum), 0.0)
        khat = (key * tail).astype(BF16)
        decay = jnp.where(last_id == before, jnp.exp(last), 0.0)
        qt = proj[0, p, :, :width].astype(BF16).astype(F32) * ecum
        enters = col == before
        qe = jnp.where(enters, qt, 0.0).astype(BF16)
        qt = qt.astype(BF16)
        kt = (key * encum).astype(BF16)
        visible = (col == row) & (row_index >= col_index)
        for h in range(heads):
            at = slice(h * 128, h * 128 + 128)
            values = proj[0, p, :, 2 * width + h * 128 : 2 * width + h * 128 + 128].astype(BF16)
            grad = grad_out[0, p, :, at]
            grad_enter = jnp.where(enters, grad, 0.0)
            grad, grad_low = split_two(grad)
            after = state[p, h]
            after_high, after_low = split_two(after)
            now = kept[0, p, h]
            mixing = jnp.where(visible, mm(qt[:, at], kt[:, at], NT), 0.0).astype(BF16)
            grad_mixing = mm(grad, values, NT) + mm(grad_low, values, NT)
            grad_mixing = jnp.where(visible, grad_mixing, 0.0).astype(BF16)
            grad_qt = mm(grad_mixing, kt[:, at]) + mm_split(grad_enter, now)
            grad_kt = mm(grad_mixing, qt[:, at], TN)
            grad_values = mm(mixing, grad, TN) + mm(khat[:, at], after_high, NT)
            grad_khat = mm(values, after_high) + mm(values, after_low)
            grad_decay = jnp.sum(after * now, axis=0, keepdims=True)
            own = mm(grad, qe[:, at], TN) + mm(grad_low, qe[:, at], TN)
            state[p, h] = after * decay[:, at] + own
            through = grad_khat * khat[:, at].astype(F32)
            grad_cum = (
                grad_qt * qt[:, at].astype(F32) - grad_kt * kt[:, at].astype(F32) - through
            )
            grad_last = jnp.sum(through, axis=0, keepdims=True) + grad_decay * decay[:, at]
            grad_log = running_sum(ones_up, grad_cum) + grad_last
            grad_keys = grad_kt * encum[:, at] + grad_khat * tail[:, at]
            grad_gap = grad_keys - grad_log / (1.0 - gap_gate[:, at])
            gap_part[:, at] += jnp.sum(grad_gap * open_gate[:, at], axis=0, keepdims=True)
            grad_forget = -grad_gap * gap_gate[:, at] * (1.0 - open_gate[:, at])
            grad_proj[0, p, :, at] = (grad_qt * ecum[:, at]).astype(BF16)
            grad_proj[0, p, :, width + h * 128 : width + h * 128 + 128] = grad_forget.astype(BF16)
            grad_proj[0, p, :, 2 * width + h * 128 : 2 * width + h * 128 + 128] = (
                grad_values.astype(BF16)
            )
        grad_proj[0, p, :, 3 * width :] = grad_gate[0, p]


def recur_call(kernel, steps, half, reverse, ins, outs, scratch, flops, name):
    def index(kind):
        def rows(j):
            b = steps - 1 - j if reverse else j
            return (b // half, 0, b % half, kind if isinstance(kind, int) else 0)

        def block(j):
            return (steps - 1 - j if reverse else j, 0, 0, 0, 0)

        return rows if isinstance(kind, int) else block

    in_specs, arrays = [], []
    for array, kind, shape in ins:
        arrays.append(array)
        if kind == "smem":
            in_specs.append(pl.BlockSpec(memory_space=pltpu.SMEM))
        elif kind == "whole":
            in_specs.append(pl.BlockSpec(array.shape, lambda j, n=array.ndim: (0,) * n))
        else:
            in_specs.append(pl.BlockSpec(shape, index(kind)))
    out_specs, out_shapes = [], []
    for shape, dtype, kind, block in outs:
        out_shapes.append(jax.ShapeDtypeStruct(shape, dtype))
        if kind == "whole":
            out_specs.append(pl.BlockSpec(shape, lambda j, n=len(shape): (0,) * n))
        else:
            out_specs.append(pl.BlockSpec(block, index(kind)))
    moved = sum(a.size * a.dtype.itemsize for a in arrays)
    return pl.pallas_call(
        kernel,
        grid=(steps,),
        in_specs=in_specs,
        out_specs=out_specs,
        out_shape=out_shapes,
        scratch_shapes=scratch,
        compiler_params=pltpu.CompilerParams(
            dimension_semantics=("arbitrary",), vmem_limit_bytes=48 << 20
        ),
        cost_estimate=pl.CostEstimate(flops=flops, bytes_accessed=moved, transcendentals=0),
        name=name,
    )(*arrays)


def swap(value, across):
    return lax.ppermute(value, "seq", [(i, i ^ across) for i in range(lax.axis_size("seq"))])


CORE, XLINK, YLINK = 1, 2, 4
TILE = 128


def plane_gather(own):
    half = own.shape[0] // 2
    got = {0: own, XLINK: swap(own, XLINK), YLINK: swap(own, YLINK), CORE: swap(own, CORE)}
    first = swap(got[YLINK][:half], XLINK)
    second = swap(got[XLINK][half:], YLINK)
    got[XLINK + CORE] = swap(got[XLINK], CORE)
    got[YLINK + CORE] = swap(got[YLINK], CORE)
    got[XLINK + YLINK] = jnp.concatenate([first, second])
    got[XLINK + YLINK + CORE] = jnp.concatenate([swap(first, CORE), swap(second, CORE)])
    return got


def add_low(a, b):
    return (a.astype(F32) + b.astype(F32)).astype(BF16)


def plane_scatter(parts):
    half = parts[0].shape[0] // 2
    chip = {}
    for a in (6, 2, 4, 0):
        chip[a] = add_low(parts[a], swap(parts[a ^ CORE], CORE))
    from_x = swap(chip[6][:half], XLINK)
    from_y = swap(chip[6][half:], YLINK)
    mine_x = swap(chip[2][:half], XLINK)
    mine_y = swap(chip[4][half:], YLINK)
    last_y = swap(add_low(chip[4][:half], from_x), YLINK)
    last_x = swap(add_low(chip[2][half:], from_y), XLINK)
    low = chip[0][:half].astype(F32) + mine_x.astype(F32) + last_y.astype(F32)
    high = chip[0][half:].astype(F32) + mine_y.astype(F32) + last_x.astype(F32)
    return jnp.concatenate([low, high])


def pick(array, index, axis):
    return lax.dynamic_index_in_dim(array, index, axis, keepdims=False)


def plane_device(
    tokens,
    norm1_gain,
    w_mix_in,
    forget_gap,
    group_gain,
    w_mix_out,
    norm2_gain,
    w_gate_up,
    w_down,
    doc_lengths,
    out_cotangent,
):
    seq_count, mp_count = lax.axis_size("seq"), lax.axis_size("mp")
    seq_index, mp_index = lax.axis_index("seq"), lax.axis_index("mp")
    core, chip = seq_index % 2, seq_index // 2
    chips = seq_count // 2
    span, packs, width = tokens.shape
    rows = span * packs
    run = span * mp_count
    heads, head_size = forget_gap.shape
    chans = heads * head_size
    hidden_units = w_gate_up.shape[2]
    slice_d = width // seq_count

    def pack_major(array):
        return jnp.transpose(array, (1, 0, 2)).reshape(rows, width)

    def token_major(array):
        return jnp.transpose(array.reshape(packs, span, width), (1, 0, 2))

    own = pack_major(tokens)
    scale_one = rms_scale(own)
    normed = (own * scale_one * norm1_gain).astype(BF16)
    in_flat = w_mix_in.reshape(width, 4 * chans)
    normed_all = lax.all_gather(normed, "mp", axis=0, tiled=True)

    cot_own = pack_major(lax.dynamic_slice_in_dim(out_cotangent, mp_index * span, span, 0))
    cot = plane_gather(cot_own.astype(BF16))

    share = -(-hidden_units // (chips * TILE)) * TILE
    local_ff = 2 * share
    spare = share * chips - hidden_units
    begin = jnp.minimum(chip * share, hidden_units - share)
    gu_part = lax.dynamic_slice_in_dim(pick(w_gate_up, core, 1), begin, share, 1)
    dn_part = lax.dynamic_slice_in_dim(w_down, begin, share, 0)
    fresh = lax.broadcasted_iota(jnp.int32, (share, 1), 0) >= chip * share - begin
    dn_part = jnp.where(fresh, dn_part, jnp.zeros_like(dn_part))
    dn_part = lax.dynamic_slice_in_dim(dn_part, core * (share // 2), share // 2, 0)

    def collect(part):
        pairs = lax.all_gather(part, "mp", axis=0).reshape((2, 2) + part.shape)
        mine = pick(pairs, core, 0)
        other = swap(pick(pairs, 1 - core, 0), CORE)
        return jnp.where(core == 0, mine, other), jnp.where(core == 0, other, mine)

    normed_all, in_flat, gu_part, dn_part, cot = lax.optimization_barrier(
        (normed_all, in_flat, gu_part, dn_part, cot)
    )
    w_gate, w_up = collect(gu_part)
    w_gu = jnp.concatenate([w_gate[0], w_gate[1], w_up[0], w_up[1]], axis=1)
    w_dn = jnp.concatenate(collect(dn_part), axis=1).reshape(local_ff, width)

    projected = mm(normed_all, in_flat).reshape(mp_count, packs, span, 4 * chans)

    start = jnp.stack([seq_index * run, seq_index]).astype(jnp.int32)
    gap_row = forget_gap.reshape(1, chans)
    gain_row = group_gain.reshape(1, chans)
    steps, half = run // BLOCK, span // BLOCK
    block = (1, packs, BLOCK, chans)
    wide = (1, packs, BLOCK, 4 * chans)
    state_shape = (packs, heads, head_size, head_size)
    unit = 2 * BLOCK * head_size * head_size * packs * heads * steps
    common = [(doc_lengths, "smem", None), (start, "smem", None), (gap_row, "whole", None)]
    run_state, run_decay = recur_call(
        states_kernel,
        steps,
        half,
        False,
        common + [(projected, 1, block), (projected, 2, block)],
        [(state_shape, F32, "whole", None), ((packs, 1, chans), F32, "whole", None)],
        [],
        3 * unit,
        "run_states",
    )
    all_states = lax.all_gather(run_state.astype(BF16), "seq")
    all_decays = lax.all_gather(run_decay, "seq")
    row_shape = (mp_count, packs, span, chans)
    heads_out, mixed, kept = recur_call(
        forward_kernel,
        steps,
        half,
        False,
        common
        + [
            (gain_row, "whole", None),
            (projected, 0, wide),
            (all_states, "whole", None),
            (all_decays, "whole", None),
        ],
        [
            (row_shape, BF16, 0, block),
            (row_shape, F32, 0, block),
            ((steps,) + state_shape, F32, "block", (1,) + state_shape),
        ],
        [pltpu.VMEM(state_shape, F32)],
        6 * unit,
        "mix_forward",
    )
    heads_tok = lax.all_to_all(
        heads_out.reshape(mp_count, rows, chans), "mp", split_axis=0, concat_axis=0, tiled=True
    )
    heads_tok = jnp.transpose(heads_tok, (1, 0, 2)).reshape(rows, mp_count * chans)
    out_flat = w_mix_out.reshape(-1, width)
    hidden = own + mm(heads_tok, out_flat)
    scale_two = rms_scale(hidden)
    normed_two = (hidden * scale_two * norm2_gain).astype(BF16)

    two = plane_gather(normed_two)
    groups = ((6, 7), (2, 3, 4, 5), (0, 1))
    act_of, pre_of, two_of, cot_of = {}, {}, {}, {}
    down_parts = {}
    for group in reversed(groups):
        two_of[group] = jnp.concatenate([two[a] for a in group])
        cot_of[group] = jnp.concatenate([cot[a] for a in group])
        pre = mm(two_of[group], w_gu)
        pre_of[group] = pre
        act_of[group] = (jax.nn.silu(pre[:, :local_ff]) * pre[:, local_ff:]).astype(BF16)
    for group in groups:
        made = mm(act_of[group], w_dn).astype(BF16)
        for k, a in enumerate(group):
            down_parts[a] = made[k * rows : k * rows + rows]
    back_parts, grad_of = {}, {}
    for group in groups:
        pre_gate, pre_up = pre_of[group][:, :local_ff], pre_of[group][:, local_ff:]
        grad_act = mm(cot_of[group], w_dn, NT)
        grad_of[group] = jnp.concatenate(
            [grad_act * pre_up * silu_slope(pre_gate), grad_act * jax.nn.silu(pre_gate)], axis=1
        ).astype(BF16)
        made = mm(grad_of[group], w_gu, NT).astype(BF16)
        for k, a in enumerate(group):
            back_parts[a] = made[k * rows : k * rows + rows]
    grad_normed_two = plane_scatter(back_parts)
    gu_grad = sum(mm(two_of[g], grad_of[g], TN) for g in groups).astype(BF16)
    dn_grad = sum(mm(act_of[g], cot_of[g], TN) for g in groups).astype(BF16)
    grad_normed_two, gu_grad, dn_grad, down_parts = lax.optimization_barrier(
        (grad_normed_two, gu_grad, dn_grad, down_parts)
    )
    layer_out = token_major(hidden + plane_scatter(down_parts))

    norm2_part = jnp.sum(grad_normed_two * hidden * scale_two, axis=0)
    grad_hidden = cot_own + rms_back(grad_normed_two, hidden, scale_two, norm2_gain)
    grad_mix = grad_hidden.astype(BF16)
    grad_tok = mm(grad_mix, out_flat, NT).astype(BF16)
    grad_tok = jnp.transpose(grad_tok.reshape(rows, mp_count, chans), (1, 0, 2))
    grad_heads = lax.all_to_all(grad_tok, "mp", split_axis=0, concat_axis=0, tiled=True)
    grad_heads = grad_heads.reshape(row_shape)

    def deliver(parts):
        mine = pick(parts, core, 0)
        other = swap(pick(parts, 1 - core, 0), CORE)
        low = jnp.where(core == 0, mine, other)
        high = jnp.where(core == 0, other, mine)
        return lax.psum_scatter(
            jnp.concatenate([low, high]), "mp", scatter_dimension=0, tiled=True
        )[0]

    def hand_round(piece):
        got = [pick(piece, chip, 0)]
        got += [swap(pick(piece, chip ^ a, 0), 2 * a) for a in range(1, chips)]
        got = jnp.stack(got)
        return [pick(got, chip ^ c, 0) for c in range(chips)]

    gu_grad = gu_grad.reshape(chips, 2, slice_d, 2, 2, share)
    gu_grad = jnp.transpose(gu_grad, (1, 4, 3, 0, 2, 5))
    got = [q.astype(F32) for q in hand_round(jnp.transpose(deliver(gu_grad), (1, 0, 2, 3)))]
    got[-1] = got[-1][:, :, spare:]
    gate_up_grad = jnp.transpose(jnp.concatenate(got, axis=-1), (1, 0, 2))
    dn_grad = dn_grad.reshape(2, share, chips, 2, slice_d)
    got = hand_round(deliver(jnp.transpose(dn_grad, (3, 0, 2, 1, 4))))
    got[-1] = got[-1][spare:]
    down_grad = jnp.concatenate(got, axis=0).astype(F32)

    out_grad = mm(heads_tok, grad_mix, TN).astype(BF16)
    out_grad = out_grad.reshape(mp_count * heads, seq_count, head_size // seq_count, width)
    out_grad = plane_scatter(
        {a: pick(out_grad, seq_index ^ a, 1) for a in range(seq_count)}
    ).astype(BF16)
    mix_out_grad = lax.psum_scatter(out_grad, "mp", scatter_dimension=0, tiled=True).astype(F32)

    grad_out, grad_gate, group_part, run_grad = recur_call(
        gate_back_kernel,
        steps,
        half,
        True,
        common
        + [
            (gain_row, "whole", None),
            (projected, 0, wide),
            (mixed, 0, block),
            (grad_heads, 0, block),
        ],
        [
            (row_shape, F32, 0, block),
            (row_shape, BF16, 0, block),
            ((1, chans), F32, "whole", None),
            (state_shape, F32, "whole", None),
        ],
        [],
        3 * unit,
        "gate_back",
    )
    all_grads = lax.all_gather(run_grad.astype(BF16), "seq")
    grad_projected, gap_part = recur_call(
        backward_kernel,
        steps,
        half,
        True,
        common
        + [
            (projected, 0, wide),
            (grad_out, 0, block),
            (grad_gate, 0, block),
            (kept, "block", (1,) + state_shape),
            (all_grads, "whole", None),
            (all_decays, "whole", None),
        ],
        [((mp_count, packs, span, 4 * chans), BF16, 0, wide), ((1, chans), F32, "whole", None)],
        [pltpu.VMEM(state_shape, F32)],
        12 * unit,
        "mix_backward",
    )
    grad_flat = grad_projected.reshape(mp_count * rows, 4 * chans)
    back_in = mm(grad_flat, in_flat, NT)
    norm1_part = jnp.sum(back_in * normed_all.astype(F32), axis=0) / norm1_gain
    grad_normed = lax.psum_scatter(
        back_in.astype(BF16), "mp", scatter_dimension=0, tiled=True
    ).astype(F32)
    in_grad = mm(normed_all, grad_flat, TN).astype(BF16)
    in_grad = in_grad.reshape(seq_count, slice_d, 4 * chans)
    mix_in_grad = plane_scatter(
        {a: pick(in_grad, seq_index ^ a, 0) for a in range(seq_count)}
    ).reshape(slice_d, 4, chans)

    tokens_grad = token_major(
        grad_hidden + rms_back(grad_normed, own, scale_one, norm1_gain)
    )
    small = jnp.stack([group_part, gap_part]).reshape(2, heads, head_size)
    small = lax.psum_scatter(small, "seq", scatter_dimension=2, tiled=True)
    norm1_grad = lax.psum_scatter(norm1_part, ("seq", "mp"), scatter_dimension=0, tiled=True)
    norm2_grad = lax.psum_scatter(norm2_part, ("seq", "mp"), scatter_dimension=0, tiled=True)
    return (
        layer_out,
        tokens_grad,
        norm1_grad,
        mix_in_grad,
        small[1],
        small[0],
        mix_out_grad,
        norm2_grad,
        gate_up_grad,
        down_grad,
    )


def solution(mesh):
    body = plane_device if dict(mesh.shape) == {"seq": 8, "mp": 4} else generic_device
    placed = (
        P(("seq", "mp"), None, None),
        P(),
        P(None, None, "mp"),
        P("mp", None),
        P("mp", None),
        P(),
        P(),
        P(None, None, "mp"),
        P("mp", None),
        P(),
        P("seq", None, None),
    )
    return jax.shard_map(
        body,
        mesh=mesh,
        in_specs=placed,
        out_specs=(
            P(("seq", "mp"), None, None),
            P(("seq", "mp"), None, None),
            P(("seq", "mp")),
            P("seq", None, "mp"),
            P("mp", "seq"),
            P("mp", "seq"),
            P("mp", "seq", None),
            P(("seq", "mp")),
            P("seq", None, "mp"),
            P("mp", "seq"),
        ),
        check_vma=False,
    )
```

```python
import functools

import jax
import jax.numpy as jnp
from jax import lax
from jax.experimental import pallas as pl
from jax.experimental.pallas import tpu as pltpu
from jax.sharding import PartitionSpec as P

BLOCK = 128


EPSILON = 1e-06
PRECISE = lax.Precision.HIGHEST


def entering(x, axis, combine, identity, reverse):
    length, index = (lax.axis_size(axis), lax.axis_index(axis))
    everything = jax.tree.map(
        lambda part, kind: lax.all_gather(part.astype(kind), axis), x, (jnp.bfloat16, jnp.bfloat16)
    )
    start = jax.tree.map(
        lambda part, zero: jnp.broadcast_to(jnp.asarray(zero, part.dtype), part.shape), x, identity
    )

    def turn(k, before):
        at = length - 1 - k if reverse else k
        reached = at > index if reverse else at < index
        new = combine(
            before, jax.tree.map(lambda part, own: part[at].astype(own.dtype), everything, x)
        )
        return jax.tree.map(lambda a, b: jnp.where(reached, a, b), new, before)

    return lax.fori_loop(0, length, turn, start)


def rounded(signal):
    return lax.optimization_barrier(signal.astype(jnp.bfloat16)).astype(jnp.float32)


def rms_scale(signal):
    return lax.rsqrt(jnp.mean(signal * signal, axis=-1, keepdims=True) + EPSILON)


def rms_back(gradient, signal, scaling, gain_vec):
    weighted = gradient * gain_vec
    inner_sum = jnp.mean(weighted * signal, axis=-1, keepdims=True)
    return scaling * weighted - signal * (scaling * scaling * scaling) * inner_sum


def silu_slope(signal):
    sigma_val = jax.nn.sigmoid(signal)
    return sigma_val * (1.0 + signal * (1.0 - sigma_val))


def doc_index(doc_lengths, positions):
    doc_ends = jnp.stack(
        [jnp.sum(doc_lengths[:, : k + 1], axis=1) for k in range(doc_lengths.shape[1])], axis=1
    )
    return jnp.sum((positions[:, None, None] >= doc_ends[None, :, :]).astype(jnp.int32), axis=2)


def chain_combine(earlier, later_part):
    return (earlier[0] * later_part[0], later_part[0][..., None] * earlier[1] + later_part[1])


def block_tables(log_forget, doc_ids, previous):
    length = log_forget.shape[1]
    row_index = lax.broadcasted_iota(jnp.int32, (length, length), 0)
    col_index = lax.broadcasted_iota(jnp.int32, (length, length), 1)
    lower_ones = (row_index >= col_index).astype(jnp.float32)
    cumulated = jnp.einsum("ij,njshk->nishk", lower_ones, log_forget, precision=PRECISE)
    last_sum = cumulated[:, -1]
    same_doc = doc_ids[:, :, None, :] == doc_ids[:, None, :, :]
    visible = jnp.transpose(same_doc & (row_index >= col_index)[None, :, :, None], (0, 3, 1, 2))[
        :, :, None
    ]
    enters = (doc_ids == previous[:, None, :]).astype(jnp.float32)[..., None, None]
    at_end = (doc_ids == doc_ids[:, -1:, :]).astype(jnp.float32)[..., None, None]
    alive_end = (doc_ids[:, -1] == previous).astype(jnp.float32)[..., None, None]
    decays = jnp.exp(last_sum) * alive_end
    return (lower_ones, cumulated, last_sum, visible, enters, at_end, decays)


def block_factors(queries, key_vec, cumulated, last_sum, at_end):
    q_tilde = queries * jnp.exp(cumulated)
    k_tilde = key_vec * jnp.exp(-cumulated)
    k_hat = key_vec * jnp.exp(last_sum[:, None] - cumulated) * at_end
    return (q_tilde, k_tilde, k_hat)


def recur_forward(queries, key_vec, values_in, log_forget, doc_ids, previous):
    lower_ones, cumulated, last_sum, visible, enters, at_end, decays = block_tables(
        log_forget, doc_ids, previous
    )
    q_tilde, k_tilde, k_hat = block_factors(queries, key_vec, cumulated, last_sum, at_end)
    scores = jnp.einsum("nishk,njshk->nshij", q_tilde, k_tilde, precision=PRECISE)
    mixing = jnp.where(visible, scores, 0.0)
    inside = jnp.einsum("nshij,njshv->nishv", mixing, values_in, precision=PRECISE)
    local_sum = jnp.einsum("njshk,njshv->nshkv", k_hat, values_in, precision=PRECISE)

    def advance(carried, element):
        state_now, product = carried
        factor, addend = element
        return ((factor[..., None] * state_now + addend, product * factor), (state_now, product))

    zero_state = jnp.zeros(local_sum.shape[1:], jnp.float32)
    unit_decay = jnp.ones(decays.shape[1:], jnp.float32)
    (run_state, run_decay), (prefix_state, prefix_decay) = lax.scan(
        advance, (zero_state, unit_decay), (decays, local_sum)
    )
    incoming = entering(
        (run_decay, run_state), "seq", chain_combine, (unit_decay, zero_state), False
    )[1]
    start_state = prefix_state + prefix_decay[..., None] * incoming[None]
    carried_in = jnp.einsum("nishk,nshkv->nishv", q_tilde * enters, start_state, precision=PRECISE)
    return (inside + carried_in, start_state)


def recur_backward(
    queries, key_vec, values_in, log_forget, doc_ids, previous, start_state, grad_out
):
    lower_ones, cumulated, last_sum, visible, enters, at_end, decays = block_tables(
        log_forget, doc_ids, previous
    )
    q_tilde, k_tilde, k_hat = block_factors(queries, key_vec, cumulated, last_sum, at_end)
    scores = jnp.einsum("nishk,njshk->nshij", q_tilde, k_tilde, precision=PRECISE)
    mixing = jnp.where(visible, scores, 0.0)
    own_term = jnp.einsum("nishk,nishv->nshkv", q_tilde * enters, grad_out, precision=PRECISE)

    def retreat(carried, element):
        running, product = carried
        factor, addend = element
        return ((addend + factor[..., None] * running, product * factor), (running, product))

    zero_state = jnp.zeros(own_term.shape[1:], jnp.float32)
    unit_decay = jnp.ones(decays.shape[1:], jnp.float32)
    (run_grad, run_decay), (after_sum, after_decay) = lax.scan(
        retreat, (zero_state, unit_decay), (decays, own_term), reverse=True
    )
    outgoing = entering(
        (run_decay, run_grad), "seq", chain_combine, (unit_decay, zero_state), True
    )[1]
    next_grad = after_sum + after_decay[..., None] * outgoing[None]
    grad_mixing = jnp.where(
        visible, jnp.einsum("nishv,njshv->nshij", grad_out, values_in, precision=PRECISE), 0.0
    )
    grad_qt = jnp.einsum("nshij,njshk->nishk", grad_mixing, k_tilde, precision=PRECISE)
    grad_qt = grad_qt + jnp.einsum(
        "nishv,nshkv->nishk", grad_out * enters, start_state, precision=PRECISE
    )
    grad_kt = jnp.einsum("nshij,nishk->njshk", grad_mixing, q_tilde, precision=PRECISE)
    grad_values = jnp.einsum("nshij,nishv->njshv", mixing, grad_out, precision=PRECISE)
    grad_values = grad_values + jnp.einsum(
        "njshk,nshkv->njshv", k_hat, next_grad, precision=PRECISE
    )
    grad_khat = jnp.einsum("njshv,nshkv->njshk", values_in, next_grad, precision=PRECISE) * at_end
    grad_decay = jnp.sum(next_grad * start_state, axis=-1)
    grad_queries = grad_qt * jnp.exp(cumulated)
    grad_keys = grad_kt * jnp.exp(-cumulated) + grad_khat * jnp.exp(last_sum[:, None] - cumulated)
    grad_cum = grad_qt * q_tilde - grad_kt * k_tilde - grad_khat * k_hat
    grad_last = jnp.sum(grad_khat * k_hat, axis=1) + grad_decay * decays
    grad_log = (
        jnp.einsum("it,nishk->ntshk", lower_ones, grad_cum, precision=PRECISE) + grad_last[:, None]
    )
    return (grad_queries, grad_keys, grad_values, grad_log)


def generic_device(
    tokens,
    norm1_gain,
    w_mix_in,
    forget_gap,
    group_gain,
    w_mix_out,
    norm2_gain,
    w_gate_up,
    w_down,
    doc_lengths,
    out_cotangent,
):
    mp_count = lax.axis_size("mp")
    rows_dev, pack_count, model_width = tokens.shape
    run_length = rows_dev * mp_count
    blocks = run_length // BLOCK
    local_heads, head_size = forget_gap.shape
    local_chans = local_heads * head_size
    local_ff = w_gate_up.shape[2]
    mp_index = lax.axis_index("mp")
    run_start = lax.axis_index("seq") * run_length
    positions = run_start - 1 + jnp.arange(run_length + 1, dtype=jnp.int32)
    all_ids = doc_index(doc_lengths, positions)
    doc_ids = all_ids[1:].reshape(blocks, BLOCK, pack_count)
    previous = all_ids[0:run_length:BLOCK]
    shape_blocks = (blocks, BLOCK, pack_count, local_heads, head_size)
    shape_heads = (run_length, pack_count, local_heads, head_size)
    shape_flat = (run_length, pack_count, local_chans)
    scale_one = rms_scale(tokens)
    normed = (tokens * scale_one * norm1_gain).astype(jnp.bfloat16)
    in_flat = w_mix_in.reshape(model_width, 4 * local_chans)
    shard_rows = lax.all_gather(normed, "mp", axis=0, tiled=True)
    normed_all = shard_rows
    projected = jnp.einsum("tsd,dc->tsc", shard_rows, in_flat, preferred_element_type=jnp.float32)
    pre_query = projected[..., :local_chans]
    pre_forget = projected[..., local_chans : 2 * local_chans]
    pre_value = projected[..., 2 * local_chans : 3 * local_chans]
    pre_gate = projected[..., 3 * local_chans :]
    open_gate = jax.nn.sigmoid(-pre_forget)
    gap_gate = forget_gap.reshape(local_chans) * open_gate
    queries = rounded(pre_query).reshape(shape_blocks)
    key_vec = rounded(gap_gate).reshape(shape_blocks)
    values_in = rounded(pre_value).reshape(shape_blocks)
    log_forget = jnp.log1p(-gap_gate).reshape(shape_blocks)
    mixed, start_state = recur_forward(queries, key_vec, values_in, log_forget, doc_ids, previous)
    mixed = mixed.reshape(shape_flat)
    gate_act = jax.nn.silu(pre_gate)
    gated_four = (mixed * gate_act).reshape(shape_heads)
    scale_group = rms_scale(gated_four)
    heads_out = (gated_four * scale_group * group_gain).astype(jnp.bfloat16).reshape(shape_flat)
    heads_tok = lax.all_to_all(heads_out, "mp", split_axis=0, concat_axis=2, tiled=True)
    out_flat = w_mix_out.reshape(-1, model_width)
    hidden = tokens + jnp.einsum(
        "tsc,cd->tsd", heads_tok, out_flat, preferred_element_type=jnp.float32
    )
    scale_two = rms_scale(hidden)
    normed_two = (hidden * scale_two * norm2_gain).astype(jnp.bfloat16)
    ffn_flat = w_gate_up.reshape(model_width, 2 * local_ff)
    shard_rows = lax.all_gather(normed_two, "mp", axis=0, tiled=True)
    gate_up = jnp.einsum("tsd,dc->tsc", shard_rows, ffn_flat, preferred_element_type=jnp.float32)
    pre_gate_two = gate_up[..., :local_ff]
    pre_up = gate_up[..., local_ff:]
    silu_two = jax.nn.silu(pre_gate_two)
    activation = (silu_two * pre_up).astype(jnp.bfloat16)
    partial_value = activation
    ffn_sum = lax.psum_scatter(
        jnp.einsum("tsf,fd->tsd", partial_value, w_down, preferred_element_type=jnp.float32).astype(
            jnp.bfloat16
        ),
        "mp",
        scatter_dimension=0,
        tiled=True,
    ).astype(jnp.float32)
    layer_out = hidden + ffn_sum
    cot_low = out_cotangent.astype(jnp.bfloat16)
    cot_own = lax.dynamic_slice_in_dim(out_cotangent, mp_index * rows_dev, rows_dev, 0)
    down_part = jnp.einsum("tsf,tsd->fd", activation, cot_low, preferred_element_type=jnp.float32)
    grad_act = jnp.einsum("tsd,fd->tsf", cot_low, w_down, preferred_element_type=jnp.float32)
    grad_gate_two = grad_act * pre_up * silu_slope(pre_gate_two)
    grad_up = grad_act * silu_two
    grad_gate_up = jnp.concatenate([grad_gate_two, grad_up], axis=-1).astype(jnp.bfloat16)
    gate_up_part = jnp.einsum(
        "tsd,tsc->dc", shard_rows, grad_gate_up, preferred_element_type=jnp.float32
    )
    gate_up_part = gate_up_part.reshape(model_width, 2, local_ff)
    partial_value = grad_gate_up
    grad_normed_two = lax.psum_scatter(
        jnp.einsum(
            "tsc,dc->tsd", partial_value, ffn_flat, preferred_element_type=jnp.float32
        ).astype(jnp.bfloat16),
        "mp",
        scatter_dimension=0,
        tiled=True,
    ).astype(jnp.float32)
    norm2_part = jnp.sum(grad_normed_two * hidden * scale_two, axis=(0, 1))
    grad_hidden = cot_own + rms_back(grad_normed_two, hidden, scale_two, norm2_gain)
    grad_mix = grad_hidden.astype(jnp.bfloat16)
    out_part = jnp.einsum("tsc,tsd->cd", heads_tok, grad_mix, preferred_element_type=jnp.float32)
    grad_tok = jnp.einsum(
        "tsd,cd->tsc", grad_mix, out_flat, preferred_element_type=jnp.float32
    ).astype(jnp.bfloat16)
    grad_heads = lax.all_to_all(grad_tok, "mp", split_axis=2, concat_axis=0, tiled=True).astype(
        jnp.float32
    )
    grad_four = grad_heads.reshape(shape_heads)
    group_part = jnp.sum(grad_four * gated_four * scale_group, axis=(0, 1))
    grad_gated = rms_back(grad_four, gated_four, scale_group, group_gain).reshape(shape_flat)
    grad_mixed = grad_gated * gate_act
    grad_gate_in = grad_gated * mixed * silu_slope(pre_gate)
    grad_queries, grad_keys, grad_values, grad_log = recur_backward(
        queries,
        key_vec,
        values_in,
        log_forget,
        doc_ids,
        previous,
        start_state,
        grad_mixed.reshape(shape_blocks),
    )
    grad_gap = grad_keys.reshape(shape_flat) - grad_log.reshape(shape_flat) / (1.0 - gap_gate)
    gap_part = jnp.sum(grad_gap * open_gate, axis=(0, 1)).reshape(local_heads, head_size)
    grad_forget_in = -grad_gap * gap_gate * (1.0 - open_gate)
    grad_projected = jnp.concatenate(
        [
            grad_queries.reshape(shape_flat),
            grad_forget_in,
            grad_values.reshape(shape_flat),
            grad_gate_in,
        ],
        axis=-1,
    ).astype(jnp.bfloat16)
    mix_in_part = jnp.einsum(
        "tsd,tsc->dc", normed_all, grad_projected, preferred_element_type=jnp.float32
    )
    mix_in_part = mix_in_part.reshape(model_width, 4, local_chans)
    partial_value = grad_projected
    grad_normed = lax.psum_scatter(
        jnp.einsum(
            "tsc,dc->tsd", partial_value, in_flat, preferred_element_type=jnp.float32
        ).astype(jnp.bfloat16),
        "mp",
        scatter_dimension=0,
        tiled=True,
    ).astype(jnp.float32)
    norm1_part = jnp.sum(grad_normed * tokens * scale_one, axis=(0, 1))
    tokens_grad = grad_hidden + rms_back(grad_normed, tokens, scale_one, norm1_gain)
    seq_count = lax.axis_size("seq")
    arranged = out_part.reshape(
        mp_count, local_heads, seq_count, head_size // seq_count, model_width
    )
    arranged = jnp.transpose(arranged, (2, 0, 1, 3, 4)).reshape(
        seq_count * mp_count * local_heads, head_size // seq_count, model_width
    )
    mix_in_grad, gate_up_grad, down_grad, group_grad, gap_grad = (
        lax.psum_scatter(
            mix_in_part.astype(jnp.bfloat16), "seq", scatter_dimension=0, tiled=True
        ).astype(jnp.float32),
        lax.psum_scatter(
            gate_up_part.astype(jnp.bfloat16), "seq", scatter_dimension=0, tiled=True
        ).astype(jnp.float32),
        lax.psum_scatter(
            down_part.astype(jnp.bfloat16), "seq", scatter_dimension=1, tiled=True
        ).astype(jnp.float32),
        lax.psum_scatter(
            group_part.astype(jnp.bfloat16), "seq", scatter_dimension=1, tiled=True
        ).astype(jnp.float32),
        lax.psum_scatter(
            gap_part.astype(jnp.bfloat16), "seq", scatter_dimension=1, tiled=True
        ).astype(jnp.float32),
    )
    mix_out_grad, norm1_grad, norm2_grad = (
        lax.psum_scatter(arranged, ("seq", "mp"), scatter_dimension=0, tiled=True),
        lax.psum_scatter(norm1_part, ("seq", "mp"), scatter_dimension=0, tiled=True),
        lax.psum_scatter(norm2_part, ("seq", "mp"), scatter_dimension=0, tiled=True),
    )
    return (
        layer_out,
        tokens_grad,
        norm1_grad,
        mix_in_grad,
        gap_grad,
        group_grad,
        mix_out_grad,
        norm2_grad,
        gate_up_grad,
        down_grad,
    )


F32 = jnp.float32
BF16 = jnp.bfloat16


def mm(a, b, dims=((1,), (0,))):
    return lax.dot_general(a, b, (dims, ((), ())), preferred_element_type=F32)


NN, NT, TN = ((1,), (0,)), ((1,), (1,)), ((0,), (0,))


def split_two(value):
    high = value.astype(BF16)
    return high, (value - high.astype(F32)).astype(BF16)


def triangle(length, upper):
    row = lax.broadcasted_iota(jnp.int32, (length, length), 0)
    col = lax.broadcasted_iota(jnp.int32, (length, length), 1)
    return jnp.where((row <= col) if upper else (row >= col), 1.0, 0.0).astype(BF16)


def ids_of(lens, pack, positions):
    total, ids = 0, jnp.zeros_like(positions)
    for k in range(lens.shape[1]):
        total = total + lens[pack, k]
        ids = ids + jnp.where(positions >= total, 1, 0)
    return ids


def block_docs(lens, pack, base, length):
    col = ids_of(lens, pack, base + lax.broadcasted_iota(jnp.int32, (length, 1), 0))
    row = ids_of(lens, pack, base + lax.broadcasted_iota(jnp.int32, (1, length), 1))
    last = ids_of(lens, pack, base + length - 1 + jnp.zeros((1, 1), jnp.int32))
    before = ids_of(lens, pack, base - 1 + jnp.zeros((1, 1), jnp.int32))
    return col, row, last, before


def gates(pre_forget, gap):
    open_gate = jax.nn.sigmoid(-pre_forget)
    gap_gate = gap * open_gate
    return open_gate, gap_gate, gap_gate.astype(BF16).astype(F32), jnp.log1p(-gap_gate)


def mm_split(a, b, dims=((1,), (0,))):
    (a_high, a_low), (b_high, b_low) = split_two(a), split_two(b)
    return mm(a_high, b_high, dims) + mm(a_high, b_low, dims) + mm(a_low, b_high, dims)


def running_sum(ones, value):
    high, low = split_two(value)
    return mm(ones, high) + mm(ones, low)


def states_kernel(where, lens, gap, proj, state_out):
    step = pl.program_id(0)
    length = proj.shape[2]
    heads = state_out.shape[2]
    width = heads * 128
    first = lax.rem(step, where[3]) == 0
    base = position(where, step, length)
    ones = triangle(length, False)
    for p in range(proj.shape[1]):
        col, _, last_id, before = block_docs(lens, p, base, length)
        _, _, key, log_forget = gates(proj[0, p, :, :width], gap[...])
        cum = running_sum(ones, log_forget)
        last = cum[length - 1 :]
        khat = (key * jnp.where(col == last_id, jnp.exp(last - cum), 0.0)).astype(BF16)
        decay = jnp.where(last_id == before, jnp.exp(last), 0.0)
        for h in range(heads):
            at = slice(h * 128, h * 128 + 128)
            values = proj[0, p, :, width + h * 128 : width + h * 128 + 128].astype(BF16)
            made = mm(values, khat[:, at], TN)
            older = jnp.where(first, 0.0, state_out[p, 0, h, :128] * decay[:, at])
            state_out[p, 0, h, :128] = older + made
            kept = jnp.where(first, 1.0, state_out[p, 0, h, 128:])
            state_out[p, 0, h, 128:] = kept * decay[:, at]


def position(where, step, length):
    sub_run, part = lax.div(step, where[3]), lax.rem(step, where[3])
    return sub_run * where[1] + where[2] + part * length


def scan_kernel(reverse, count, steps, decays, states, out):
    now = jnp.zeros(out.shape[2:], F32)
    planes = states.shape[0]
    order = [(s, m) for s in range(steps) for m in range(planes)]
    for s, m in reversed(order) if reverse else order:
        out[m, s] = now.astype(BF16)
        kept = decays[m, s, 128:].astype(F32)[:1]
        now = now * kept + states[m, s, :128].astype(F32)


def forward_kernel(where, lens, gap, gain, proj, entering, heads_out, mixed_out, kept, state):
    step = pl.program_id(0)
    length = proj.shape[2]
    heads = state.shape[1]
    width = heads * 128

    @pl.when(lax.rem(step, where[3]) == 0)
    def _():
        state[...] = entering[:, 0].astype(F32)

    base = position(where, step, length)
    ones = triangle(length, False)
    row_index = lax.broadcasted_iota(jnp.int32, (length, length), 0)
    col_index = lax.broadcasted_iota(jnp.int32, (length, length), 1)
    for p in range(proj.shape[1]):
        col, row, last_id, before = block_docs(lens, p, base, length)
        _, _, key, log_forget = gates(proj[0, p, :, :width], gap[...])
        cum = running_sum(ones, log_forget)
        last = cum[length - 1 :]
        khat = (key * jnp.where(col == last_id, jnp.exp(last - cum), 0.0)).astype(BF16)
        decay = jnp.where(last_id == before, jnp.exp(last), 0.0)
        qt = proj[0, p, :, 2 * width : 3 * width].astype(BF16).astype(F32) * jnp.exp(cum)
        qe = jnp.where(col == before, qt, 0.0)
        kt = key * jnp.exp(-cum)
        visible = (col == row) & (row_index >= col_index)
        for h in range(heads):
            at = slice(h * 128, h * 128 + 128)
            values = proj[0, p, :, width + h * 128 : width + h * 128 + 128].astype(BF16)
            gate = proj[0, p, :, 3 * width + h * 128 : 3 * width + h * 128 + 128]
            now = state[p, h]
            kept[0, p, h] = now
            mixing = jnp.where(visible, mm_split(qt[:, at], kt[:, at], NT), 0.0).astype(BF16)
            mixed = mm(mixing, values) + mm_split(qe[:, at], now, NT)
            state[p, h] = now * decay[:, at] + mm(values, khat[:, at], TN)
            mixed_out[0, p, :, at] = mixed
            gated = mixed * (gate * jax.nn.sigmoid(gate))
            scale = lax.rsqrt(jnp.mean(gated * gated, axis=-1, keepdims=True) + EPSILON)
            heads_out[0, p, :, at] = (gated * scale * gain[:, at]).astype(BF16)


def gate_back_kernel(
    where, lens, gap, gain, proj, mixed_in, grad_heads, grad_out, grad_gate, group_part, run_out, state
):
    turn = pl.program_id(0)
    step = pl.num_programs(0) - 1 - turn
    length = proj.shape[2]
    heads = state.shape[1]
    width = heads * 128

    @pl.when(turn == 0)
    def _():
        group_part[...] = jnp.zeros_like(group_part)

    @pl.when(lax.rem(turn, where[3]) == 0)
    def _():
        state[...] = jnp.zeros_like(state)

    base = position(where, step, length)
    ones = triangle(length, False)
    for p in range(proj.shape[1]):
        col, _, last_id, before = block_docs(lens, p, base, length)
        _, _, _, log_forget = gates(proj[0, p, :, :width], gap[...])
        cum = running_sum(ones, log_forget)
        decay = jnp.where(last_id == before, jnp.exp(cum[length - 1 :]), 0.0)
        qt = proj[0, p, :, 2 * width : 3 * width].astype(BF16).astype(F32) * jnp.exp(cum)
        qe = jnp.where(col == before, qt, 0.0).astype(BF16)
        for h in range(heads):
            at = slice(h * 128, h * 128 + 128)
            gate = proj[0, p, :, 3 * width + h * 128 : 3 * width + h * 128 + 128]
            mixed = mixed_in[0, p, :, at]
            incoming = grad_heads[0, p, :, at].astype(F32)
            sigma = jax.nn.sigmoid(gate)
            act = gate * sigma
            gated = mixed * act
            scale = lax.rsqrt(jnp.mean(gated * gated, axis=-1, keepdims=True) + EPSILON)
            group_part[:, at] += jnp.sum(incoming * gated * scale, axis=0, keepdims=True)
            weighted = incoming * gain[:, at]
            inner = jnp.mean(weighted * gated, axis=-1, keepdims=True)
            grad_gated = scale * weighted - gated * (scale * scale * scale) * inner
            grad = grad_gated * act
            grad_out[0, p, :, at] = grad
            slope = sigma * (1.0 + gate * (1.0 - sigma))
            grad_gate[0, p, :, at] = (grad_gated * mixed * slope).astype(BF16)
            high, low = split_two(grad)
            own = mm(high, qe[:, at], TN) + mm(low, qe[:, at], TN)
            state[p, h] = state[p, h] * decay[:, at] + own
            run_out[p, 0, h] = state[p, h].astype(BF16)


def backward_kernel(
    where, lens, gap, proj, grad_out, grad_gate, kept, entering, grad_proj, gap_part, state
):
    turn = pl.program_id(0)
    step = pl.num_programs(0) - 1 - turn
    length = proj.shape[2]
    heads = state.shape[1]
    width = heads * 128

    @pl.when(turn == 0)
    def _():
        gap_part[...] = jnp.zeros_like(gap_part)

    @pl.when(lax.rem(turn, where[3]) == 0)
    def _():
        state[...] = entering[:, 0].astype(F32)

    base = position(where, step, length)
    ones = triangle(length, False)
    ones_up = triangle(length, True)
    row_index = lax.broadcasted_iota(jnp.int32, (length, length), 0)
    col_index = lax.broadcasted_iota(jnp.int32, (length, length), 1)
    for p in range(proj.shape[1]):
        col, row, last_id, before = block_docs(lens, p, base, length)
        open_gate, gap_gate, key, log_forget = gates(proj[0, p, :, :width], gap[...])
        cum = running_sum(ones, log_forget)
        last = cum[length - 1 :]
        ecum = jnp.exp(cum)
        encum = jnp.exp(-cum)
        tail = jnp.where(col == last_id, jnp.exp(last - cum), 0.0)
        khat = (key * tail).astype(BF16)
        decay = jnp.where(last_id == before, jnp.exp(last), 0.0)
        qt = proj[0, p, :, 2 * width : 3 * width].astype(BF16).astype(F32) * ecum
        enters = col == before
        qe = jnp.where(enters, qt, 0.0).astype(BF16)
        qt = qt.astype(BF16)
        kt = (key * encum).astype(BF16)
        visible = (col == row) & (row_index >= col_index)
        for h in range(heads):
            at = slice(h * 128, h * 128 + 128)
            values = proj[0, p, :, width + h * 128 : width + h * 128 + 128].astype(BF16)
            grad = grad_out[0, p, :, at]
            grad_enter = jnp.where(enters, grad, 0.0)
            grad, grad_low = split_two(grad)
            after = state[p, h]
            after_high, after_low = split_two(after)
            now = kept[0, p, h]
            mixing = jnp.where(visible, mm(qt[:, at], kt[:, at], NT), 0.0).astype(BF16)
            grad_mixing = mm(grad, values, NT) + mm(grad_low, values, NT)
            grad_mixing = jnp.where(visible, grad_mixing, 0.0).astype(BF16)
            grad_qt = mm(grad_mixing, kt[:, at]) + mm_split(grad_enter, now)
            grad_kt = mm(grad_mixing, qt[:, at], TN)
            grad_values = mm(mixing, grad, TN) + mm(khat[:, at], after_high, NT)
            grad_khat = mm(values, after_high) + mm(values, after_low)
            grad_decay = jnp.sum(after * now, axis=0, keepdims=True)
            own = mm(grad, qe[:, at], TN) + mm(grad_low, qe[:, at], TN)
            state[p, h] = after * decay[:, at] + own
            through = grad_khat * khat[:, at].astype(F32)
            grad_cum = (
                grad_qt * qt[:, at].astype(F32) - grad_kt * kt[:, at].astype(F32) - through
            )
            grad_last = jnp.sum(through, axis=0, keepdims=True) + grad_decay * decay[:, at]
            grad_log = running_sum(ones_up, grad_cum) + grad_last
            grad_keys = grad_kt * encum[:, at] + grad_khat * tail[:, at]
            grad_gap = grad_keys - grad_log / (1.0 - gap_gate[:, at])
            gap_part[:, at] += jnp.sum(grad_gap * open_gate[:, at], axis=0, keepdims=True)
            grad_forget = -grad_gap * gap_gate[:, at] * (1.0 - open_gate[:, at])
            made = (grad_forget, grad_values, grad_qt * ecum[:, at])
            for k, part in enumerate(made):
                start = k * width + h * 128
                grad_proj[0, p, :, start : start + 128] = part.astype(BF16)
        grad_proj[0, p, :, 3 * width :] = grad_gate[0, p]


def recur_call(kernel, steps, halves, reverse, where, ins, outs, scratch, flops, name):
    def index(kind, ndim):
        def place(turn, where_ref):
            step = steps - 1 - turn if reverse else turn
            run, half = lax.div(step, halves), lax.rem(step, halves)
            if kind == "near":
                return (lax.bitwise_xor(run, where_ref[0]), 0, half, 0)
            if kind == "rows":
                return (run, 0, half, 0)
            if kind == "block":
                return (step,) + (0,) * (ndim - 1)
            if kind == "run":
                return (0, run) + (0,) * (ndim - 2)
            return (0,) * ndim

        return place

    def spec(kind, block):
        if kind == "smem":
            return pl.BlockSpec(memory_space=pltpu.SMEM)
        return pl.BlockSpec(block, index(kind, len(block)))

    arrays = [array for array, _, _ in ins]
    moved = sum(a.size * a.dtype.itemsize for a in arrays)
    return pl.pallas_call(
        kernel,
        grid_spec=pltpu.PrefetchScalarGridSpec(
            num_scalar_prefetch=1,
            grid=(steps,),
            in_specs=[spec(kind, block or array.shape) for array, kind, block in ins],
            out_specs=[spec(kind, block or shape) for shape, _, kind, block in outs],
            scratch_shapes=scratch,
        ),
        out_shape=[jax.ShapeDtypeStruct(shape, dtype) for shape, dtype, _, _ in outs],
        compiler_params=pltpu.CompilerParams(
            dimension_semantics=("arbitrary",), vmem_limit_bytes=48 << 20
        ),
        cost_estimate=pl.CostEstimate(flops=flops // 20, bytes_accessed=moved // 20, transcendentals=0),
        name=name,
    )(where, *arrays)


def scan_call(decays, states, reverse):
    return pl.pallas_call(
        functools.partial(scan_kernel, reverse, states.shape[0], states.shape[1]),
        out_shape=jax.ShapeDtypeStruct(states.shape[:2] + (128, 128), BF16),
        name="scan_back" if reverse else "scan",
    )(decays, states)


def project_kernel(tiles, left, right, weights, *rest):
    out = rest[-1]
    step = pl.program_id(0)

    @pl.when(step < tiles)
    def _():
        out[0] = mm(left[...], weights[...])

    @pl.when(step >= tiles)
    def _():
        out[0] = mm(right[...], weights[...])


def project_call(made, first, count, left, right, weights):
    rows, width = left.shape
    columns = weights.shape[1]
    tile = min(256, rows)
    tiles = rows // tile
    shape = (count, rows, columns)
    in_specs = [
        pl.BlockSpec((tile, width), lambda i: (jnp.minimum(i, tiles - 1), 0)),
        pl.BlockSpec((tile, width), lambda i: (jnp.maximum(i - tiles, 0), 0)),
        pl.BlockSpec(weights.shape, lambda i: (0, 0), pipeline_mode=pl.Buffered(1)),
    ]
    arrays = [left, right, weights]
    if made is not None:
        in_specs.append(pl.BlockSpec(memory_space=pl.ANY))
        arrays.append(made)
    return pl.pallas_call(
        functools.partial(project_kernel, tiles),
        grid=(2 * tiles,),
        in_specs=in_specs,
        out_specs=pl.BlockSpec(
            (1, tile, columns), lambda i: (first + lax.div(i, tiles), lax.rem(i, tiles), 0)
        ),
        out_shape=jax.ShapeDtypeStruct(shape, F32),
        input_output_aliases={} if made is None else {3: 0},
        compiler_params=pltpu.CompilerParams(
            dimension_semantics=("arbitrary",), vmem_limit_bytes=40 << 20
        ),
        cost_estimate=pl.CostEstimate(
            flops=rows * width * columns // 5, bytes_accessed=rows * width, transcendentals=0
        ),
        name="project",
    )(*arrays)


def back_kernel(tiles, left, right, grads, weights, out_left, out_right, part):
    step = pl.program_id(0)
    made = mm(grads[0], weights[...], NT)

    @pl.when(step == 0)
    def _():
        part[...] = jnp.zeros_like(part)

    @pl.when(step < tiles)
    def _():
        out_left[...] = made.astype(BF16)
        part[...] += jnp.sum(made * left[...].astype(F32), axis=0, keepdims=True)

    @pl.when(step >= tiles)
    def _():
        out_right[...] = made.astype(BF16)
        part[...] += jnp.sum(made * right[...].astype(F32), axis=0, keepdims=True)


def back_call(grads, first, left, right, weights):
    rows, width = left.shape
    columns = weights.shape[1]
    tile = min(256, rows)
    tiles = rows // tile

    def one(i):
        return (jnp.minimum(i, tiles - 1), 0)

    def two(i):
        return (jnp.maximum(i - tiles, 0), 0)

    return pl.pallas_call(
        functools.partial(back_kernel, tiles),
        grid=(2 * tiles,),
        in_specs=[
            pl.BlockSpec((tile, width), one),
            pl.BlockSpec((tile, width), two),
            pl.BlockSpec(
                (1, tile, columns), lambda i: (first + lax.div(i, tiles), lax.rem(i, tiles), 0)
            ),
            pl.BlockSpec(weights.shape, lambda i: (0, 0), pipeline_mode=pl.Buffered(1)),
        ],
        out_specs=[
            pl.BlockSpec((tile, width), one),
            pl.BlockSpec((tile, width), two),
            pl.BlockSpec((1, width), lambda i: (0, 0)),
        ],
        out_shape=[jax.ShapeDtypeStruct((rows, width), BF16)] * 2
        + [jax.ShapeDtypeStruct((1, width), F32)],
        compiler_params=pltpu.CompilerParams(
            dimension_semantics=("arbitrary",), vmem_limit_bytes=40 << 20
        ),
        cost_estimate=pl.CostEstimate(
            flops=rows * width * columns // 5, bytes_accessed=rows * width, transcendentals=0
        ),
        name="project_back",
    )(left, right, grads, weights)


def feed_kernel(*refs):
    two_refs, cot_refs, (w_low, w_high, w_dn), outs = refs[0:2], refs[2:4], refs[4:7], refs[7:]
    units = w_dn.shape[0]
    half = w_low.shape[0]
    for k in range(2):
        act_out, grad_out, down_out, back_out = outs[4 * k : 4 * k + 4]
        pre = mm(two_refs[k][:, :half], w_low[...]) + mm(two_refs[k][:, half:], w_high[...])
        gate, up = pre[:, :units], pre[:, units:]
        sigma = jax.nn.sigmoid(gate)
        silu = gate * sigma
        act = (silu * up).astype(BF16)
        act_out[...] = act
        down_out[...] = mm(act, w_dn[...]).astype(BF16)
        grad_act = mm(cot_refs[k][...], w_dn[...], NT)
        grad_out[:, :units] = (grad_act * up * (sigma * (1.0 + gate * (1.0 - sigma)))).astype(BF16)
        grad_out[:, units:] = (grad_act * silu).astype(BF16)
        back_out[:, :half] = mm(grad_out[...], w_low[...], NT).astype(BF16)
        back_out[:, half:] = mm(grad_out[...], w_high[...], NT).astype(BF16)


def feed_call(two, cot, w_low, w_high, w_dn):
    rows, width = two[0].shape
    units = w_dn.shape[0]
    tile = min(256, rows)

    def cut(columns):
        return pl.BlockSpec((tile, columns), lambda i: (i, 0))

    def still(array):
        return pl.BlockSpec(array.shape, lambda i: (0, 0), pipeline_mode=pl.Buffered(1))

    sizes = (units, 2 * units, width, width)
    flops = 2 * 2 * rows * width * 6 * units
    return pl.pallas_call(
        feed_kernel,
        grid=(rows // tile,),
        in_specs=[cut(width)] * 4 + [still(w_low), still(w_high), still(w_dn)],
        out_specs=[cut(s) for s in sizes] * 2,
        out_shape=[jax.ShapeDtypeStruct((rows, s), BF16) for s in sizes] * 2,
        compiler_params=pltpu.CompilerParams(
            dimension_semantics=("arbitrary",), vmem_limit_bytes=58 << 20
        ),
        cost_estimate=pl.CostEstimate(
            flops=flops // 20, bytes_accessed=rows * width, transcendentals=0
        ),
        name="feed",
    )(*two, *cot, w_low, w_high, w_dn)


def outer_kernel(count, place, *refs):
    *inputs, out, total, left, right, sems = refs
    lefts, rights = inputs[:count], inputs[count:]
    if len(rights) < count:
        rights = [rights[0].at[k] for k in range(count)]
    step = pl.program_id(0)

    def fetch(block, slot):
        return (
            pltpu.make_async_copy(lefts[block], left.at[slot], sems.at[0, slot]),
            pltpu.make_async_copy(rights[block], right.at[slot], sems.at[1, slot]),
        )

    @pl.when(step == 0)
    def _():
        for copy in fetch(0, 0):
            copy.start()

    slot = lax.rem(step, 2)
    for block in range(1, count):

        @pl.when(step + 1 == block)
        def _(block=block):
            for copy in fetch(block, block % 2):
                copy.start()

    for copy in fetch(0, slot):
        copy.wait()

    @pl.when(step == 0)
    def _():
        total[...] = mm(left[0], right[0], TN)

    @pl.when(step > 0)
    def _():
        total[...] += mm(left[slot], right[slot], TN)

    @pl.when(step == count - 1)
    def _():
        place(out, total)


def outer_call(lefts, rights, shape, place, name):
    count = len(lefts)
    rows, m = lefts[0].shape
    n = rights[0].shape[-1]
    return pl.pallas_call(
        functools.partial(outer_kernel, count, place),
        grid=(count,),
        in_specs=[pl.BlockSpec(memory_space=pl.ANY)] * (count + len(rights)),
        out_specs=pl.BlockSpec(shape, lambda i: (0,) * len(shape), pipeline_mode=pl.Buffered(1)),
        out_shape=jax.ShapeDtypeStruct(shape, BF16),
        scratch_shapes=[
            pltpu.VMEM((m, n), F32),
            pltpu.VMEM((2, rows, m), BF16),
            pltpu.VMEM((2, rows, n), BF16),
            pltpu.SemaphoreType.DMA((2, 2)),
        ],
        compiler_params=pltpu.CompilerParams(
            dimension_semantics=("arbitrary",), vmem_limit_bytes=58 << 20
        ),
        cost_estimate=pl.CostEstimate(
            flops=count * rows * m * n // 10,
            bytes_accessed=rows * (m + n),
            transcendentals=0,
        ),
        name=name,
    )(*lefts, *rights)


def swap(value, across):
    return lax.ppermute(value, "seq", [(i, i ^ across) for i in range(lax.axis_size("seq"))])


CORE, XLINK, YLINK = 1, 2, 4
TILE = 128


def together(*values):
    return lax.optimization_barrier(values)


def plane_gather(own, beside=None, meet=None):
    half = own.shape[0] // 2
    got = {0: own, XLINK: swap(own, XLINK), YLINK: swap(own, YLINK), CORE: swap(own, CORE)}
    got, beside = together(got, beside)
    first = swap(got[YLINK][:half], XLINK)
    second = swap(got[XLINK][half:], YLINK)
    got[XLINK + CORE] = swap(got[XLINK], CORE)
    got[YLINK + CORE] = swap(got[YLINK], CORE)
    first, second, got, meet = together(first, second, got, meet)
    got[XLINK + YLINK] = jnp.concatenate([first, second])
    got[XLINK + YLINK + CORE] = jnp.concatenate([swap(first, CORE), swap(second, CORE)])
    return got, beside, meet


def add_low(a, b):
    return (a.astype(F32) + b.astype(F32)).astype(BF16)


def chip_sum(parts, a):
    return add_low(parts[a], swap(parts[a ^ CORE], CORE))


def plane_scatter(parts, chip=None, far=None, last=None):
    half = parts[0].shape[0] // 2
    chip = dict(chip or {})
    for a in (2, 4, 6, 0):
        if a not in chip:
            chip[a] = chip_sum(parts, a)
    mine_x = swap(chip[2][:half], XLINK)
    mine_y = swap(chip[4][half:], YLINK)
    from_x = swap(chip[6][:half], XLINK)
    from_y = swap(chip[6][half:], YLINK)
    mine_x, mine_y, from_x, from_y, far = together(mine_x, mine_y, from_x, from_y, far)
    for_y, for_x = add_low(chip[4][:half], from_x), add_low(chip[2][half:], from_y)
    if callable(last):
        for_y, for_x, far = together(for_y, for_x, far)
        last = last(far)
    last_x, last_y, last = together(swap(for_x, XLINK), swap(for_y, YLINK), last)
    low = chip[0][:half].astype(F32) + mine_x.astype(F32) + last_y.astype(F32)
    high = chip[0][half:].astype(F32) + mine_y.astype(F32) + last_x.astype(F32)
    return jnp.concatenate([low, high]), far, last


def whole_sum(value):
    for axis in ("seq", "mp"):
        count = lax.axis_size(axis)
        across = 1
        while across < count:
            value = value + lax.ppermute(value, axis, [(i, i ^ across) for i in range(count)])
            across *= 2
    return value


def pick(array, index, axis):
    return lax.dynamic_index_in_dim(array, index, axis, keepdims=False)


def plane_device(
    tokens,
    norm1_gain,
    w_mix_in,
    forget_gap,
    group_gain,
    w_mix_out,
    norm2_gain,
    w_gate_up,
    w_down,
    doc_lengths,
    out_cotangent,
):
    seq_count, mp_count = lax.axis_size("seq"), lax.axis_size("mp")
    seq_index, mp_index = lax.axis_index("seq"), lax.axis_index("mp")
    core, chip = seq_index % 2, seq_index // 2
    chips = seq_count // 2
    span, packs, width = tokens.shape
    rows = span * packs
    run = span * mp_count
    all_heads, head_size, _ = w_mix_out.shape
    heads = all_heads // seq_count
    chans = heads * head_size
    slice_d = width // seq_count

    def pack_major(array):
        return jnp.transpose(array, (1, 0, 2)).reshape(rows, width)

    def token_major(array):
        return jnp.transpose(array.reshape(packs, span, width), (1, 0, 2))

    def gather_shares(part):
        return lax.all_gather(part, "mp", axis=0).reshape((2, 2) + part.shape)

    def both_halves(pairs):
        mine = pick(pairs, core, 0)
        other = swap(pick(pairs, 1 - core, 0), CORE)
        return jnp.where(core == 0, mine, other), jnp.where(core == 0, other, mine)

    in_part = lax.dynamic_slice(
        w_mix_in, (0, 2 * core, chip * head_size), (width, 2, head_size)
    ).reshape(width, 2 * head_size)
    in_pairs = gather_shares(in_part)

    own = pack_major(tokens)
    scale_one = rms_scale(own)
    normed_own = (own * scale_one * norm1_gain).astype(BF16)

    small = pick(jnp.stack([forget_gap, group_gain]), chip, 1)[None]
    for bit in range(2):
        across = 1 << bit
        other = lax.ppermute(small, "mp", [(i, i ^ across) for i in range(mp_count)])
        low = (mp_index >> bit) % 2 == 0
        small = jnp.concatenate([jnp.where(low, small, other), jnp.where(low, other, small)])

    hidden_units = w_gate_up.shape[2]
    share = -(-hidden_units // (chips * TILE)) * TILE
    local_ff = 2 * share
    spare = share * chips - hidden_units
    begin = jnp.minimum(chip * share, hidden_units - share)
    gu_part = lax.dynamic_slice_in_dim(pick(w_gate_up, core, 1), begin, share, 1)
    dn_part = lax.dynamic_slice_in_dim(w_down, begin, share, 0)
    fresh = lax.broadcasted_iota(jnp.int32, (share, 1), 0) >= chip * share - begin
    dn_part = jnp.where(fresh, dn_part, jnp.zeros_like(dn_part))
    dn_part = lax.dynamic_slice_in_dim(dn_part, core * (share // 2), share // 2, 0)
    out_flat = w_mix_out.reshape(-1, width)
    normed, (gu_part, dn_part, small), in_pairs = plane_gather(
        normed_own, (gu_part, dn_part, small), in_pairs
    )
    gu_first, gu_second = gu_part[: width // 2], gu_part[width // 2 :]
    query_forget, value_gate = both_halves(in_pairs)
    w_in = jnp.concatenate(
        [
            part[j, :, k * head_size : (k + 1) * head_size]
            for part, k in ((query_forget, 1), (value_gate, 0), (query_forget, 0), (value_gate, 1))
            for j in range(2)
        ],
        axis=1,
    )

    cot_own = pack_major(lax.dynamic_slice_in_dim(out_cotangent, mp_index * span, span, 0))
    cot_low, gu_first, dn_part, _ = together(cot_own.astype(BF16), gu_first, dn_part, in_pairs)
    dn_pairs = gather_shares(dn_part)
    first_pairs = gather_shares(gu_first)

    small = pick(small.reshape(2, 2, 2, head_size), core, 0)
    gap_row, gain_row = small[:, 0].reshape(1, chans), small[:, 1].reshape(1, chans)

    projected = None
    for a in range(0, seq_count, 2):
        projected = project_call(projected, a, seq_count, normed[a], normed[a + 1], w_in)
    cot, projected, _ = plane_gather(cot_low, projected)
    projected = projected.reshape(seq_count, packs, span, 4 * chans)

    halves = span // BLOCK
    steps = seq_count * halves
    where = jnp.stack([seq_index, run, mp_index * span, halves]).astype(jnp.int32)
    block = (1, packs, BLOCK, chans)
    fv_block = (1, packs, BLOCK, 2 * chans)
    wide = (1, packs, BLOCK, 4 * chans)
    pairs = packs * heads
    runs_shape = (packs, seq_count, heads, head_size, head_size)
    run_block = (packs, 1, heads, head_size, head_size)
    tall_shape = (packs, seq_count, heads, head_size + 8, head_size)
    tall_block = (packs, 1, heads, head_size + 8, head_size)
    unit = 2 * BLOCK * head_size * head_size * pairs * steps
    common = [(doc_lengths, "smem", None), (gap_row, "whole", None)]
    call = functools.partial(recur_call, steps=steps, halves=halves, where=where)

    def to_scan(array):
        array = jnp.transpose(array, (0, 2, 1, 3, 4)).astype(BF16)
        array = array.reshape((pairs,) + array.shape[2:])
        return lax.all_to_all(array, "mp", split_axis=0, concat_axis=0, tiled=True)

    def from_scan(array):
        array = lax.all_to_all(array, "mp", split_axis=0, concat_axis=0, tiled=True)
        array = array.reshape((packs, heads) + array.shape[1:])
        return jnp.transpose(array, (0, 2, 1, 3, 4))

    [run_state] = call(
        states_kernel,
        reverse=False,
        ins=common + [(projected, "near", fv_block)],
        outs=[(tall_shape, F32, "run", tall_block)],
        scratch=[],
        flops=3 * unit,
        name="run_states",
    )
    decays = to_scan(run_state)
    entering = from_scan(scan_call(decays, decays, False))
    row_shape = (seq_count, packs, span, chans)
    state_shape = (packs, heads, head_size, head_size)
    heads_out, mixed, kept = call(
        forward_kernel,
        reverse=False,
        ins=common
        + [(gain_row, "whole", None), (projected, "near", wide), (entering, "run", run_block)],
        outs=[
            (row_shape, BF16, "rows", block),
            (row_shape, F32, "rows", block),
            ((steps,) + state_shape, F32, "block", (1,) + state_shape),
        ],
        scratch=[pltpu.VMEM(state_shape, F32)],
        flops=6 * unit,
        name="mix_forward",
    )
    gu_second, dn_pairs, first_pairs, cot, _ = together(
        gu_second, dn_pairs, first_pairs, cot, entering
    )
    second_pairs = gather_shares(gu_second)

    def side_by_side(pairs):
        gate, up = both_halves(pairs)
        return jnp.concatenate([gate[0], gate[1], up[0], up[1]], axis=1)

    w_dn = jnp.concatenate(both_halves(dn_pairs), axis=1).reshape(local_ff, width)
    w_low, w_high = side_by_side(first_pairs), side_by_side(second_pairs)

    split = (chips, 2, rows, 2, head_size)
    heads_tok = lax.all_to_all(
        heads_out.reshape(seq_count, rows, chans), "seq", split_axis=0, concat_axis=0, tiled=True
    )
    heads_tok = jnp.transpose(heads_tok.reshape(split), (2, 1, 3, 0, 4)).reshape(rows, -1)
    hidden = own + mm(heads_tok, out_flat)
    scale_two = rms_scale(hidden)
    normed_two = (hidden * scale_two * norm2_gain).astype(BF16)

    def ready(parts):
        mine = pick(parts, core, 0)
        other = swap(pick(parts, 1 - core, 0), CORE)
        low = jnp.where(core == 0, mine, other)
        high = jnp.where(core == 0, other, mine)
        return jnp.concatenate([low, high])

    def deliver(terms):
        return lax.psum_scatter(terms, "mp", scatter_dimension=0, tiled=True)[0]

    def hand_round(piece):
        got = [pick(piece, chip, 0)]
        got += [swap(pick(piece, chip ^ a, 0), 2 * a) for a in range(1, chips)]
        got = jnp.stack(got)
        return [pick(got, chip ^ c, 0) for c in range(chips)]

    act, grad_gu, down_parts, back_parts = {}, {}, {}, {}
    order = range(seq_count)

    def feed(a):
        made = feed_call((two[a], two[a + 1]), (cot[a], cot[a + 1]), w_low, w_high, w_dn)
        for k, at in enumerate((a, a + 1)):
            act[at], grad_gu[at], down_parts[at], back_parts[at] = made[4 * k : 4 * k + 4]

    two = {0: normed_two}
    for across in (CORE, XLINK, YLINK):
        two[across] = swap(normed_two, across)
    feed(0)
    two[XLINK], two[YLINK], down_parts[0] = together(two[XLINK], two[YLINK], down_parts[0])
    middle = rows // 2
    far_first = swap(two[YLINK][:middle], XLINK)
    far_second = swap(two[XLINK][middle:], YLINK)
    two[3], two[5] = swap(two[XLINK], CORE), swap(two[YLINK], CORE)
    feed(2)
    two[YLINK], down_parts[2] = together(two[YLINK], down_parts[2])
    feed(4)
    chip_back = {2: chip_sum(back_parts, 2)}
    far_first, far_second, chip_back, down_parts[4] = together(
        far_first, far_second, chip_back, down_parts[4]
    )
    two[6] = jnp.concatenate([far_first, far_second])
    two[7] = jnp.concatenate([swap(far_first, CORE), swap(far_second, CORE)])
    feed(6)
    for a in (4, 6, 0):
        chip_back[a] = chip_sum(back_parts, a)

    def place_gu(out, total):
        for d in range(seq_count):
            for j in range(2):
                for g in range(2):
                    at = (2 * g + j) * share
                    out[d % 2, j, d // 2, g] = total[
                        d * slice_d : (d + 1) * slice_d, at : at + share
                    ].astype(BF16)

    def place_dn(out, total):
        for d in range(seq_count):
            for j in range(2):
                out[d % 2, j, d // 2] = total[
                    j * share : (j + 1) * share, d * slice_d : (d + 1) * slice_d
                ].astype(BF16)

    chip_back, grad_gu = together(chip_back, grad_gu)
    gu_grad = outer_call(
        [two[a] for a in order],
        [grad_gu[a] for a in order],
        (2, 2, chips, 2, slice_d, share),
        place_gu,
        "gate_up_grad",
    )

    def during_last(gu_grad):
        held, first_act = together(gu_grad, act[0])
        dn_grad = outer_call(
            [first_act] + [act[a] for a in order[1:]],
            [cot[a] for a in order],
            (2, 2, chips, share, slice_d),
            place_dn,
            "down_grad",
        )
        return ready(held), dn_grad

    grad_normed_two, _, (gu_grad, dn_grad) = plane_scatter(
        back_parts, chip_back, gu_grad, during_last
    )
    grad_normed_two, down_parts = together(grad_normed_two, down_parts)
    gu_grad = deliver(gu_grad)

    norm2_part = jnp.sum(grad_normed_two * hidden * scale_two, axis=0)
    grad_hidden = cot_own + rms_back(grad_normed_two, hidden, scale_two, norm2_gain)
    grad_mix = grad_hidden.astype(BF16)
    grad_tok = mm(grad_mix, out_flat, NT).astype(BF16)
    grad_tok = jnp.transpose(
        grad_tok.reshape(rows, 2, 2, chips, head_size), (3, 1, 0, 2, 4)
    ).reshape(seq_count, rows, chans)
    grad_tok, dn_grad = together(grad_tok, ready(dn_grad))
    dn_grad = deliver(dn_grad)
    grad_heads = lax.all_to_all(grad_tok, "seq", split_axis=0, concat_axis=0, tiled=True)
    grad_heads = grad_heads.reshape(row_shape)

    out_grad = mm(heads_tok, grad_mix, TN).astype(BF16)
    out_grad = out_grad.reshape(all_heads, seq_count, head_size // seq_count, width)

    grad_out, grad_gate, group_part, run_grad = call(
        gate_back_kernel,
        reverse=True,
        ins=common
        + [
            (gain_row, "whole", None),
            (projected, "near", wide),
            (mixed, "rows", block),
            (grad_heads, "rows", block),
        ],
        outs=[
            (row_shape, F32, "rows", block),
            (row_shape, BF16, "rows", block),
            ((1, chans), F32, "whole", None),
            (runs_shape, BF16, "run", run_block),
        ],
        scratch=[pltpu.VMEM(state_shape, F32)],
        flops=3 * unit,
        name="gate_back",
    )
    entering_back = from_scan(scan_call(decays, to_scan(run_grad), True))
    out_grad = plane_scatter(
        {a: pick(out_grad, seq_index ^ a, 1) for a in range(seq_count)}, None, entering_back
    )[0].astype(BF16)
    mix_out_grad = lax.psum_scatter(out_grad, "mp", scatter_dimension=0, tiled=True).astype(F32)
    grad_projected, gap_part = call(
        backward_kernel,
        reverse=True,
        ins=common
        + [
            (projected, "near", wide),
            (grad_out, "rows", block),
            (grad_gate, "rows", block),
            (kept, "block", (1,) + state_shape),
            (entering_back, "run", run_block),
        ],
        outs=[
            ((seq_count, packs, span, 4 * chans), BF16, "near", wide),
            ((1, chans), F32, "whole", None),
        ],
        scratch=[pltpu.VMEM(state_shape, F32)],
        flops=12 * unit,
        name="mix_backward",
    )
    grad_projected = grad_projected.reshape(seq_count, rows, 4 * chans)
    def place_in(out, total):
        for d in range(seq_count):
            for j in range(2):
                for k, of in enumerate((2, 0, 1, 3)):
                    at = of * chans + j * head_size
                    out[d % 2, j, d // 2, :, k * head_size : (k + 1) * head_size] = total[
                        d * slice_d : (d + 1) * slice_d, at : at + head_size
                    ].astype(BF16)

    in_grad = outer_call(
        [normed[a] for a in order],
        [grad_projected],
        (2, 2, chips, slice_d, 4 * head_size),
        place_in,
        "mix_in_grad",
    )
    grad_projected, in_grad = together(grad_projected, in_grad)
    in_parts, norm1_part, chip_in = {}, 0.0, {}
    in_grad = ready(in_grad)
    for a in (2, 4, 0, 6):
        in_parts[a], in_parts[a + 1], part = back_call(
            grad_projected, a, normed[a], normed[a + 1], w_in
        )
        norm1_part = norm1_part + part
        if a == 2:
            grad_projected, in_grad, part = together(grad_projected, in_grad, part)
            in_grad = deliver(in_grad)
        elif a != 6:
            chip_in[2 if a == 4 else 4] = chip_sum(in_parts, 2 if a == 4 else 4)
            grad_projected, chip_in, part = together(grad_projected, chip_in, part)
    norm1_part = norm1_part[0] / norm1_gain
    layer_out = token_major(
        hidden + plane_scatter(down_parts, None, entering_back, grad_projected)[0]
    )
    got = [q.astype(F32) for q in hand_round(gu_grad)]
    got[-1] = got[-1][:, :, spare:]
    gate_up_grad = jnp.transpose(jnp.concatenate(got, axis=-1), (1, 0, 2))
    got = hand_round(dn_grad)
    got[-1] = got[-1][spare:]
    down_grad = jnp.concatenate(got, axis=0).astype(F32)

    grad_normed, _, (gate_up_grad, down_grad, layer_out) = plane_scatter(
        in_parts, chip_in, None, (gate_up_grad, down_grad, layer_out)
    )
    got = [q.astype(F32).reshape(slice_d, 4, head_size) for q in hand_round(in_grad)]
    mix_in_grad = jnp.concatenate(got, axis=-1)

    tokens_grad = token_major(
        grad_hidden + rms_back(grad_normed, own, scale_one, norm1_gain)
    )

    def set_heads(part):
        row = jnp.zeros((2, 2, chips, head_size), F32)
        mine = part.reshape(1, 2, 1, head_size)
        return lax.dynamic_update_slice(row, mine, (core, 0, chip, 0)).reshape(-1)

    gains = whole_sum(
        jnp.stack([norm1_part, norm2_part, set_heads(gap_part), set_heads(group_part)])
    )
    own_slice = width // (seq_count * mp_count)
    norms = lax.dynamic_slice_in_dim(
        gains[:2], (seq_index * mp_count + mp_index) * own_slice, own_slice, 1
    )
    tall, narrow = all_heads // mp_count, head_size // seq_count
    small = lax.dynamic_slice(
        gains[2:].reshape(2, all_heads, head_size),
        (0, mp_index * tall, seq_index * narrow),
        (2, tall, narrow),
    )
    return (
        layer_out,
        tokens_grad,
        norms[0],
        mix_in_grad,
        small[0],
        small[1],
        mix_out_grad,
        norms[1],
        gate_up_grad,
        down_grad,
    )


def solution(mesh):
    body = plane_device if dict(mesh.shape) == {"seq": 8, "mp": 4} else generic_device
    placed = (
        P(("seq", "mp"), None, None),
        P(),
        P(None, None, "mp"),
        P("mp", None),
        P("mp", None),
        P(),
        P(),
        P(None, None, "mp"),
        P("mp", None),
        P(),
        P("seq", None, None),
    )
    return jax.shard_map(
        body,
        mesh=mesh,
        in_specs=placed,
        out_specs=(
            P(("seq", "mp"), None, None),
            P(("seq", "mp"), None, None),
            P(("seq", "mp")),
            P("seq", None, "mp"),
            P("mp", "seq"),
            P("mp", "seq"),
            P("mp", "seq", None),
            P(("seq", "mp")),
            P("seq", None, "mp"),
            P("mp", "seq"),
        ),
        check_vma=False,
    )
```

```python
import functools

import jax
import jax.numpy as jnp
from jax import lax
from jax.experimental import pallas as pl
from jax.experimental.pallas import tpu as pltpu
from jax.sharding import PartitionSpec as P

BLOCK = 128


EPSILON = 1e-06
PRECISE = lax.Precision.HIGHEST


def entering(x, axis, combine, identity, reverse):
    length, index = (lax.axis_size(axis), lax.axis_index(axis))
    everything = jax.tree.map(
        lambda part, kind: lax.all_gather(part.astype(kind), axis), x, (jnp.bfloat16, jnp.bfloat16)
    )
    start = jax.tree.map(
        lambda part, zero: jnp.broadcast_to(jnp.asarray(zero, part.dtype), part.shape), x, identity
    )

    def turn(k, before):
        at = length - 1 - k if reverse else k
        reached = at > index if reverse else at < index
        new = combine(
            before, jax.tree.map(lambda part, own: part[at].astype(own.dtype), everything, x)
        )
        return jax.tree.map(lambda a, b: jnp.where(reached, a, b), new, before)

    return lax.fori_loop(0, length, turn, start)


def rounded(signal):
    return lax.optimization_barrier(signal.astype(jnp.bfloat16)).astype(jnp.float32)


def rms_scale(signal):
    return lax.rsqrt(jnp.mean(signal * signal, axis=-1, keepdims=True) + EPSILON)


def rms_back(gradient, signal, scaling, gain_vec):
    weighted = gradient * gain_vec
    inner_sum = jnp.mean(weighted * signal, axis=-1, keepdims=True)
    return scaling * weighted - signal * (scaling * scaling * scaling) * inner_sum


def silu_slope(signal):
    sigma_val = jax.nn.sigmoid(signal)
    return sigma_val * (1.0 + signal * (1.0 - sigma_val))


def doc_index(doc_lengths, positions):
    doc_ends = jnp.stack(
        [jnp.sum(doc_lengths[:, : k + 1], axis=1) for k in range(doc_lengths.shape[1])], axis=1
    )
    return jnp.sum((positions[:, None, None] >= doc_ends[None, :, :]).astype(jnp.int32), axis=2)


def chain_combine(earlier, later_part):
    return (earlier[0] * later_part[0], later_part[0][..., None] * earlier[1] + later_part[1])


def block_tables(log_forget, doc_ids, previous):
    length = log_forget.shape[1]
    row_index = lax.broadcasted_iota(jnp.int32, (length, length), 0)
    col_index = lax.broadcasted_iota(jnp.int32, (length, length), 1)
    lower_ones = (row_index >= col_index).astype(jnp.float32)
    cumulated = jnp.einsum("ij,njshk->nishk", lower_ones, log_forget, precision=PRECISE)
    last_sum = cumulated[:, -1]
    same_doc = doc_ids[:, :, None, :] == doc_ids[:, None, :, :]
    visible = jnp.transpose(same_doc & (row_index >= col_index)[None, :, :, None], (0, 3, 1, 2))[
        :, :, None
    ]
    enters = (doc_ids == previous[:, None, :]).astype(jnp.float32)[..., None, None]
    at_end = (doc_ids == doc_ids[:, -1:, :]).astype(jnp.float32)[..., None, None]
    alive_end = (doc_ids[:, -1] == previous).astype(jnp.float32)[..., None, None]
    decays = jnp.exp(last_sum) * alive_end
    return (lower_ones, cumulated, last_sum, visible, enters, at_end, decays)


def block_factors(queries, key_vec, cumulated, last_sum, at_end):
    q_tilde = queries * jnp.exp(cumulated)
    k_tilde = key_vec * jnp.exp(-cumulated)
    k_hat = key_vec * jnp.exp(last_sum[:, None] - cumulated) * at_end
    return (q_tilde, k_tilde, k_hat)


def recur_forward(queries, key_vec, values_in, log_forget, doc_ids, previous):
    lower_ones, cumulated, last_sum, visible, enters, at_end, decays = block_tables(
        log_forget, doc_ids, previous
    )
    q_tilde, k_tilde, k_hat = block_factors(queries, key_vec, cumulated, last_sum, at_end)
    scores = jnp.einsum("nishk,njshk->nshij", q_tilde, k_tilde, precision=PRECISE)
    mixing = jnp.where(visible, scores, 0.0)
    inside = jnp.einsum("nshij,njshv->nishv", mixing, values_in, precision=PRECISE)
    local_sum = jnp.einsum("njshk,njshv->nshkv", k_hat, values_in, precision=PRECISE)

    def advance(carried, element):
        state_now, product = carried
        factor, addend = element
        return ((factor[..., None] * state_now + addend, product * factor), (state_now, product))

    zero_state = jnp.zeros(local_sum.shape[1:], jnp.float32)
    unit_decay = jnp.ones(decays.shape[1:], jnp.float32)
    (run_state, run_decay), (prefix_state, prefix_decay) = lax.scan(
        advance, (zero_state, unit_decay), (decays, local_sum)
    )
    incoming = entering(
        (run_decay, run_state), "seq", chain_combine, (unit_decay, zero_state), False
    )[1]
    start_state = prefix_state + prefix_decay[..., None] * incoming[None]
    carried_in = jnp.einsum("nishk,nshkv->nishv", q_tilde * enters, start_state, precision=PRECISE)
    return (inside + carried_in, start_state)


def recur_backward(
    queries, key_vec, values_in, log_forget, doc_ids, previous, start_state, grad_out
):
    lower_ones, cumulated, last_sum, visible, enters, at_end, decays = block_tables(
        log_forget, doc_ids, previous
    )
    q_tilde, k_tilde, k_hat = block_factors(queries, key_vec, cumulated, last_sum, at_end)
    scores = jnp.einsum("nishk,njshk->nshij", q_tilde, k_tilde, precision=PRECISE)
    mixing = jnp.where(visible, scores, 0.0)
    own_term = jnp.einsum("nishk,nishv->nshkv", q_tilde * enters, grad_out, precision=PRECISE)

    def retreat(carried, element):
        running, product = carried
        factor, addend = element
        return ((addend + factor[..., None] * running, product * factor), (running, product))

    zero_state = jnp.zeros(own_term.shape[1:], jnp.float32)
    unit_decay = jnp.ones(decays.shape[1:], jnp.float32)
    (run_grad, run_decay), (after_sum, after_decay) = lax.scan(
        retreat, (zero_state, unit_decay), (decays, own_term), reverse=True
    )
    outgoing = entering(
        (run_decay, run_grad), "seq", chain_combine, (unit_decay, zero_state), True
    )[1]
    next_grad = after_sum + after_decay[..., None] * outgoing[None]
    grad_mixing = jnp.where(
        visible, jnp.einsum("nishv,njshv->nshij", grad_out, values_in, precision=PRECISE), 0.0
    )
    grad_qt = jnp.einsum("nshij,njshk->nishk", grad_mixing, k_tilde, precision=PRECISE)
    grad_qt = grad_qt + jnp.einsum(
        "nishv,nshkv->nishk", grad_out * enters, start_state, precision=PRECISE
    )
    grad_kt = jnp.einsum("nshij,nishk->njshk", grad_mixing, q_tilde, precision=PRECISE)
    grad_values = jnp.einsum("nshij,nishv->njshv", mixing, grad_out, precision=PRECISE)
    grad_values = grad_values + jnp.einsum(
        "njshk,nshkv->njshv", k_hat, next_grad, precision=PRECISE
    )
    grad_khat = jnp.einsum("njshv,nshkv->njshk", values_in, next_grad, precision=PRECISE) * at_end
    grad_decay = jnp.sum(next_grad * start_state, axis=-1)
    grad_queries = grad_qt * jnp.exp(cumulated)
    grad_keys = grad_kt * jnp.exp(-cumulated) + grad_khat * jnp.exp(last_sum[:, None] - cumulated)
    grad_cum = grad_qt * q_tilde - grad_kt * k_tilde - grad_khat * k_hat
    grad_last = jnp.sum(grad_khat * k_hat, axis=1) + grad_decay * decays
    grad_log = (
        jnp.einsum("it,nishk->ntshk", lower_ones, grad_cum, precision=PRECISE) + grad_last[:, None]
    )
    return (grad_queries, grad_keys, grad_values, grad_log)


def generic_device(
    tokens,
    norm1_gain,
    w_mix_in,
    forget_gap,
    group_gain,
    w_mix_out,
    norm2_gain,
    w_gate_up,
    w_down,
    doc_lengths,
    out_cotangent,
):
    mp_count = lax.axis_size("mp")
    rows_dev, pack_count, model_width = tokens.shape
    run_length = rows_dev * mp_count
    blocks = run_length // BLOCK
    local_heads, head_size = forget_gap.shape
    local_chans = local_heads * head_size
    local_ff = w_gate_up.shape[2]
    mp_index = lax.axis_index("mp")
    run_start = lax.axis_index("seq") * run_length
    positions = run_start - 1 + jnp.arange(run_length + 1, dtype=jnp.int32)
    all_ids = doc_index(doc_lengths, positions)
    doc_ids = all_ids[1:].reshape(blocks, BLOCK, pack_count)
    previous = all_ids[0:run_length:BLOCK]
    shape_blocks = (blocks, BLOCK, pack_count, local_heads, head_size)
    shape_heads = (run_length, pack_count, local_heads, head_size)
    shape_flat = (run_length, pack_count, local_chans)
    scale_one = rms_scale(tokens)
    normed = (tokens * scale_one * norm1_gain).astype(jnp.bfloat16)
    in_flat = w_mix_in.reshape(model_width, 4 * local_chans)
    shard_rows = lax.all_gather(normed, "mp", axis=0, tiled=True)
    normed_all = shard_rows
    projected = jnp.einsum("tsd,dc->tsc", shard_rows, in_flat, preferred_element_type=jnp.float32)
    pre_query = projected[..., :local_chans]
    pre_forget = projected[..., local_chans : 2 * local_chans]
    pre_value = projected[..., 2 * local_chans : 3 * local_chans]
    pre_gate = projected[..., 3 * local_chans :]
    open_gate = jax.nn.sigmoid(-pre_forget)
    gap_gate = forget_gap.reshape(local_chans) * open_gate
    queries = rounded(pre_query).reshape(shape_blocks)
    key_vec = rounded(gap_gate).reshape(shape_blocks)
    values_in = rounded(pre_value).reshape(shape_blocks)
    log_forget = jnp.log1p(-gap_gate).reshape(shape_blocks)
    mixed, start_state = recur_forward(queries, key_vec, values_in, log_forget, doc_ids, previous)
    mixed = mixed.reshape(shape_flat)
    gate_act = jax.nn.silu(pre_gate)
    gated_four = (mixed * gate_act).reshape(shape_heads)
    scale_group = rms_scale(gated_four)
    heads_out = (gated_four * scale_group * group_gain).astype(jnp.bfloat16).reshape(shape_flat)
    heads_tok = lax.all_to_all(heads_out, "mp", split_axis=0, concat_axis=2, tiled=True)
    out_flat = w_mix_out.reshape(-1, model_width)
    hidden = tokens + jnp.einsum(
        "tsc,cd->tsd", heads_tok, out_flat, preferred_element_type=jnp.float32
    )
    scale_two = rms_scale(hidden)
    normed_two = (hidden * scale_two * norm2_gain).astype(jnp.bfloat16)
    ffn_flat = w_gate_up.reshape(model_width, 2 * local_ff)
    shard_rows = lax.all_gather(normed_two, "mp", axis=0, tiled=True)
    gate_up = jnp.einsum("tsd,dc->tsc", shard_rows, ffn_flat, preferred_element_type=jnp.float32)
    pre_gate_two = gate_up[..., :local_ff]
    pre_up = gate_up[..., local_ff:]
    silu_two = jax.nn.silu(pre_gate_two)
    activation = (silu_two * pre_up).astype(jnp.bfloat16)
    partial_value = activation
    ffn_sum = lax.psum_scatter(
        jnp.einsum("tsf,fd->tsd", partial_value, w_down, preferred_element_type=jnp.float32).astype(
            jnp.bfloat16
        ),
        "mp",
        scatter_dimension=0,
        tiled=True,
    ).astype(jnp.float32)
    layer_out = hidden + ffn_sum
    cot_low = out_cotangent.astype(jnp.bfloat16)
    cot_own = lax.dynamic_slice_in_dim(out_cotangent, mp_index * rows_dev, rows_dev, 0)
    down_part = jnp.einsum("tsf,tsd->fd", activation, cot_low, preferred_element_type=jnp.float32)
    grad_act = jnp.einsum("tsd,fd->tsf", cot_low, w_down, preferred_element_type=jnp.float32)
    grad_gate_two = grad_act * pre_up * silu_slope(pre_gate_two)
    grad_up = grad_act * silu_two
    grad_gate_up = jnp.concatenate([grad_gate_two, grad_up], axis=-1).astype(jnp.bfloat16)
    gate_up_part = jnp.einsum(
        "tsd,tsc->dc", shard_rows, grad_gate_up, preferred_element_type=jnp.float32
    )
    gate_up_part = gate_up_part.reshape(model_width, 2, local_ff)
    partial_value = grad_gate_up
    grad_normed_two = lax.psum_scatter(
        jnp.einsum(
            "tsc,dc->tsd", partial_value, ffn_flat, preferred_element_type=jnp.float32
        ).astype(jnp.bfloat16),
        "mp",
        scatter_dimension=0,
        tiled=True,
    ).astype(jnp.float32)
    norm2_part = jnp.sum(grad_normed_two * hidden * scale_two, axis=(0, 1))
    grad_hidden = cot_own + rms_back(grad_normed_two, hidden, scale_two, norm2_gain)
    grad_mix = grad_hidden.astype(jnp.bfloat16)
    out_part = jnp.einsum("tsc,tsd->cd", heads_tok, grad_mix, preferred_element_type=jnp.float32)
    grad_tok = jnp.einsum(
        "tsd,cd->tsc", grad_mix, out_flat, preferred_element_type=jnp.float32
    ).astype(jnp.bfloat16)
    grad_heads = lax.all_to_all(grad_tok, "mp", split_axis=2, concat_axis=0, tiled=True).astype(
        jnp.float32
    )
    grad_four = grad_heads.reshape(shape_heads)
    group_part = jnp.sum(grad_four * gated_four * scale_group, axis=(0, 1))
    grad_gated = rms_back(grad_four, gated_four, scale_group, group_gain).reshape(shape_flat)
    grad_mixed = grad_gated * gate_act
    grad_gate_in = grad_gated * mixed * silu_slope(pre_gate)
    grad_queries, grad_keys, grad_values, grad_log = recur_backward(
        queries,
        key_vec,
        values_in,
        log_forget,
        doc_ids,
        previous,
        start_state,
        grad_mixed.reshape(shape_blocks),
    )
    grad_gap = grad_keys.reshape(shape_flat) - grad_log.reshape(shape_flat) / (1.0 - gap_gate)
    gap_part = jnp.sum(grad_gap * open_gate, axis=(0, 1)).reshape(local_heads, head_size)
    grad_forget_in = -grad_gap * gap_gate * (1.0 - open_gate)
    grad_projected = jnp.concatenate(
        [
            grad_queries.reshape(shape_flat),
            grad_forget_in,
            grad_values.reshape(shape_flat),
            grad_gate_in,
        ],
        axis=-1,
    ).astype(jnp.bfloat16)
    mix_in_part = jnp.einsum(
        "tsd,tsc->dc", normed_all, grad_projected, preferred_element_type=jnp.float32
    )
    mix_in_part = mix_in_part.reshape(model_width, 4, local_chans)
    partial_value = grad_projected
    grad_normed = lax.psum_scatter(
        jnp.einsum(
            "tsc,dc->tsd", partial_value, in_flat, preferred_element_type=jnp.float32
        ).astype(jnp.bfloat16),
        "mp",
        scatter_dimension=0,
        tiled=True,
    ).astype(jnp.float32)
    norm1_part = jnp.sum(grad_normed * tokens * scale_one, axis=(0, 1))
    tokens_grad = grad_hidden + rms_back(grad_normed, tokens, scale_one, norm1_gain)
    seq_count = lax.axis_size("seq")
    arranged = out_part.reshape(
        mp_count, local_heads, seq_count, head_size // seq_count, model_width
    )
    arranged = jnp.transpose(arranged, (2, 0, 1, 3, 4)).reshape(
        seq_count * mp_count * local_heads, head_size // seq_count, model_width
    )
    mix_in_grad, gate_up_grad, down_grad, group_grad, gap_grad = (
        lax.psum_scatter(
            mix_in_part.astype(jnp.bfloat16), "seq", scatter_dimension=0, tiled=True
        ).astype(jnp.float32),
        lax.psum_scatter(
            gate_up_part.astype(jnp.bfloat16), "seq", scatter_dimension=0, tiled=True
        ).astype(jnp.float32),
        lax.psum_scatter(
            down_part.astype(jnp.bfloat16), "seq", scatter_dimension=1, tiled=True
        ).astype(jnp.float32),
        lax.psum_scatter(
            group_part.astype(jnp.bfloat16), "seq", scatter_dimension=1, tiled=True
        ).astype(jnp.float32),
        lax.psum_scatter(
            gap_part.astype(jnp.bfloat16), "seq", scatter_dimension=1, tiled=True
        ).astype(jnp.float32),
    )
    mix_out_grad, norm1_grad, norm2_grad = (
        lax.psum_scatter(arranged, ("seq", "mp"), scatter_dimension=0, tiled=True),
        lax.psum_scatter(norm1_part, ("seq", "mp"), scatter_dimension=0, tiled=True),
        lax.psum_scatter(norm2_part, ("seq", "mp"), scatter_dimension=0, tiled=True),
    )
    return (
        layer_out,
        tokens_grad,
        norm1_grad,
        mix_in_grad,
        gap_grad,
        group_grad,
        mix_out_grad,
        norm2_grad,
        gate_up_grad,
        down_grad,
    )


F32 = jnp.float32
BF16 = jnp.bfloat16


def mm(a, b, dims=((1,), (0,))):
    return lax.dot_general(a, b, (dims, ((), ())), preferred_element_type=F32)


NN, NT, TN = ((1,), (0,)), ((1,), (1,)), ((0,), (0,))


def split_two(value):
    high = value.astype(BF16)
    return high, (value - high.astype(F32)).astype(BF16)


def triangle(length, upper):
    row = lax.broadcasted_iota(jnp.int32, (length, length), 0)
    col = lax.broadcasted_iota(jnp.int32, (length, length), 1)
    return jnp.where((row <= col) if upper else (row >= col), 1.0, 0.0).astype(BF16)


def ids_of(lens, pack, positions):
    total, ids = 0, jnp.zeros_like(positions)
    for k in range(lens.shape[1]):
        total = total + lens[pack, k]
        ids = ids + jnp.where(positions >= total, 1, 0)
    return ids


def block_docs(lens, pack, base, length):
    col = ids_of(lens, pack, base + lax.broadcasted_iota(jnp.int32, (length, 1), 0))
    row = ids_of(lens, pack, base + lax.broadcasted_iota(jnp.int32, (1, length), 1))
    last = ids_of(lens, pack, base + length - 1 + jnp.zeros((1, 1), jnp.int32))
    before = ids_of(lens, pack, base - 1 + jnp.zeros((1, 1), jnp.int32))
    return col, row, last, before


def gates(pre_forget, gap):
    open_gate = jax.nn.sigmoid(-pre_forget)
    gap_gate = gap * open_gate
    return open_gate, gap_gate, gap_gate.astype(BF16).astype(F32), jnp.log1p(-gap_gate)


def mm_split(a, b, dims=((1,), (0,))):
    (a_high, a_low), (b_high, b_low) = split_two(a), split_two(b)
    return mm(a_high, b_high, dims) + mm(a_high, b_low, dims) + mm(a_low, b_high, dims)


def running_sum(ones, value):
    high, low = split_two(value)
    return mm(ones, high) + mm(ones, low)


def states_kernel(where, lens, gap, proj, state_out):
    step = pl.program_id(0)
    length = proj.shape[2]
    heads = state_out.shape[2]
    width = heads * 128
    first = lax.rem(step, where[3]) == 0
    base = position(where, step, length)
    ones = triangle(length, False)
    for p in range(proj.shape[1]):
        col, _, last_id, before = block_docs(lens, p, base, length)
        _, _, key, log_forget = gates(proj[0, p, :, :width], gap[...])
        cum = running_sum(ones, log_forget)
        last = cum[length - 1 :]
        khat = (key * jnp.where(col == last_id, jnp.exp(last - cum), 0.0)).astype(BF16)
        decay = jnp.where(last_id == before, jnp.exp(last), 0.0)
        for h in range(heads):
            at = slice(h * 128, h * 128 + 128)
            values = proj[0, p, :, width + h * 128 : width + h * 128 + 128].astype(BF16)
            made = mm(values, khat[:, at], TN)
            older = jnp.where(first, 0.0, state_out[p, 0, h, :128] * decay[:, at])
            state_out[p, 0, h, :128] = older + made
            kept = jnp.where(first, 1.0, state_out[p, 0, h, 128:])
            state_out[p, 0, h, 128:] = kept * decay[:, at]


def position(where, step, length):
    sub_run, part = lax.div(step, where[3]), lax.rem(step, where[3])
    return sub_run * where[1] + where[2] + part * length


def scan_kernel(reverse, count, steps, decays, states, out):
    now = jnp.zeros(out.shape[2:], F32)
    planes = states.shape[0]
    order = [(s, m) for s in range(steps) for m in range(planes)]
    for s, m in reversed(order) if reverse else order:
        out[m, s] = now.astype(BF16)
        kept = decays[m, s, 128:].astype(F32)[:1]
        now = now * kept + states[m, s, :128].astype(F32)


def forward_kernel(where, lens, gap, gain, proj, entering, heads_out, mixed_out, kept, state):
    step = pl.program_id(0)
    length = proj.shape[2]
    heads = state.shape[1]
    width = heads * 128

    @pl.when(lax.rem(step, where[3]) == 0)
    def _():
        state[...] = entering[:, 0].astype(F32)

    base = position(where, step, length)
    ones = triangle(length, False)
    row_index = lax.broadcasted_iota(jnp.int32, (length, length), 0)
    col_index = lax.broadcasted_iota(jnp.int32, (length, length), 1)
    for p in range(proj.shape[1]):
        col, row, last_id, before = block_docs(lens, p, base, length)
        _, _, key, log_forget = gates(proj[0, p, :, :width], gap[...])
        cum = running_sum(ones, log_forget)
        last = cum[length - 1 :]
        khat = (key * jnp.where(col == last_id, jnp.exp(last - cum), 0.0)).astype(BF16)
        decay = jnp.where(last_id == before, jnp.exp(last), 0.0)
        qt = proj[0, p, :, 2 * width : 3 * width].astype(BF16).astype(F32) * jnp.exp(cum)
        qe = jnp.where(col == before, qt, 0.0)
        kt = key * jnp.exp(-cum)
        visible = (col == row) & (row_index >= col_index)
        for h in range(heads):
            at = slice(h * 128, h * 128 + 128)
            values = proj[0, p, :, width + h * 128 : width + h * 128 + 128].astype(BF16)
            gate = proj[0, p, :, 3 * width + h * 128 : 3 * width + h * 128 + 128]
            now = state[p, h]
            kept[0, p, h] = now
            mixing = jnp.where(visible, mm_split(qt[:, at], kt[:, at], NT), 0.0).astype(BF16)
            mixed = mm(mixing, values) + mm_split(qe[:, at], now, NT)
            state[p, h] = now * decay[:, at] + mm(values, khat[:, at], TN)
            mixed_out[0, p, :, at] = mixed
            gated = mixed * (gate * jax.nn.sigmoid(gate))
            scale = lax.rsqrt(jnp.mean(gated * gated, axis=-1, keepdims=True) + EPSILON)
            heads_out[0, p, :, at] = (gated * scale * gain[:, at]).astype(BF16)


def gate_back_kernel(
    where, lens, gap, gain, proj, mixed_in, grad_heads, grad_out, grad_gate, group_part, run_out, state
):
    turn = pl.program_id(0)
    step = pl.num_programs(0) - 1 - turn
    length = proj.shape[2]
    heads = state.shape[1]
    width = heads * 128

    @pl.when(turn == 0)
    def _():
        group_part[...] = jnp.zeros_like(group_part)

    @pl.when(lax.rem(turn, where[3]) == 0)
    def _():
        state[...] = jnp.zeros_like(state)

    base = position(where, step, length)
    ones = triangle(length, False)
    for p in range(proj.shape[1]):
        col, _, last_id, before = block_docs(lens, p, base, length)
        _, _, _, log_forget = gates(proj[0, p, :, :width], gap[...])
        cum = running_sum(ones, log_forget)
        decay = jnp.where(last_id == before, jnp.exp(cum[length - 1 :]), 0.0)
        qt = proj[0, p, :, 2 * width : 3 * width].astype(BF16).astype(F32) * jnp.exp(cum)
        qe = jnp.where(col == before, qt, 0.0).astype(BF16)
        for h in range(heads):
            at = slice(h * 128, h * 128 + 128)
            gate = proj[0, p, :, 3 * width + h * 128 : 3 * width + h * 128 + 128]
            mixed = mixed_in[0, p, :, at]
            incoming = grad_heads[0, p, :, at].astype(F32)
            sigma = jax.nn.sigmoid(gate)
            act = gate * sigma
            gated = mixed * act
            scale = lax.rsqrt(jnp.mean(gated * gated, axis=-1, keepdims=True) + EPSILON)
            group_part[:, at] += jnp.sum(incoming * gated * scale, axis=0, keepdims=True)
            weighted = incoming * gain[:, at]
            inner = jnp.mean(weighted * gated, axis=-1, keepdims=True)
            grad_gated = scale * weighted - gated * (scale * scale * scale) * inner
            grad = grad_gated * act
            grad_out[0, p, :, at] = grad
            slope = sigma * (1.0 + gate * (1.0 - sigma))
            grad_gate[0, p, :, at] = (grad_gated * mixed * slope).astype(BF16)
            high, low = split_two(grad)
            own = mm(high, qe[:, at], TN) + mm(low, qe[:, at], TN)
            state[p, h] = state[p, h] * decay[:, at] + own
            run_out[p, 0, h] = state[p, h].astype(BF16)


def backward_kernel(
    where, lens, gap, proj, grad_out, grad_gate, kept, entering, grad_proj, gap_part, state
):
    turn = pl.program_id(0)
    step = pl.num_programs(0) - 1 - turn
    length = proj.shape[2]
    heads = state.shape[1]
    width = heads * 128

    @pl.when(turn == 0)
    def _():
        gap_part[...] = jnp.zeros_like(gap_part)

    @pl.when(lax.rem(turn, where[3]) == 0)
    def _():
        state[...] = entering[:, 0].astype(F32)

    base = position(where, step, length)
    ones = triangle(length, False)
    ones_up = triangle(length, True)
    row_index = lax.broadcasted_iota(jnp.int32, (length, length), 0)
    col_index = lax.broadcasted_iota(jnp.int32, (length, length), 1)
    for p in range(proj.shape[1]):
        col, row, last_id, before = block_docs(lens, p, base, length)
        open_gate, gap_gate, key, log_forget = gates(proj[0, p, :, :width], gap[...])
        cum = running_sum(ones, log_forget)
        last = cum[length - 1 :]
        ecum = jnp.exp(cum)
        encum = jnp.exp(-cum)
        tail = jnp.where(col == last_id, jnp.exp(last - cum), 0.0)
        khat = (key * tail).astype(BF16)
        decay = jnp.where(last_id == before, jnp.exp(last), 0.0)
        qt = proj[0, p, :, 2 * width : 3 * width].astype(BF16).astype(F32) * ecum
        enters = col == before
        qe = jnp.where(enters, qt, 0.0).astype(BF16)
        qt = qt.astype(BF16)
        kt = (key * encum).astype(BF16)
        visible = (col == row) & (row_index >= col_index)
        for h in range(heads):
            at = slice(h * 128, h * 128 + 128)
            values = proj[0, p, :, width + h * 128 : width + h * 128 + 128].astype(BF16)
            grad = grad_out[0, p, :, at]
            grad_enter = jnp.where(enters, grad, 0.0)
            grad, grad_low = split_two(grad)
            after = state[p, h]
            after_high, after_low = split_two(after)
            now = kept[0, p, h]
            mixing = jnp.where(visible, mm(qt[:, at], kt[:, at], NT), 0.0).astype(BF16)
            grad_mixing = mm(grad, values, NT) + mm(grad_low, values, NT)
            grad_mixing = jnp.where(visible, grad_mixing, 0.0).astype(BF16)
            grad_qt = mm(grad_mixing, kt[:, at]) + mm_split(grad_enter, now)
            grad_kt = mm(grad_mixing, qt[:, at], TN)
            grad_values = mm(mixing, grad, TN) + mm(khat[:, at], after_high, NT)
            grad_khat = mm(values, after_high) + mm(values, after_low)
            grad_decay = jnp.sum(after * now, axis=0, keepdims=True)
            own = mm(grad, qe[:, at], TN) + mm(grad_low, qe[:, at], TN)
            state[p, h] = after * decay[:, at] + own
            through = grad_khat * khat[:, at].astype(F32)
            grad_cum = (
                grad_qt * qt[:, at].astype(F32) - grad_kt * kt[:, at].astype(F32) - through
            )
            grad_last = jnp.sum(through, axis=0, keepdims=True) + grad_decay * decay[:, at]
            grad_log = running_sum(ones_up, grad_cum) + grad_last
            grad_keys = grad_kt * encum[:, at] + grad_khat * tail[:, at]
            grad_gap = grad_keys - grad_log / (1.0 - gap_gate[:, at])
            gap_part[:, at] += jnp.sum(grad_gap * open_gate[:, at], axis=0, keepdims=True)
            grad_forget = -grad_gap * gap_gate[:, at] * (1.0 - open_gate[:, at])
            made = (grad_forget, grad_values, grad_qt * ecum[:, at])
            for k, part in enumerate(made):
                start = k * width + h * 128
                grad_proj[0, p, :, start : start + 128] = part.astype(BF16)
        grad_proj[0, p, :, 3 * width :] = grad_gate[0, p]


def recur_call(kernel, steps, halves, reverse, where, ins, outs, scratch, flops, name):
    def index(kind, ndim):
        def place(turn, where_ref):
            step = steps - 1 - turn if reverse else turn
            run, half = lax.div(step, halves), lax.rem(step, halves)
            if kind == "near":
                return (lax.bitwise_xor(run, where_ref[0]), 0, half, 0)
            if kind == "rows":
                return (run, 0, half, 0)
            if kind == "block":
                return (step,) + (0,) * (ndim - 1)
            if kind == "run":
                return (0, run) + (0,) * (ndim - 2)
            return (0,) * ndim

        return place

    def spec(kind, block):
        if kind == "smem":
            return pl.BlockSpec(memory_space=pltpu.SMEM)
        return pl.BlockSpec(block, index(kind, len(block)))

    arrays = [array for array, _, _ in ins]
    moved = sum(a.size * a.dtype.itemsize for a in arrays)
    return pl.pallas_call(
        kernel,
        grid_spec=pltpu.PrefetchScalarGridSpec(
            num_scalar_prefetch=1,
            grid=(steps,),
            in_specs=[spec(kind, block or array.shape) for array, kind, block in ins],
            out_specs=[spec(kind, block or shape) for shape, _, kind, block in outs],
            scratch_shapes=scratch,
        ),
        out_shape=[jax.ShapeDtypeStruct(shape, dtype) for shape, dtype, _, _ in outs],
        compiler_params=pltpu.CompilerParams(
            dimension_semantics=("arbitrary",), vmem_limit_bytes=48 << 20
        ),
        cost_estimate=pl.CostEstimate(flops=flops, bytes_accessed=moved // 20, transcendentals=0),
        name=name,
    )(where, *arrays)


def scan_call(decays, states, reverse):
    return pl.pallas_call(
        functools.partial(scan_kernel, reverse, states.shape[0], states.shape[1]),
        out_shape=jax.ShapeDtypeStruct(states.shape[:2] + (128, 128), BF16),
        name="scan_back" if reverse else "scan",
    )(decays, states)


def project_kernel(tiles, left, right, weights, *rest):
    out = rest[-1]
    step = pl.program_id(0)

    @pl.when(step < tiles)
    def _():
        out[0] = mm(left[...], weights[...])

    @pl.when(step >= tiles)
    def _():
        out[0] = mm(right[...], weights[...])


def project_call(made, first, count, left, right, weights):
    rows, width = left.shape
    columns = weights.shape[1]
    tile = min(256, rows)
    tiles = rows // tile
    shape = (count, rows, columns)
    in_specs = [
        pl.BlockSpec((tile, width), lambda i: (jnp.minimum(i, tiles - 1), 0)),
        pl.BlockSpec((tile, width), lambda i: (jnp.maximum(i - tiles, 0), 0)),
        pl.BlockSpec(weights.shape, lambda i: (0, 0), pipeline_mode=pl.Buffered(1)),
    ]
    arrays = [left, right, weights]
    if made is not None:
        in_specs.append(pl.BlockSpec(memory_space=pl.ANY))
        arrays.append(made)
    return pl.pallas_call(
        functools.partial(project_kernel, tiles),
        grid=(2 * tiles,),
        in_specs=in_specs,
        out_specs=pl.BlockSpec(
            (1, tile, columns), lambda i: (first + lax.div(i, tiles), lax.rem(i, tiles), 0)
        ),
        out_shape=jax.ShapeDtypeStruct(shape, F32),
        input_output_aliases={} if made is None else {3: 0},
        compiler_params=pltpu.CompilerParams(
            dimension_semantics=("arbitrary",), vmem_limit_bytes=40 << 20
        ),
        cost_estimate=pl.CostEstimate(
            flops=rows * width * columns * 240 // 100, bytes_accessed=rows * width, transcendentals=0
        ),
        name="project",
    )(*arrays)


def back_kernel(tiles, left, right, grads, weights, out_left, out_right, part):
    step = pl.program_id(0)
    made = mm(grads[0], weights[...], NT)

    @pl.when(step == 0)
    def _():
        part[...] = jnp.zeros_like(part)

    @pl.when(step < tiles)
    def _():
        out_left[...] = made.astype(BF16)
        part[...] += jnp.sum(made * left[...].astype(F32), axis=0, keepdims=True)

    @pl.when(step >= tiles)
    def _():
        out_right[...] = made.astype(BF16)
        part[...] += jnp.sum(made * right[...].astype(F32), axis=0, keepdims=True)


def back_call(grads, first, left, right, weights):
    rows, width = left.shape
    columns = weights.shape[1]
    tile = min(256, rows)
    tiles = rows // tile

    def one(i):
        return (jnp.minimum(i, tiles - 1), 0)

    def two(i):
        return (jnp.maximum(i - tiles, 0), 0)

    return pl.pallas_call(
        functools.partial(back_kernel, tiles),
        grid=(2 * tiles,),
        in_specs=[
            pl.BlockSpec((tile, width), one),
            pl.BlockSpec((tile, width), two),
            pl.BlockSpec(
                (1, tile, columns), lambda i: (first + lax.div(i, tiles), lax.rem(i, tiles), 0)
            ),
            pl.BlockSpec(weights.shape, lambda i: (0, 0), pipeline_mode=pl.Buffered(1)),
        ],
        out_specs=[
            pl.BlockSpec((tile, width), one),
            pl.BlockSpec((tile, width), two),
            pl.BlockSpec((1, width), lambda i: (0, 0)),
        ],
        out_shape=[jax.ShapeDtypeStruct((rows, width), BF16)] * 2
        + [jax.ShapeDtypeStruct((1, width), F32)],
        compiler_params=pltpu.CompilerParams(
            dimension_semantics=("arbitrary",), vmem_limit_bytes=40 << 20
        ),
        cost_estimate=pl.CostEstimate(
            flops=rows * width * columns * 240 // 100, bytes_accessed=rows * width, transcendentals=0
        ),
        name="project_back",
    )(left, right, grads, weights)


def feed_kernel(*refs):
    two_refs, cot_refs, (w_low, w_high, w_dn), outs = refs[0:2], refs[2:4], refs[4:7], refs[7:]
    units = w_dn.shape[0]
    half = w_low.shape[0]
    for k in range(2):
        act_out, grad_out, down_out, back_out = outs[4 * k : 4 * k + 4]
        pre = mm(two_refs[k][:, :half], w_low[...]) + mm(two_refs[k][:, half:], w_high[...])
        gate, up = pre[:, :units], pre[:, units:]
        sigma = jax.nn.sigmoid(gate)
        silu = gate * sigma
        act = (silu * up).astype(BF16)
        act_out[...] = act
        down_out[...] = mm(act, w_dn[...]).astype(BF16)
        grad_act = mm(cot_refs[k][...], w_dn[...], NT)
        grad_out[:, :units] = (grad_act * up * (sigma * (1.0 + gate * (1.0 - sigma)))).astype(BF16)
        grad_out[:, units:] = (grad_act * silu).astype(BF16)
        back_out[:, :half] = mm(grad_out[...], w_low[...], NT).astype(BF16)
        back_out[:, half:] = mm(grad_out[...], w_high[...], NT).astype(BF16)


def feed_call(two, cot, w_low, w_high, w_dn):
    rows, width = two[0].shape
    units = w_dn.shape[0]
    tile = min(256, rows)

    def cut(columns):
        return pl.BlockSpec((tile, columns), lambda i: (i, 0))

    def still(array):
        return pl.BlockSpec(array.shape, lambda i: (0, 0), pipeline_mode=pl.Buffered(1))

    sizes = (units, 2 * units, width, width)
    flops = 2 * 2 * rows * width * 6 * units
    return pl.pallas_call(
        feed_kernel,
        grid=(rows // tile,),
        in_specs=[cut(width)] * 4 + [still(w_low), still(w_high), still(w_dn)],
        out_specs=[cut(s) for s in sizes] * 2,
        out_shape=[jax.ShapeDtypeStruct((rows, s), BF16) for s in sizes] * 2,
        compiler_params=pltpu.CompilerParams(
            dimension_semantics=("arbitrary",), vmem_limit_bytes=58 << 20
        ),
        cost_estimate=pl.CostEstimate(
            flops=flops * 60 // 100, bytes_accessed=rows * width, transcendentals=0
        ),
        name="feed",
    )(*two, *cot, w_low, w_high, w_dn)


def spread_kernel(grads, weights, out):
    units = weights[0, :, 0].reshape(-1, weights.shape[-1])
    out[0] = mm(grads[...], units, NT).astype(BF16)


def spread_call(grads, weights):
    cores, shards, chips, size, width = weights.shape
    rows = grads.shape[0]
    return pl.pallas_call(
        spread_kernel,
        grid=(cores * chips,),
        in_specs=[
            pl.BlockSpec(grads.shape, lambda s: (0, 0)),
            pl.BlockSpec(
                (1, shards, 1, size, width),
                lambda s: (lax.rem(s, cores), 0, lax.div(s, cores), 0, 0),
            ),
        ],
        out_specs=pl.BlockSpec((1, rows, shards * size), lambda s: (s, 0, 0)),
        out_shape=jax.ShapeDtypeStruct((cores * chips, rows, shards * size), BF16),
        compiler_params=pltpu.CompilerParams(
            dimension_semantics=("arbitrary",), vmem_limit_bytes=32 << 20
        ),
        cost_estimate=pl.CostEstimate(
            flops=rows * width * size * 1920 // 100, bytes_accessed=rows * width, transcendentals=0
        ),
        name="spread",
    )(grads, weights)


def heads_grad_kernel(pieces, heads, grads, out):
    made = mm(heads[0], grads[...], TN).astype(BF16)
    tall = made.shape[0] // out.shape[2]
    low = tall // pieces
    for j in range(out.shape[2]):
        for s in range(pieces):
            out[s, 0, j, 0] = made[j * tall + s * low : j * tall + (s + 1) * low]


def heads_grad_call(heads, grads, cores, shards):
    count, rows, chans = heads.shape
    width = grads.shape[1]
    size = chans // shards
    chips = count // cores
    shape = (count, cores, shards, chips, size // count, width)
    return pl.pallas_call(
        functools.partial(heads_grad_kernel, count),
        grid=(count,),
        in_specs=[
            pl.BlockSpec((1, rows, chans), lambda s: (s, 0, 0)),
            pl.BlockSpec(grads.shape, lambda s: (0, 0)),
        ],
        out_specs=pl.BlockSpec(
            (count, 1, shards, 1, size // count, width),
            lambda s: (0, lax.rem(s, cores), 0, lax.div(s, cores), 0, 0),
        ),
        out_shape=jax.ShapeDtypeStruct(shape, BF16),
        compiler_params=pltpu.CompilerParams(
            dimension_semantics=("arbitrary",), vmem_limit_bytes=32 << 20
        ),
        cost_estimate=pl.CostEstimate(
            flops=rows * width * size * 1920 // 100, bytes_accessed=rows * width, transcendentals=0
        ),
        name="mix_out_grad",
    )(heads, grads)


def outer_kernel(count, place, *refs):
    *inputs, out, total, left, right, sems = refs
    lefts, rights = inputs[:count], inputs[count:]
    if len(rights) < count:
        rights = [rights[0].at[k] for k in range(count)]
    step = pl.program_id(0)

    def fetch(block, slot):
        return (
            pltpu.make_async_copy(lefts[block], left.at[slot], sems.at[0, slot]),
            pltpu.make_async_copy(rights[block], right.at[slot], sems.at[1, slot]),
        )

    @pl.when(step == 0)
    def _():
        for copy in fetch(0, 0):
            copy.start()

    slot = lax.rem(step, 2)
    for block in range(1, count):

        @pl.when(step + 1 == block)
        def _(block=block):
            for copy in fetch(block, block % 2):
                copy.start()

    for copy in fetch(0, slot):
        copy.wait()

    @pl.when(step == 0)
    def _():
        total[...] = mm(left[0], right[0], TN)

    @pl.when(step > 0)
    def _():
        total[...] += mm(left[slot], right[slot], TN)

    @pl.when(step == count - 1)
    def _():
        place(out, total)


def outer_call(lefts, rights, shape, place, name):
    count = len(lefts)
    rows, m = lefts[0].shape
    n = rights[0].shape[-1]
    return pl.pallas_call(
        functools.partial(outer_kernel, count, place),
        grid=(count,),
        in_specs=[pl.BlockSpec(memory_space=pl.ANY)] * (count + len(rights)),
        out_specs=pl.BlockSpec(shape, lambda i: (0,) * len(shape), pipeline_mode=pl.Buffered(1)),
        out_shape=jax.ShapeDtypeStruct(shape, BF16),
        scratch_shapes=[
            pltpu.VMEM((m, n), F32),
            pltpu.VMEM((2, rows, m), BF16),
            pltpu.VMEM((2, rows, n), BF16),
            pltpu.SemaphoreType.DMA((2, 2)),
        ],
        compiler_params=pltpu.CompilerParams(
            dimension_semantics=("arbitrary",), vmem_limit_bytes=58 << 20
        ),
        cost_estimate=pl.CostEstimate(
            flops=count * rows * m * n * 120 // 100,
            bytes_accessed=rows * (m + n),
            transcendentals=0,
        ),
        name=name,
    )(*lefts, *rights)


def swap(value, across):
    return lax.ppermute(value, "seq", [(i, i ^ across) for i in range(lax.axis_size("seq"))])


CORE, XLINK, YLINK = 1, 2, 4
TILE = 128


def together(*values):
    return lax.optimization_barrier(values)


def plane_gather(own, beside=None, meet=None):
    half = own.shape[0] // 2
    got = {0: own, XLINK: swap(own, XLINK), YLINK: swap(own, YLINK), CORE: swap(own, CORE)}
    got, beside = together(got, beside)
    first = swap(got[YLINK][:half], XLINK)
    second = swap(got[XLINK][half:], YLINK)
    got[XLINK + CORE] = swap(got[XLINK], CORE)
    got[YLINK + CORE] = swap(got[YLINK], CORE)
    first, second, got, meet = together(first, second, got, meet)
    got[XLINK + YLINK] = jnp.concatenate([first, second])
    got[XLINK + YLINK + CORE] = jnp.concatenate([swap(first, CORE), swap(second, CORE)])
    return got, beside, meet


def add_low(a, b):
    return (a.astype(F32) + b.astype(F32)).astype(BF16)


def chip_sum(parts, a):
    return add_low(parts[a], swap(parts[a ^ CORE], CORE))


def first_hops(chip):
    half = chip[0].shape[0] // 2
    return (
        swap(chip[2][:half], XLINK),
        swap(chip[4][half:], YLINK),
        swap(chip[6][:half], XLINK),
        swap(chip[6][half:], YLINK),
    )


def turned(chip, hops):
    half = chip[4].shape[0] // 2
    return add_low(chip[4][:half], hops[2]), add_low(chip[2][half:], hops[3])


def last_hops(pair):
    return swap(pair[0], YLINK), swap(pair[1], XLINK)


def arrived(chip, hops, lasts):
    half = chip[0].shape[0] // 2
    low = chip[0][:half].astype(F32) + hops[0].astype(F32) + lasts[0].astype(F32)
    high = chip[0][half:].astype(F32) + hops[1].astype(F32) + lasts[1].astype(F32)
    return jnp.concatenate([low, high])


def pick(array, index, axis):
    return lax.dynamic_index_in_dim(array, index, axis, keepdims=False)


def plane_device(
    tokens,
    norm1_gain,
    w_mix_in,
    forget_gap,
    group_gain,
    w_mix_out,
    norm2_gain,
    w_gate_up,
    w_down,
    doc_lengths,
    out_cotangent,
):
    seq_count, mp_count = lax.axis_size("seq"), lax.axis_size("mp")
    seq_index, mp_index = lax.axis_index("seq"), lax.axis_index("mp")
    core, chip = seq_index % 2, seq_index // 2
    chips = seq_count // 2
    span, packs, width = tokens.shape
    rows = span * packs
    run = span * mp_count
    all_heads, head_size, _ = w_mix_out.shape
    heads = all_heads // seq_count
    chans = heads * head_size
    slice_d = width // seq_count

    def pack_major(array):
        return jnp.transpose(array, (1, 0, 2)).reshape(rows, width)

    def token_major(array):
        return jnp.transpose(array.reshape(packs, span, width), (1, 0, 2))

    def gather_shares(part):
        return lax.all_gather(part, "mp", axis=0).reshape((2, 2) + part.shape)

    def both_halves(pairs):
        mine = pick(pairs, core, 0)
        other = swap(pick(pairs, 1 - core, 0), CORE)
        return jnp.where(core == 0, mine, other), jnp.where(core == 0, other, mine)

    in_part = lax.dynamic_slice(
        w_mix_in, (0, 2 * core, chip * head_size), (width, 2, head_size)
    ).reshape(width, 2 * head_size)
    in_pairs = gather_shares(in_part)

    own = pack_major(tokens)
    scale_one = rms_scale(own)
    normed_own = (own * scale_one * norm1_gain).astype(BF16)

    small = pick(jnp.stack([forget_gap, group_gain]), chip, 1)[None]
    for bit in range(2):
        across = 1 << bit
        other = lax.ppermute(small, "mp", [(i, i ^ across) for i in range(mp_count)])
        low = (mp_index >> bit) % 2 == 0
        small = jnp.concatenate([jnp.where(low, small, other), jnp.where(low, other, small)])

    hidden_units = w_gate_up.shape[2]
    share = -(-hidden_units // (chips * TILE)) * TILE
    local_ff = 2 * share
    spare = share * chips - hidden_units
    begin = jnp.minimum(chip * share, hidden_units - share)
    gu_part = lax.dynamic_slice_in_dim(pick(w_gate_up, core, 1), begin, share, 1)
    dn_part = lax.dynamic_slice_in_dim(w_down, begin, share, 0)
    fresh = lax.broadcasted_iota(jnp.int32, (share, 1), 0) >= chip * share - begin
    dn_part = jnp.where(fresh, dn_part, jnp.zeros_like(dn_part))
    dn_part = lax.dynamic_slice_in_dim(dn_part, core * (share // 2), share // 2, 0)
    out_flat = w_mix_out.reshape(-1, width)
    normed, (gu_part, dn_part, small), in_pairs = plane_gather(
        normed_own, (gu_part, dn_part, small), in_pairs
    )
    gu_first, gu_second = gu_part[: width // 2], gu_part[width // 2 :]
    query_forget, value_gate = both_halves(in_pairs)
    w_in = jnp.concatenate(
        [
            part[j, :, k * head_size : (k + 1) * head_size]
            for part, k in ((query_forget, 1), (value_gate, 0), (query_forget, 0), (value_gate, 1))
            for j in range(2)
        ],
        axis=1,
    )

    cot_own = pack_major(lax.dynamic_slice_in_dim(out_cotangent, mp_index * span, span, 0))
    cot_low, gu_first, dn_part, _ = together(cot_own.astype(BF16), gu_first, dn_part, in_pairs)

    dn_pairs = gather_shares(dn_part)
    first_pairs = gather_shares(gu_first)

    small = pick(small.reshape(2, 2, 2, head_size), core, 0)
    gap_row, gain_row = small[:, 0].reshape(1, chans), small[:, 1].reshape(1, chans)

    projected = None
    for a in range(0, seq_count, 2):
        projected = project_call(projected, a, seq_count, normed[a], normed[a + 1], w_in)
    projected = projected.reshape(seq_count, packs, span, 4 * chans)

    halves = span // BLOCK
    steps = seq_count * halves
    where = jnp.stack([seq_index, run, mp_index * span, halves]).astype(jnp.int32)
    block = (1, packs, BLOCK, chans)
    fv_block = (1, packs, BLOCK, 2 * chans)
    wide = (1, packs, BLOCK, 4 * chans)
    pairs = packs * heads
    runs_shape = (packs, seq_count, heads, head_size, head_size)
    run_block = (packs, 1, heads, head_size, head_size)
    tall_shape = (packs, seq_count, heads, head_size + 8, head_size)
    tall_block = (packs, 1, heads, head_size + 8, head_size)
    unit = 2 * BLOCK * head_size * head_size * pairs * steps
    common = [(doc_lengths, "smem", None), (gap_row, "whole", None)]
    call = functools.partial(recur_call, steps=steps, halves=halves, where=where)

    def to_scan(array):
        array = jnp.transpose(array, (0, 2, 1, 3, 4)).astype(BF16)
        array = array.reshape((pairs,) + array.shape[2:])
        return lax.all_to_all(array, "mp", split_axis=0, concat_axis=0, tiled=True)

    def from_scan(array):
        array = lax.all_to_all(array, "mp", split_axis=0, concat_axis=0, tiled=True)
        array = array.reshape((packs, heads) + array.shape[1:])
        return jnp.transpose(array, (0, 2, 1, 3, 4))

    [run_state] = call(
        states_kernel,
        reverse=False,
        ins=common + [(projected, "near", fv_block)],
        outs=[(tall_shape, F32, "run", tall_block)],
        scratch=[],
        flops=27 * unit,
        name="run_states",
    )
    cot, run_state, _ = plane_gather(cot_low, run_state)
    decays = to_scan(run_state)
    entering = from_scan(scan_call(decays, decays, False))
    row_shape = (seq_count, packs, span, chans)
    state_shape = (packs, heads, head_size, head_size)
    heads_out, mixed, kept = call(
        forward_kernel,
        reverse=False,
        ins=common
        + [(gain_row, "whole", None), (projected, "near", wide), (entering, "run", run_block)],
        outs=[
            (row_shape, BF16, "rows", block),
            (row_shape, F32, "rows", block),
            ((steps,) + state_shape, F32, "block", (1,) + state_shape),
        ],
        scratch=[pltpu.VMEM(state_shape, F32)],
        flops=45 * unit,
        name="mix_forward",
    )
    gu_second, dn_pairs, first_pairs, cot, _ = together(
        gu_second, dn_pairs, first_pairs, cot, entering
    )
    second_pairs = gather_shares(gu_second)

    def side_by_side(pairs):
        gate, up = both_halves(pairs)
        return jnp.concatenate([gate[0], gate[1], up[0], up[1]], axis=1)

    w_dn = jnp.concatenate(both_halves(dn_pairs), axis=1).reshape(local_ff, width)
    w_low, w_high = side_by_side(first_pairs), side_by_side(second_pairs)

    split = (chips, 2, rows, 2, head_size)
    heads_by = lax.all_to_all(
        heads_out.reshape(seq_count, rows, chans), "seq", split_axis=0, concat_axis=0, tiled=True
    )
    heads_tok = jnp.transpose(heads_by.reshape(split), (2, 1, 3, 0, 4)).reshape(rows, -1)
    hidden = own + mm(heads_tok, out_flat)
    scale_two = rms_scale(hidden)
    normed_two = (hidden * scale_two * norm2_gain).astype(BF16)

    def ready(parts):
        mine = pick(parts, core, 0)
        other = swap(pick(parts, 1 - core, 0), CORE)
        low = jnp.where(core == 0, mine, other)
        high = jnp.where(core == 0, other, mine)
        return jnp.concatenate([low, high])

    def deliver(terms):
        return lax.psum_scatter(terms, "mp", scatter_dimension=0, tiled=True)[0]

    def handed(piece):
        groups = [list(range(k, seq_count, 2)) for k in range(2)]
        return lax.all_to_all(
            piece, "seq", split_axis=0, concat_axis=0, axis_index_groups=groups, tiled=True
        )

    act, grad_gu, down_parts, back_parts = {}, {}, {}, {}
    order = range(seq_count)

    def feed(a):
        made = feed_call((two[a], two[a + 1]), (cot[a], cot[a + 1]), w_low, w_high, w_dn)
        for k, at in enumerate((a, a + 1)):
            act[at], grad_gu[at], down_parts[at], back_parts[at] = made[4 * k : 4 * k + 4]

    two = {0: normed_two}
    for across in (CORE, XLINK, YLINK):
        two[across] = swap(normed_two, across)
    feed(0)
    two[XLINK], two[YLINK], down_parts[0] = together(two[XLINK], two[YLINK], down_parts[0])
    middle = rows // 2
    far_first = swap(two[YLINK][:middle], XLINK)
    far_second = swap(two[XLINK][middle:], YLINK)
    two[3], two[5] = swap(two[XLINK], CORE), swap(two[YLINK], CORE)
    feed(2)
    two[YLINK], down_parts[2] = together(two[YLINK], down_parts[2])
    feed(4)
    chip_back = {2: chip_sum(back_parts, 2)}
    far_first, far_second, chip_back, down_parts[4] = together(
        far_first, far_second, chip_back, down_parts[4]
    )
    two[6] = jnp.concatenate([far_first, far_second])
    two[7] = jnp.concatenate([swap(far_first, CORE), swap(far_second, CORE)])
    other = swap(back_parts[5], CORE)
    feed(6)
    other, back_parts = together(other, back_parts)
    chip_back[4] = add_low(back_parts[4], other)
    chip_back[6] = chip_sum(back_parts, 6)

    def place_gu(out, total):
        for d in range(seq_count):
            for j in range(2):
                for g in range(2):
                    at = (2 * g + j) * share
                    out[d % 2, j, d // 2, g] = total[
                        d * slice_d : (d + 1) * slice_d, at : at + share
                    ].astype(BF16)

    def place_dn(out, total):
        for d in range(seq_count):
            for j in range(2):
                out[d % 2, j, d // 2] = total[
                    j * share : (j + 1) * share, d * slice_d : (d + 1) * slice_d
                ].astype(BF16)

    chip_back, grad_gu = together(chip_back, grad_gu)
    gu_grad = outer_call(
        [two[a] for a in order],
        [grad_gu[a] for a in order],
        (2, 2, chips, 2, slice_d, share),
        place_gu,
        "gate_up_grad",
    )
    chip_back[0] = chip_sum(back_parts, 0)
    hops, chip_back, gu_grad = together(first_hops(chip_back), chip_back, gu_grad)
    onward, act = together(turned(chip_back, hops), act)
    dn_grad = outer_call(
        [act[a] for a in order],
        [cot[a] for a in order],
        (2, 2, chips, share, slice_d),
        place_dn,
        "down_grad",
    )
    lasts, dn_grad = together(last_hops(onward), dn_grad)
    grad_normed_two = arrived(chip_back, hops, lasts)
    grad_normed_two, down_parts = together(grad_normed_two, down_parts)

    norm2_part = jnp.sum(grad_normed_two * hidden * scale_two, axis=0)
    grad_hidden = cot_own + rms_back(grad_normed_two, hidden, scale_two, norm2_gain)
    grad_mix = grad_hidden.astype(BF16)
    grad_tok = spread_call(grad_mix, w_mix_out.reshape(2, 2, chips, head_size, width))
    grad_tok, dn_grad = together(grad_tok, ready(dn_grad))
    dn_grad = deliver(dn_grad)
    grad_heads = lax.all_to_all(grad_tok, "seq", split_axis=0, concat_axis=0, tiled=True)
    chip_down = {a: chip_sum(down_parts, a) for a in (2, 4, 6, 0)}
    out_grad = heads_grad_call(heads_by, grad_mix, 2, 2)
    grad_heads, chip_down, out_grad = together(
        grad_heads.reshape(row_shape), chip_down, out_grad
    )

    grad_out, grad_gate, group_part, run_grad = call(
        gate_back_kernel,
        reverse=True,
        ins=common
        + [
            (gain_row, "whole", None),
            (projected, "near", wide),
            (mixed, "rows", block),
            (grad_heads, "rows", block),
        ],
        outs=[
            (row_shape, F32, "rows", block),
            (row_shape, BF16, "rows", block),
            ((1, chans), F32, "whole", None),
            (runs_shape, BF16, "run", run_block),
        ],
        scratch=[pltpu.VMEM(state_shape, F32)],
        flops=35 * unit,
        name="gate_back",
    )
    out_grad = out_grad.reshape(seq_count, all_heads, head_size // seq_count, width)
    out_parts = {a: pick(out_grad, seq_index ^ a, 0) for a in range(seq_count)}
    chip_out = {a: chip_sum(out_parts, a) for a in (2, 4, 6, 0)}
    run_grad, chip_out = together(to_scan(run_grad), chip_out)
    entering_back = from_scan(scan_call(decays, run_grad, True))
    hops_down = first_hops(chip_down)
    entering_back, gu_grad = together(entering_back, ready(gu_grad))
    gu_grad = deliver(gu_grad)
    grad_projected, gap_part = call(
        backward_kernel,
        reverse=True,
        ins=common
        + [
            (projected, "near", wide),
            (grad_out, "rows", block),
            (grad_gate, "rows", block),
            (kept, "block", (1,) + state_shape),
            (entering_back, "run", run_block),
        ],
        outs=[
            ((seq_count, packs, span, 4 * chans), BF16, "near", wide),
            ((1, chans), F32, "whole", None),
        ],
        scratch=[pltpu.VMEM(state_shape, F32)],
        flops=69 * unit,
        name="mix_backward",
    )
    grad_projected = grad_projected.reshape(seq_count, rows, 4 * chans)
    grad_projected, dn_grad, hops_down = together(grad_projected, dn_grad, hops_down)
    dn_round = handed(dn_grad)
    lasts_down = last_hops(turned(chip_down, hops_down))
    chip_out = together(chip_out, grad_projected)[0]
    hops_out = first_hops(chip_out)
    def place_in(out, total):
        for d in range(seq_count):
            for j in range(2):
                for k, of in enumerate((2, 0, 1, 3)):
                    at = of * chans + j * head_size
                    out[d % 2, j, d // 2, :, k * head_size : (k + 1) * head_size] = total[
                        d * slice_d : (d + 1) * slice_d, at : at + head_size
                    ].astype(BF16)

    in_grad = outer_call(
        [normed[a] for a in order],
        [grad_projected],
        (2, 2, chips, slice_d, 4 * head_size),
        place_in,
        "mix_in_grad",
    )
    grad_projected, in_grad, lasts_down, dn_round = together(
        grad_projected, in_grad, lasts_down, dn_round
    )
    layer_out = token_major(hidden + arrived(chip_down, hops_down, lasts_down))
    in_parts, chip_in = {}, {}

    def back(a):
        in_parts[a], in_parts[a + 1], part = back_call(
            grad_projected, a, normed[a], normed[a + 1], w_in
        )
        return part

    def from_core(a):
        return swap(in_parts[a + 1], CORE)

    half = rows // 2
    in_mine = pick(in_grad, core, 0)
    in_other = swap(pick(in_grad, 1 - core, 0), CORE)
    norm1_part = back(6)
    grad_projected, in_mine, in_other, hops_out, in_parts = together(
        grad_projected, in_mine, in_other, hops_out, in_parts
    )
    lasts_out = last_hops(turned(chip_out, hops_out))
    in_grad = jnp.concatenate(
        [jnp.where(core == 0, in_mine, in_other), jnp.where(core == 0, in_other, in_mine)]
    )
    other = from_core(6)
    norm1_part = norm1_part + back(2)
    grad_projected, lasts_out, other, in_parts, in_grad, gu_grad = together(
        grad_projected, lasts_out, other, in_parts, in_grad, gu_grad
    )
    in_grad = deliver(in_grad)
    chip_in[6] = add_low(in_parts[6], other)
    far_hops = swap(chip_in[6][:half], XLINK), swap(chip_in[6][half:], YLINK)
    out_grad = arrived(chip_out, hops_out, lasts_out).astype(BF16)
    out_grad = out_grad.reshape((mp_count, all_heads // mp_count) + out_grad.shape[1:])
    other = from_core(2)
    norm1_part = norm1_part + back(4)
    grad_projected, other, in_parts = together(grad_projected, other, in_parts)
    chip_in[2] = add_low(in_parts[2], other)
    mine_x = swap(chip_in[2][:half], XLINK)
    other = from_core(4)
    norm1_part = norm1_part + back(0)
    def set_heads(part):
        row = jnp.zeros((2, 2, chips, head_size), F32)
        mine = part.reshape(1, 2, 1, head_size)
        row = lax.dynamic_update_slice(row, mine, (core, 0, chip, 0))
        row = row.reshape(mp_count, all_heads // mp_count, seq_count, head_size // seq_count)
        return jnp.transpose(row, (2, 0, 1, 3)).reshape(-1)

    gains = jnp.stack(
        [norm1_part[0] / norm1_gain, norm2_part, set_heads(gap_part), set_heads(group_part)]
    )
    gains = jnp.transpose(gains.reshape(4, seq_count, width // seq_count), (1, 0, 2))
    far_hops, other, in_parts, chip_in, gu_round, gains, out_grad = together(
        far_hops, other, in_parts, chip_in, handed(gu_grad), gains, out_grad
    )
    out_grad = lax.psum_scatter(out_grad, "mp", scatter_dimension=0, tiled=True)[0]
    chip_in[4] = add_low(in_parts[4], other)
    hops = mine_x, swap(chip_in[4][half:], YLINK)
    lasts = last_hops(turned(chip_in, (None, None) + far_hops))
    chip_in[0] = chip_sum(in_parts, 0)
    gains = jnp.sum(lax.all_to_all(gains, "seq", split_axis=0, concat_axis=0, tiled=True), axis=0)
    gains = jnp.transpose(gains.reshape(4, mp_count, -1), (1, 0, 2))
    hops, lasts, chip_in, layer_out, gains = together(hops, lasts, chip_in, layer_out, gains)
    gains = jnp.sum(lax.all_to_all(gains, "mp", split_axis=0, concat_axis=0, tiled=True), axis=0)
    grad_normed = arrived(chip_in, hops, lasts)
    got = [gu_round[c].astype(F32) for c in range(chips)]
    got[-1] = got[-1][:, :, spare:]
    gate_up_grad = jnp.transpose(jnp.concatenate(got, axis=-1), (1, 0, 2))
    got = [dn_round[c] for c in range(chips)]
    got[-1] = got[-1][spare:]
    down_grad = jnp.concatenate(got, axis=0).astype(F32)
    mix_out_grad = out_grad.astype(F32)
    in_round = handed(in_grad)
    got = [in_round[c].astype(F32).reshape(slice_d, 4, head_size) for c in range(chips)]
    mix_in_grad = jnp.concatenate(got, axis=-1)

    tokens_grad = token_major(
        grad_hidden + rms_back(grad_normed, own, scale_one, norm1_gain)
    )

    small = gains[2:].reshape(2, all_heads // mp_count, head_size // seq_count)
    return (
        layer_out,
        tokens_grad,
        gains[0],
        mix_in_grad,
        small[0],
        small[1],
        mix_out_grad,
        gains[1],
        gate_up_grad,
        down_grad,
    )


def solution(mesh):
    body = plane_device if dict(mesh.shape) == {"seq": 8, "mp": 4} else generic_device
    placed = (
        P(("seq", "mp"), None, None),
        P(),
        P(None, None, "mp"),
        P("mp", None),
        P("mp", None),
        P(),
        P(),
        P(None, None, "mp"),
        P("mp", None),
        P(),
        P("seq", None, None),
    )
    return jax.shard_map(
        body,
        mesh=mesh,
        in_specs=placed,
        out_specs=(
            P(("seq", "mp"), None, None),
            P(("seq", "mp"), None, None),
            P(("seq", "mp")),
            P("seq", None, "mp"),
            P("mp", "seq"),
            P("mp", "seq"),
            P("mp", "seq", None),
            P(("seq", "mp")),
            P("seq", None, "mp"),
            P("mp", "seq"),
        ),
        check_vma=False,
    )
```

```python
import functools

import jax
import jax.numpy as jnp
from jax import lax
from jax.experimental import pallas as pl
from jax.experimental.pallas import tpu as pltpu
from jax.sharding import PartitionSpec as P

BLOCK = 128


EPSILON = 1e-06
PRECISE = lax.Precision.HIGHEST


def entering(x, axis, combine, identity, reverse):
    length, index = (lax.axis_size(axis), lax.axis_index(axis))
    everything = jax.tree.map(
        lambda part, kind: lax.all_gather(part.astype(kind), axis), x, (jnp.bfloat16, jnp.bfloat16)
    )
    start = jax.tree.map(
        lambda part, zero: jnp.broadcast_to(jnp.asarray(zero, part.dtype), part.shape), x, identity
    )

    def turn(k, before):
        at = length - 1 - k if reverse else k
        reached = at > index if reverse else at < index
        new = combine(
            before, jax.tree.map(lambda part, own: part[at].astype(own.dtype), everything, x)
        )
        return jax.tree.map(lambda a, b: jnp.where(reached, a, b), new, before)

    return lax.fori_loop(0, length, turn, start)


def rounded(signal):
    return lax.optimization_barrier(signal.astype(jnp.bfloat16)).astype(jnp.float32)


def rms_scale(signal):
    return lax.rsqrt(jnp.mean(signal * signal, axis=-1, keepdims=True) + EPSILON)


def rms_back(gradient, signal, scaling, gain_vec):
    weighted = gradient * gain_vec
    inner_sum = jnp.mean(weighted * signal, axis=-1, keepdims=True)
    return scaling * weighted - signal * (scaling * scaling * scaling) * inner_sum


def silu_slope(signal):
    sigma_val = jax.nn.sigmoid(signal)
    return sigma_val * (1.0 + signal * (1.0 - sigma_val))


def doc_index(doc_lengths, positions):
    doc_ends = jnp.stack(
        [jnp.sum(doc_lengths[:, : k + 1], axis=1) for k in range(doc_lengths.shape[1])], axis=1
    )
    return jnp.sum((positions[:, None, None] >= doc_ends[None, :, :]).astype(jnp.int32), axis=2)


def chain_combine(earlier, later_part):
    return (earlier[0] * later_part[0], later_part[0][..., None] * earlier[1] + later_part[1])


def block_tables(log_forget, doc_ids, previous):
    length = log_forget.shape[1]
    row_index = lax.broadcasted_iota(jnp.int32, (length, length), 0)
    col_index = lax.broadcasted_iota(jnp.int32, (length, length), 1)
    lower_ones = (row_index >= col_index).astype(jnp.float32)
    cumulated = jnp.einsum("ij,njshk->nishk", lower_ones, log_forget, precision=PRECISE)
    last_sum = cumulated[:, -1]
    same_doc = doc_ids[:, :, None, :] == doc_ids[:, None, :, :]
    visible = jnp.transpose(same_doc & (row_index >= col_index)[None, :, :, None], (0, 3, 1, 2))[
        :, :, None
    ]
    enters = (doc_ids == previous[:, None, :]).astype(jnp.float32)[..., None, None]
    at_end = (doc_ids == doc_ids[:, -1:, :]).astype(jnp.float32)[..., None, None]
    alive_end = (doc_ids[:, -1] == previous).astype(jnp.float32)[..., None, None]
    decays = jnp.exp(last_sum) * alive_end
    return (lower_ones, cumulated, last_sum, visible, enters, at_end, decays)


def block_factors(queries, key_vec, cumulated, last_sum, at_end):
    q_tilde = queries * jnp.exp(cumulated)
    k_tilde = key_vec * jnp.exp(-cumulated)
    k_hat = key_vec * jnp.exp(last_sum[:, None] - cumulated) * at_end
    return (q_tilde, k_tilde, k_hat)


def recur_forward(queries, key_vec, values_in, log_forget, doc_ids, previous):
    lower_ones, cumulated, last_sum, visible, enters, at_end, decays = block_tables(
        log_forget, doc_ids, previous
    )
    q_tilde, k_tilde, k_hat = block_factors(queries, key_vec, cumulated, last_sum, at_end)
    scores = jnp.einsum("nishk,njshk->nshij", q_tilde, k_tilde, precision=PRECISE)
    mixing = jnp.where(visible, scores, 0.0)
    inside = jnp.einsum("nshij,njshv->nishv", mixing, values_in, precision=PRECISE)
    local_sum = jnp.einsum("njshk,njshv->nshkv", k_hat, values_in, precision=PRECISE)

    def advance(carried, element):
        state_now, product = carried
        factor, addend = element
        return ((factor[..., None] * state_now + addend, product * factor), (state_now, product))

    zero_state = jnp.zeros(local_sum.shape[1:], jnp.float32)
    unit_decay = jnp.ones(decays.shape[1:], jnp.float32)
    (run_state, run_decay), (prefix_state, prefix_decay) = lax.scan(
        advance, (zero_state, unit_decay), (decays, local_sum)
    )
    incoming = entering(
        (run_decay, run_state), "seq", chain_combine, (unit_decay, zero_state), False
    )[1]
    start_state = prefix_state + prefix_decay[..., None] * incoming[None]
    carried_in = jnp.einsum("nishk,nshkv->nishv", q_tilde * enters, start_state, precision=PRECISE)
    return (inside + carried_in, start_state)


def recur_backward(
    queries, key_vec, values_in, log_forget, doc_ids, previous, start_state, grad_out
):
    lower_ones, cumulated, last_sum, visible, enters, at_end, decays = block_tables(
        log_forget, doc_ids, previous
    )
    q_tilde, k_tilde, k_hat = block_factors(queries, key_vec, cumulated, last_sum, at_end)
    scores = jnp.einsum("nishk,njshk->nshij", q_tilde, k_tilde, precision=PRECISE)
    mixing = jnp.where(visible, scores, 0.0)
    own_term = jnp.einsum("nishk,nishv->nshkv", q_tilde * enters, grad_out, precision=PRECISE)

    def retreat(carried, element):
        running, product = carried
        factor, addend = element
        return ((addend + factor[..., None] * running, product * factor), (running, product))

    zero_state = jnp.zeros(own_term.shape[1:], jnp.float32)
    unit_decay = jnp.ones(decays.shape[1:], jnp.float32)
    (run_grad, run_decay), (after_sum, after_decay) = lax.scan(
        retreat, (zero_state, unit_decay), (decays, own_term), reverse=True
    )
    outgoing = entering(
        (run_decay, run_grad), "seq", chain_combine, (unit_decay, zero_state), True
    )[1]
    next_grad = after_sum + after_decay[..., None] * outgoing[None]
    grad_mixing = jnp.where(
        visible, jnp.einsum("nishv,njshv->nshij", grad_out, values_in, precision=PRECISE), 0.0
    )
    grad_qt = jnp.einsum("nshij,njshk->nishk", grad_mixing, k_tilde, precision=PRECISE)
    grad_qt = grad_qt + jnp.einsum(
        "nishv,nshkv->nishk", grad_out * enters, start_state, precision=PRECISE
    )
    grad_kt = jnp.einsum("nshij,nishk->njshk", grad_mixing, q_tilde, precision=PRECISE)
    grad_values = jnp.einsum("nshij,nishv->njshv", mixing, grad_out, precision=PRECISE)
    grad_values = grad_values + jnp.einsum(
        "njshk,nshkv->njshv", k_hat, next_grad, precision=PRECISE
    )
    grad_khat = jnp.einsum("njshv,nshkv->njshk", values_in, next_grad, precision=PRECISE) * at_end
    grad_decay = jnp.sum(next_grad * start_state, axis=-1)
    grad_queries = grad_qt * jnp.exp(cumulated)
    grad_keys = grad_kt * jnp.exp(-cumulated) + grad_khat * jnp.exp(last_sum[:, None] - cumulated)
    grad_cum = grad_qt * q_tilde - grad_kt * k_tilde - grad_khat * k_hat
    grad_last = jnp.sum(grad_khat * k_hat, axis=1) + grad_decay * decays
    grad_log = (
        jnp.einsum("it,nishk->ntshk", lower_ones, grad_cum, precision=PRECISE) + grad_last[:, None]
    )
    return (grad_queries, grad_keys, grad_values, grad_log)


def generic_device(
    tokens,
    norm1_gain,
    w_mix_in,
    forget_gap,
    group_gain,
    w_mix_out,
    norm2_gain,
    w_gate_up,
    w_down,
    doc_lengths,
    out_cotangent,
):
    mp_count = lax.axis_size("mp")
    rows_dev, pack_count, model_width = tokens.shape
    run_length = rows_dev * mp_count
    blocks = run_length // BLOCK
    local_heads, head_size = forget_gap.shape
    local_chans = local_heads * head_size
    local_ff = w_gate_up.shape[2]
    mp_index = lax.axis_index("mp")
    run_start = lax.axis_index("seq") * run_length
    positions = run_start - 1 + jnp.arange(run_length + 1, dtype=jnp.int32)
    all_ids = doc_index(doc_lengths, positions)
    doc_ids = all_ids[1:].reshape(blocks, BLOCK, pack_count)
    previous = all_ids[0:run_length:BLOCK]
    shape_blocks = (blocks, BLOCK, pack_count, local_heads, head_size)
    shape_heads = (run_length, pack_count, local_heads, head_size)
    shape_flat = (run_length, pack_count, local_chans)
    scale_one = rms_scale(tokens)
    normed = (tokens * scale_one * norm1_gain).astype(jnp.bfloat16)
    in_flat = w_mix_in.reshape(model_width, 4 * local_chans)
    shard_rows = lax.all_gather(normed, "mp", axis=0, tiled=True)
    normed_all = shard_rows
    projected = jnp.einsum("tsd,dc->tsc", shard_rows, in_flat, preferred_element_type=jnp.float32)
    pre_query = projected[..., :local_chans]
    pre_forget = projected[..., local_chans : 2 * local_chans]
    pre_value = projected[..., 2 * local_chans : 3 * local_chans]
    pre_gate = projected[..., 3 * local_chans :]
    open_gate = jax.nn.sigmoid(-pre_forget)
    gap_gate = forget_gap.reshape(local_chans) * open_gate
    queries = rounded(pre_query).reshape(shape_blocks)
    key_vec = rounded(gap_gate).reshape(shape_blocks)
    values_in = rounded(pre_value).reshape(shape_blocks)
    log_forget = jnp.log1p(-gap_gate).reshape(shape_blocks)
    mixed, start_state = recur_forward(queries, key_vec, values_in, log_forget, doc_ids, previous)
    mixed = mixed.reshape(shape_flat)
    gate_act = jax.nn.silu(pre_gate)
    gated_four = (mixed * gate_act).reshape(shape_heads)
    scale_group = rms_scale(gated_four)
    heads_out = (gated_four * scale_group * group_gain).astype(jnp.bfloat16).reshape(shape_flat)
    heads_tok = lax.all_to_all(heads_out, "mp", split_axis=0, concat_axis=2, tiled=True)
    out_flat = w_mix_out.reshape(-1, model_width)
    hidden = tokens + jnp.einsum(
        "tsc,cd->tsd", heads_tok, out_flat, preferred_element_type=jnp.float32
    )
    scale_two = rms_scale(hidden)
    normed_two = (hidden * scale_two * norm2_gain).astype(jnp.bfloat16)
    ffn_flat = w_gate_up.reshape(model_width, 2 * local_ff)
    shard_rows = lax.all_gather(normed_two, "mp", axis=0, tiled=True)
    gate_up = jnp.einsum("tsd,dc->tsc", shard_rows, ffn_flat, preferred_element_type=jnp.float32)
    pre_gate_two = gate_up[..., :local_ff]
    pre_up = gate_up[..., local_ff:]
    silu_two = jax.nn.silu(pre_gate_two)
    activation = (silu_two * pre_up).astype(jnp.bfloat16)
    partial_value = activation
    ffn_sum = lax.psum_scatter(
        jnp.einsum("tsf,fd->tsd", partial_value, w_down, preferred_element_type=jnp.float32).astype(
            jnp.bfloat16
        ),
        "mp",
        scatter_dimension=0,
        tiled=True,
    ).astype(jnp.float32)
    layer_out = hidden + ffn_sum
    cot_low = out_cotangent.astype(jnp.bfloat16)
    cot_own = lax.dynamic_slice_in_dim(out_cotangent, mp_index * rows_dev, rows_dev, 0)
    down_part = jnp.einsum("tsf,tsd->fd", activation, cot_low, preferred_element_type=jnp.float32)
    grad_act = jnp.einsum("tsd,fd->tsf", cot_low, w_down, preferred_element_type=jnp.float32)
    grad_gate_two = grad_act * pre_up * silu_slope(pre_gate_two)
    grad_up = grad_act * silu_two
    grad_gate_up = jnp.concatenate([grad_gate_two, grad_up], axis=-1).astype(jnp.bfloat16)
    gate_up_part = jnp.einsum(
        "tsd,tsc->dc", shard_rows, grad_gate_up, preferred_element_type=jnp.float32
    )
    gate_up_part = gate_up_part.reshape(model_width, 2, local_ff)
    partial_value = grad_gate_up
    grad_normed_two = lax.psum_scatter(
        jnp.einsum(
            "tsc,dc->tsd", partial_value, ffn_flat, preferred_element_type=jnp.float32
        ).astype(jnp.bfloat16),
        "mp",
        scatter_dimension=0,
        tiled=True,
    ).astype(jnp.float32)
    norm2_part = jnp.sum(grad_normed_two * hidden * scale_two, axis=(0, 1))
    grad_hidden = cot_own + rms_back(grad_normed_two, hidden, scale_two, norm2_gain)
    grad_mix = grad_hidden.astype(jnp.bfloat16)
    out_part = jnp.einsum("tsc,tsd->cd", heads_tok, grad_mix, preferred_element_type=jnp.float32)
    grad_tok = jnp.einsum(
        "tsd,cd->tsc", grad_mix, out_flat, preferred_element_type=jnp.float32
    ).astype(jnp.bfloat16)
    grad_heads = lax.all_to_all(grad_tok, "mp", split_axis=2, concat_axis=0, tiled=True).astype(
        jnp.float32
    )
    grad_four = grad_heads.reshape(shape_heads)
    group_part = jnp.sum(grad_four * gated_four * scale_group, axis=(0, 1))
    grad_gated = rms_back(grad_four, gated_four, scale_group, group_gain).reshape(shape_flat)
    grad_mixed = grad_gated * gate_act
    grad_gate_in = grad_gated * mixed * silu_slope(pre_gate)
    grad_queries, grad_keys, grad_values, grad_log = recur_backward(
        queries,
        key_vec,
        values_in,
        log_forget,
        doc_ids,
        previous,
        start_state,
        grad_mixed.reshape(shape_blocks),
    )
    grad_gap = grad_keys.reshape(shape_flat) - grad_log.reshape(shape_flat) / (1.0 - gap_gate)
    gap_part = jnp.sum(grad_gap * open_gate, axis=(0, 1)).reshape(local_heads, head_size)
    grad_forget_in = -grad_gap * gap_gate * (1.0 - open_gate)
    grad_projected = jnp.concatenate(
        [
            grad_queries.reshape(shape_flat),
            grad_forget_in,
            grad_values.reshape(shape_flat),
            grad_gate_in,
        ],
        axis=-1,
    ).astype(jnp.bfloat16)
    mix_in_part = jnp.einsum(
        "tsd,tsc->dc", normed_all, grad_projected, preferred_element_type=jnp.float32
    )
    mix_in_part = mix_in_part.reshape(model_width, 4, local_chans)
    partial_value = grad_projected
    grad_normed = lax.psum_scatter(
        jnp.einsum(
            "tsc,dc->tsd", partial_value, in_flat, preferred_element_type=jnp.float32
        ).astype(jnp.bfloat16),
        "mp",
        scatter_dimension=0,
        tiled=True,
    ).astype(jnp.float32)
    norm1_part = jnp.sum(grad_normed * tokens * scale_one, axis=(0, 1))
    tokens_grad = grad_hidden + rms_back(grad_normed, tokens, scale_one, norm1_gain)
    seq_count = lax.axis_size("seq")
    arranged = out_part.reshape(
        mp_count, local_heads, seq_count, head_size // seq_count, model_width
    )
    arranged = jnp.transpose(arranged, (2, 0, 1, 3, 4)).reshape(
        seq_count * mp_count * local_heads, head_size // seq_count, model_width
    )
    mix_in_grad, gate_up_grad, down_grad, group_grad, gap_grad = (
        lax.psum_scatter(
            mix_in_part.astype(jnp.bfloat16), "seq", scatter_dimension=0, tiled=True
        ).astype(jnp.float32),
        lax.psum_scatter(
            gate_up_part.astype(jnp.bfloat16), "seq", scatter_dimension=0, tiled=True
        ).astype(jnp.float32),
        lax.psum_scatter(
            down_part.astype(jnp.bfloat16), "seq", scatter_dimension=1, tiled=True
        ).astype(jnp.float32),
        lax.psum_scatter(
            group_part.astype(jnp.bfloat16), "seq", scatter_dimension=1, tiled=True
        ).astype(jnp.float32),
        lax.psum_scatter(
            gap_part.astype(jnp.bfloat16), "seq", scatter_dimension=1, tiled=True
        ).astype(jnp.float32),
    )
    mix_out_grad, norm1_grad, norm2_grad = (
        lax.psum_scatter(arranged, ("seq", "mp"), scatter_dimension=0, tiled=True),
        lax.psum_scatter(norm1_part, ("seq", "mp"), scatter_dimension=0, tiled=True),
        lax.psum_scatter(norm2_part, ("seq", "mp"), scatter_dimension=0, tiled=True),
    )
    return (
        layer_out,
        tokens_grad,
        norm1_grad,
        mix_in_grad,
        gap_grad,
        group_grad,
        mix_out_grad,
        norm2_grad,
        gate_up_grad,
        down_grad,
    )


F32 = jnp.float32
BF16 = jnp.bfloat16


def mm(a, b, dims=((1,), (0,))):
    return lax.dot_general(a, b, (dims, ((), ())), preferred_element_type=F32)


NN, NT, TN = ((1,), (0,)), ((1,), (1,)), ((0,), (0,))


def split_two(value):
    high = value.astype(BF16)
    return high, (value - high.astype(F32)).astype(BF16)


def triangle(length, upper):
    row = lax.broadcasted_iota(jnp.int32, (length, length), 0)
    col = lax.broadcasted_iota(jnp.int32, (length, length), 1)
    return jnp.where((row <= col) if upper else (row >= col), 1.0, 0.0).astype(BF16)


def ids_of(lens, pack, positions):
    total, ids = 0, jnp.zeros_like(positions)
    for k in range(lens.shape[1]):
        total = total + lens[pack, k]
        ids = ids + jnp.where(positions >= total, 1, 0)
    return ids


def block_docs(lens, pack, base, length):
    col = ids_of(lens, pack, base + lax.broadcasted_iota(jnp.int32, (length, 1), 0))
    row = ids_of(lens, pack, base + lax.broadcasted_iota(jnp.int32, (1, length), 1))
    last = ids_of(lens, pack, base + length - 1 + jnp.zeros((1, 1), jnp.int32))
    before = ids_of(lens, pack, base - 1 + jnp.zeros((1, 1), jnp.int32))
    return col, row, last, before


def gates(pre_forget, gap):
    open_gate = jax.nn.sigmoid(-pre_forget)
    gap_gate = gap * open_gate
    return open_gate, gap_gate, gap_gate.astype(BF16).astype(F32), jnp.log1p(-gap_gate)


def mm_split(a, b, dims=((1,), (0,))):
    (a_high, a_low), (b_high, b_low) = split_two(a), split_two(b)
    return mm(a_high, b_high, dims) + mm(a_high, b_low, dims) + mm(a_low, b_high, dims)


def running_sum(ones, value):
    high, low = split_two(value)
    return mm(ones, high) + mm(ones, low)


def states_kernel(where, lens, gap, proj, state_out):
    step = pl.program_id(0)
    length = proj.shape[2]
    heads = state_out.shape[2]
    width = heads * 128
    first = lax.rem(step, where[3]) == 0
    base = position(where, step, length)
    ones = triangle(length, False)
    for p in range(proj.shape[1]):
        col, _, last_id, before = block_docs(lens, p, base, length)
        _, _, key, log_forget = gates(proj[0, p, :, :width], gap[...])
        cum = running_sum(ones, log_forget)
        last = cum[length - 1 :]
        khat = (key * jnp.where(col == last_id, jnp.exp(last - cum), 0.0)).astype(BF16)
        decay = jnp.where(last_id == before, jnp.exp(last), 0.0)
        for h in range(heads):
            at = slice(h * 128, h * 128 + 128)
            values = proj[0, p, :, width + h * 128 : width + h * 128 + 128].astype(BF16)
            made = mm(values, khat[:, at], TN)
            older = jnp.where(first, 0.0, state_out[p, 0, h, :128] * decay[:, at])
            state_out[p, 0, h, :128] = older + made
            kept = jnp.where(first, 1.0, state_out[p, 0, h, 128:])
            state_out[p, 0, h, 128:] = kept * decay[:, at]


def position(where, step, length):
    sub_run, part = lax.div(step, where[3]), lax.rem(step, where[3])
    return sub_run * where[1] + where[2] + part * length


def scan_kernel(reverse, count, steps, decays, states, out):
    now = jnp.zeros(out.shape[2:], F32)
    planes = states.shape[0]
    order = [(s, m) for s in range(steps) for m in range(planes)]
    for s, m in reversed(order) if reverse else order:
        out[m, s] = now.astype(BF16)
        kept = decays[m, s, 128:].astype(F32)[:1]
        now = now * kept + states[m, s, :128].astype(F32)


def forward_kernel(where, lens, gap, gain, proj, entering, heads_out, mixed_out, kept, state):
    step = pl.program_id(0)
    length = proj.shape[2]
    heads = state.shape[1]
    width = heads * 128

    @pl.when(lax.rem(step, where[3]) == 0)
    def _():
        state[...] = entering[:, 0].astype(F32)

    base = position(where, step, length)
    ones = triangle(length, False)
    row_index = lax.broadcasted_iota(jnp.int32, (length, length), 0)
    col_index = lax.broadcasted_iota(jnp.int32, (length, length), 1)
    for p in range(proj.shape[1]):
        col, row, last_id, before = block_docs(lens, p, base, length)
        _, _, key, log_forget = gates(proj[0, p, :, :width], gap[...])
        cum = running_sum(ones, log_forget)
        last = cum[length - 1 :]
        khat = (key * jnp.where(col == last_id, jnp.exp(last - cum), 0.0)).astype(BF16)
        decay = jnp.where(last_id == before, jnp.exp(last), 0.0)
        qt = proj[0, p, :, 2 * width : 3 * width].astype(BF16).astype(F32) * jnp.exp(cum)
        qe = jnp.where(col == before, qt, 0.0)
        kt = key * jnp.exp(-cum)
        visible = (col == row) & (row_index >= col_index)
        for h in range(heads):
            at = slice(h * 128, h * 128 + 128)
            values = proj[0, p, :, width + h * 128 : width + h * 128 + 128].astype(BF16)
            gate = proj[0, p, :, 3 * width + h * 128 : 3 * width + h * 128 + 128]
            now = state[p, h]
            kept[0, p, h] = now
            mixing = jnp.where(visible, mm_split(qt[:, at], kt[:, at], NT), 0.0).astype(BF16)
            mixed = mm(mixing, values) + mm_split(qe[:, at], now, NT)
            state[p, h] = now * decay[:, at] + mm(values, khat[:, at], TN)
            mixed_out[0, p, :, at] = mixed
            gated = mixed * (gate * jax.nn.sigmoid(gate))
            scale = lax.rsqrt(jnp.mean(gated * gated, axis=-1, keepdims=True) + EPSILON)
            heads_out[0, p, :, at] = (gated * scale * gain[:, at]).astype(BF16)


def gate_back_kernel(
    where, lens, gap, gain, proj, mixed_in, grad_heads, grad_out, grad_gate, group_part, run_out, state
):
    turn = pl.program_id(0)
    step = pl.num_programs(0) - 1 - turn
    length = proj.shape[2]
    heads = state.shape[1]
    width = heads * 128

    @pl.when(turn == 0)
    def _():
        group_part[...] = jnp.zeros_like(group_part)

    @pl.when(lax.rem(turn, where[3]) == 0)
    def _():
        state[...] = jnp.zeros_like(state)

    base = position(where, step, length)
    ones = triangle(length, False)
    for p in range(proj.shape[1]):
        col, _, last_id, before = block_docs(lens, p, base, length)
        _, _, _, log_forget = gates(proj[0, p, :, :width], gap[...])
        cum = running_sum(ones, log_forget)
        decay = jnp.where(last_id == before, jnp.exp(cum[length - 1 :]), 0.0)
        qt = proj[0, p, :, 2 * width : 3 * width].astype(BF16).astype(F32) * jnp.exp(cum)
        qe = jnp.where(col == before, qt, 0.0).astype(BF16)
        for h in range(heads):
            at = slice(h * 128, h * 128 + 128)
            gate = proj[0, p, :, 3 * width + h * 128 : 3 * width + h * 128 + 128]
            mixed = mixed_in[0, p, :, at]
            incoming = grad_heads[0, p, :, at].astype(F32)
            sigma = jax.nn.sigmoid(gate)
            act = gate * sigma
            gated = mixed * act
            scale = lax.rsqrt(jnp.mean(gated * gated, axis=-1, keepdims=True) + EPSILON)
            group_part[:, at] += jnp.sum(incoming * gated * scale, axis=0, keepdims=True)
            weighted = incoming * gain[:, at]
            inner = jnp.mean(weighted * gated, axis=-1, keepdims=True)
            grad_gated = scale * weighted - gated * (scale * scale * scale) * inner
            grad = grad_gated * act
            grad_out[0, p, :, at] = grad
            slope = sigma * (1.0 + gate * (1.0 - sigma))
            grad_gate[0, p, :, at] = (grad_gated * mixed * slope).astype(BF16)
            high, low = split_two(grad)
            own = mm(high, qe[:, at], TN) + mm(low, qe[:, at], TN)
            state[p, h] = state[p, h] * decay[:, at] + own
            run_out[p, 0, h] = state[p, h].astype(BF16)


def backward_kernel(
    where, lens, gap, proj, grad_out, grad_gate, kept, entering, grad_proj, gap_part, state
):
    turn = pl.program_id(0)
    step = pl.num_programs(0) - 1 - turn
    length = proj.shape[2]
    heads = state.shape[1]
    width = heads * 128

    @pl.when(turn == 0)
    def _():
        gap_part[...] = jnp.zeros_like(gap_part)

    @pl.when(lax.rem(turn, where[3]) == 0)
    def _():
        state[...] = entering[:, 0].astype(F32)

    base = position(where, step, length)
    ones = triangle(length, False)
    ones_up = triangle(length, True)
    row_index = lax.broadcasted_iota(jnp.int32, (length, length), 0)
    col_index = lax.broadcasted_iota(jnp.int32, (length, length), 1)
    for p in range(proj.shape[1]):
        col, row, last_id, before = block_docs(lens, p, base, length)
        open_gate, gap_gate, key, log_forget = gates(proj[0, p, :, :width], gap[...])
        cum = running_sum(ones, log_forget)
        last = cum[length - 1 :]
        ecum = jnp.exp(cum)
        encum = jnp.exp(-cum)
        tail = jnp.where(col == last_id, jnp.exp(last - cum), 0.0)
        khat = (key * tail).astype(BF16)
        decay = jnp.where(last_id == before, jnp.exp(last), 0.0)
        qt = proj[0, p, :, 2 * width : 3 * width].astype(BF16).astype(F32) * ecum
        enters = col == before
        qe = jnp.where(enters, qt, 0.0).astype(BF16)
        qt = qt.astype(BF16)
        kt = (key * encum).astype(BF16)
        visible = (col == row) & (row_index >= col_index)
        for h in range(heads):
            at = slice(h * 128, h * 128 + 128)
            values = proj[0, p, :, width + h * 128 : width + h * 128 + 128].astype(BF16)
            grad = grad_out[0, p, :, at]
            grad_enter = jnp.where(enters, grad, 0.0)
            grad, grad_low = split_two(grad)
            after = state[p, h]
            after_high, after_low = split_two(after)
            now = kept[0, p, h]
            mixing = jnp.where(visible, mm(qt[:, at], kt[:, at], NT), 0.0).astype(BF16)
            grad_mixing = mm(grad, values, NT) + mm(grad_low, values, NT)
            grad_mixing = jnp.where(visible, grad_mixing, 0.0).astype(BF16)
            grad_qt = mm(grad_mixing, kt[:, at]) + mm_split(grad_enter, now)
            grad_kt = mm(grad_mixing, qt[:, at], TN)
            grad_values = mm(mixing, grad, TN) + mm(khat[:, at], after_high, NT)
            grad_khat = mm(values, after_high) + mm(values, after_low)
            grad_decay = jnp.sum(after * now, axis=0, keepdims=True)
            own = mm(grad, qe[:, at], TN) + mm(grad_low, qe[:, at], TN)
            state[p, h] = after * decay[:, at] + own
            through = grad_khat * khat[:, at].astype(F32)
            grad_cum = (
                grad_qt * qt[:, at].astype(F32) - grad_kt * kt[:, at].astype(F32) - through
            )
            grad_last = jnp.sum(through, axis=0, keepdims=True) + grad_decay * decay[:, at]
            grad_log = running_sum(ones_up, grad_cum) + grad_last
            grad_keys = grad_kt * encum[:, at] + grad_khat * tail[:, at]
            grad_gap = grad_keys - grad_log / (1.0 - gap_gate[:, at])
            gap_part[:, at] += jnp.sum(grad_gap * open_gate[:, at], axis=0, keepdims=True)
            grad_forget = -grad_gap * gap_gate[:, at] * (1.0 - open_gate[:, at])
            made = (grad_forget, grad_values, grad_qt * ecum[:, at])
            for k, part in enumerate(made):
                start = k * width + h * 128
                grad_proj[0, p, :, start : start + 128] = part.astype(BF16)
        grad_proj[0, p, :, 3 * width :] = grad_gate[0, p]


def recur_call(kernel, steps, halves, reverse, where, ins, outs, scratch, flops, name):
    def index(kind, ndim):
        def place(turn, where_ref):
            step = steps - 1 - turn if reverse else turn
            run, half = lax.div(step, halves), lax.rem(step, halves)
            if kind == "near":
                return (lax.bitwise_xor(run, where_ref[0]), 0, half, 0)
            if kind == "rows":
                return (run, 0, half, 0)
            if kind == "block":
                return (step,) + (0,) * (ndim - 1)
            if kind == "run":
                return (0, run) + (0,) * (ndim - 2)
            return (0,) * ndim

        return place

    def spec(kind, block):
        if kind == "smem":
            return pl.BlockSpec(memory_space=pltpu.SMEM)
        return pl.BlockSpec(block, index(kind, len(block)))

    arrays = [array for array, _, _ in ins]
    moved = sum(a.size * a.dtype.itemsize for a in arrays)
    return pl.pallas_call(
        kernel,
        grid_spec=pltpu.PrefetchScalarGridSpec(
            num_scalar_prefetch=1,
            grid=(steps,),
            in_specs=[spec(kind, block or array.shape) for array, kind, block in ins],
            out_specs=[spec(kind, block or shape) for shape, _, kind, block in outs],
            scratch_shapes=scratch,
        ),
        out_shape=[jax.ShapeDtypeStruct(shape, dtype) for shape, dtype, _, _ in outs],
        compiler_params=pltpu.CompilerParams(
            dimension_semantics=("arbitrary",), vmem_limit_bytes=48 << 20
        ),
        cost_estimate=pl.CostEstimate(flops=flops, bytes_accessed=moved // 20, transcendentals=0),
        name=name,
    )(where, *arrays)


def scan_call(decays, states, reverse):
    return pl.pallas_call(
        functools.partial(scan_kernel, reverse, states.shape[0], states.shape[1]),
        out_shape=jax.ShapeDtypeStruct(states.shape[:2] + (128, 128), BF16),
        name="scan_back" if reverse else "scan",
    )(decays, states)


def project_kernel(tiles, left, right, weights, *rest):
    out = rest[-1]
    step = pl.program_id(0)

    @pl.when(step < tiles)
    def _():
        out[0] = mm(left[...], weights[...])

    @pl.when(step >= tiles)
    def _():
        out[0] = mm(right[...], weights[...])


def project_call(made, first, count, left, right, weights):
    rows, width = left.shape
    columns = weights.shape[1]
    tile = min(256, rows)
    tiles = rows // tile
    shape = (count, rows, columns)
    in_specs = [
        pl.BlockSpec((tile, width), lambda i: (jnp.minimum(i, tiles - 1), 0)),
        pl.BlockSpec((tile, width), lambda i: (jnp.maximum(i - tiles, 0), 0)),
        pl.BlockSpec(weights.shape, lambda i: (0, 0), pipeline_mode=pl.Buffered(1)),
    ]
    arrays = [left, right, weights]
    if made is not None:
        in_specs.append(pl.BlockSpec(memory_space=pl.ANY))
        arrays.append(made)
    return pl.pallas_call(
        functools.partial(project_kernel, tiles),
        grid=(2 * tiles,),
        in_specs=in_specs,
        out_specs=pl.BlockSpec(
            (1, tile, columns), lambda i: (first + lax.div(i, tiles), lax.rem(i, tiles), 0)
        ),
        out_shape=jax.ShapeDtypeStruct(shape, F32),
        input_output_aliases={} if made is None else {3: 0},
        compiler_params=pltpu.CompilerParams(
            dimension_semantics=("arbitrary",), vmem_limit_bytes=40 << 20
        ),
        cost_estimate=pl.CostEstimate(
            flops=rows * width * columns * 240 // 100, bytes_accessed=rows * width, transcendentals=0
        ),
        name="project",
    )(*arrays)


def back_kernel(tiles, left, right, grads, weights, out_left, out_right, part):
    step = pl.program_id(0)
    made = mm(grads[0], weights[...], NT)

    @pl.when(step == 0)
    def _():
        part[...] = jnp.zeros_like(part)

    @pl.when(step < tiles)
    def _():
        out_left[...] = made.astype(BF16)
        part[...] += jnp.sum(made * left[...].astype(F32), axis=0, keepdims=True)

    @pl.when(step >= tiles)
    def _():
        out_right[...] = made.astype(BF16)
        part[...] += jnp.sum(made * right[...].astype(F32), axis=0, keepdims=True)


def back_call(grads, first, left, right, weights):
    rows, width = left.shape
    columns = weights.shape[1]
    tile = min(256, rows)
    tiles = rows // tile

    def one(i):
        return (jnp.minimum(i, tiles - 1), 0)

    def two(i):
        return (jnp.maximum(i - tiles, 0), 0)

    return pl.pallas_call(
        functools.partial(back_kernel, tiles),
        grid=(2 * tiles,),
        in_specs=[
            pl.BlockSpec((tile, width), one),
            pl.BlockSpec((tile, width), two),
            pl.BlockSpec(
                (1, tile, columns), lambda i: (first + lax.div(i, tiles), lax.rem(i, tiles), 0)
            ),
            pl.BlockSpec(weights.shape, lambda i: (0, 0), pipeline_mode=pl.Buffered(1)),
        ],
        out_specs=[
            pl.BlockSpec((tile, width), one),
            pl.BlockSpec((tile, width), two),
            pl.BlockSpec((1, width), lambda i: (0, 0)),
        ],
        out_shape=[jax.ShapeDtypeStruct((rows, width), BF16)] * 2
        + [jax.ShapeDtypeStruct((1, width), F32)],
        compiler_params=pltpu.CompilerParams(
            dimension_semantics=("arbitrary",), vmem_limit_bytes=40 << 20
        ),
        cost_estimate=pl.CostEstimate(
            flops=rows * width * columns * 240 // 100, bytes_accessed=rows * width, transcendentals=0
        ),
        name="project_back",
    )(left, right, grads, weights)


def feed_kernel(*refs):
    two_refs, cot_refs, (w_low, w_high, w_dn), outs = refs[0:2], refs[2:4], refs[4:7], refs[7:]
    units = w_dn.shape[0]
    half = w_low.shape[0]
    for k in range(2):
        act_out, grad_out, down_out, back_out = outs[4 * k : 4 * k + 4]
        pre = mm(two_refs[k][:, :half], w_low[...]) + mm(two_refs[k][:, half:], w_high[...])
        gate, up = pre[:, :units], pre[:, units:]
        sigma = jax.nn.sigmoid(gate)
        silu = gate * sigma
        act = (silu * up).astype(BF16)
        act_out[...] = act
        down_out[...] = mm(act, w_dn[...]).astype(BF16)
        grad_act = mm(cot_refs[k][...], w_dn[...], NT)
        grad_out[:, :units] = (grad_act * up * (sigma * (1.0 + gate * (1.0 - sigma)))).astype(BF16)
        grad_out[:, units:] = (grad_act * silu).astype(BF16)
        back_out[:, :half] = mm(grad_out[...], w_low[...], NT).astype(BF16)
        back_out[:, half:] = mm(grad_out[...], w_high[...], NT).astype(BF16)


def feed_call(two, cot, w_low, w_high, w_dn):
    rows, width = two[0].shape
    units = w_dn.shape[0]
    tile = min(256, rows)

    def cut(columns):
        return pl.BlockSpec((tile, columns), lambda i: (i, 0))

    def still(array):
        return pl.BlockSpec(array.shape, lambda i: (0, 0), pipeline_mode=pl.Buffered(1))

    sizes = (units, 2 * units, width, width)
    flops = 2 * 2 * rows * width * 6 * units
    return pl.pallas_call(
        feed_kernel,
        grid=(rows // tile,),
        in_specs=[cut(width)] * 4 + [still(w_low), still(w_high), still(w_dn)],
        out_specs=[cut(s) for s in sizes] * 2,
        out_shape=[jax.ShapeDtypeStruct((rows, s), BF16) for s in sizes] * 2,
        compiler_params=pltpu.CompilerParams(
            dimension_semantics=("arbitrary",), vmem_limit_bytes=58 << 20
        ),
        cost_estimate=pl.CostEstimate(
            flops=flops * 60 // 100, bytes_accessed=rows * width, transcendentals=0
        ),
        name="feed",
    )(*two, *cot, w_low, w_high, w_dn)


def spread_kernel(grads, weights, out):
    units = weights[0, :, 0].reshape(-1, weights.shape[-1])
    out[0] = mm(grads[...], units, NT).astype(BF16)


def spread_call(grads, weights):
    cores, shards, chips, size, width = weights.shape
    rows = grads.shape[0]
    return pl.pallas_call(
        spread_kernel,
        grid=(cores * chips,),
        in_specs=[
            pl.BlockSpec(grads.shape, lambda s: (0, 0)),
            pl.BlockSpec(
                (1, shards, 1, size, width),
                lambda s: (lax.rem(s, cores), 0, lax.div(s, cores), 0, 0),
            ),
        ],
        out_specs=pl.BlockSpec((1, rows, shards * size), lambda s: (s, 0, 0)),
        out_shape=jax.ShapeDtypeStruct((cores * chips, rows, shards * size), BF16),
        compiler_params=pltpu.CompilerParams(
            dimension_semantics=("arbitrary",), vmem_limit_bytes=32 << 20
        ),
        cost_estimate=pl.CostEstimate(
            flops=rows * width * size * 1920 // 100, bytes_accessed=rows * width, transcendentals=0
        ),
        name="spread",
    )(grads, weights)


def heads_grad_kernel(pieces, heads, grads, out):
    made = mm(heads[0], grads[...], TN).astype(BF16)
    tall = made.shape[0] // out.shape[2]
    low = tall // pieces
    for j in range(out.shape[2]):
        for s in range(pieces):
            out[s, 0, j, 0] = made[j * tall + s * low : j * tall + (s + 1) * low]


def heads_grad_call(heads, grads, cores, shards):
    count, rows, chans = heads.shape
    width = grads.shape[1]
    size = chans // shards
    chips = count // cores
    shape = (count, cores, shards, chips, size // count, width)
    return pl.pallas_call(
        functools.partial(heads_grad_kernel, count),
        grid=(count,),
        in_specs=[
            pl.BlockSpec((1, rows, chans), lambda s: (s, 0, 0)),
            pl.BlockSpec(grads.shape, lambda s: (0, 0)),
        ],
        out_specs=pl.BlockSpec(
            (count, 1, shards, 1, size // count, width),
            lambda s: (0, lax.rem(s, cores), 0, lax.div(s, cores), 0, 0),
        ),
        out_shape=jax.ShapeDtypeStruct(shape, BF16),
        compiler_params=pltpu.CompilerParams(
            dimension_semantics=("arbitrary",), vmem_limit_bytes=32 << 20
        ),
        cost_estimate=pl.CostEstimate(
            flops=rows * width * size * 1920 // 100, bytes_accessed=rows * width, transcendentals=0
        ),
        name="mix_out_grad",
    )(heads, grads)


def outer_kernel(count, place, *refs):
    *inputs, out, total, left, right, sems = refs
    lefts, rights = inputs[:count], inputs[count:]
    if len(rights) < count:
        rights = [rights[0].at[k] for k in range(count)]
    step = pl.program_id(0)

    def fetch(block, slot):
        return (
            pltpu.make_async_copy(lefts[block], left.at[slot], sems.at[0, slot]),
            pltpu.make_async_copy(rights[block], right.at[slot], sems.at[1, slot]),
        )

    @pl.when(step == 0)
    def _():
        for copy in fetch(0, 0):
            copy.start()

    slot = lax.rem(step, 2)
    for block in range(1, count):

        @pl.when(step + 1 == block)
        def _(block=block):
            for copy in fetch(block, block % 2):
                copy.start()

    for copy in fetch(0, slot):
        copy.wait()

    @pl.when(step == 0)
    def _():
        total[...] = mm(left[0], right[0], TN)

    @pl.when(step > 0)
    def _():
        total[...] += mm(left[slot], right[slot], TN)

    @pl.when(step == count - 1)
    def _():
        place(out, total)


def outer_call(lefts, rights, shape, place, name):
    count = len(lefts)
    rows, m = lefts[0].shape
    n = rights[0].shape[-1]
    return pl.pallas_call(
        functools.partial(outer_kernel, count, place),
        grid=(count,),
        in_specs=[pl.BlockSpec(memory_space=pl.ANY)] * (count + len(rights)),
        out_specs=pl.BlockSpec(shape, lambda i: (0,) * len(shape), pipeline_mode=pl.Buffered(1)),
        out_shape=jax.ShapeDtypeStruct(shape, BF16),
        scratch_shapes=[
            pltpu.VMEM((m, n), F32),
            pltpu.VMEM((2, rows, m), BF16),
            pltpu.VMEM((2, rows, n), BF16),
            pltpu.SemaphoreType.DMA((2, 2)),
        ],
        compiler_params=pltpu.CompilerParams(
            dimension_semantics=("arbitrary",), vmem_limit_bytes=58 << 20
        ),
        cost_estimate=pl.CostEstimate(
            flops=count * rows * m * n * 120 // 100,
            bytes_accessed=rows * (m + n),
            transcendentals=0,
        ),
        name=name,
    )(*lefts, *rights)


def swap(value, across):
    return lax.ppermute(value, "seq", [(i, i ^ across) for i in range(lax.axis_size("seq"))])


CORE, XLINK, YLINK = 1, 2, 4
TILE = 128


def together(*values):
    return lax.optimization_barrier(values)


def plane_gather(own, beside=None, meet=None):
    half = own.shape[0] // 2
    got = {0: own, XLINK: swap(own, XLINK), YLINK: swap(own, YLINK), CORE: swap(own, CORE)}
    got, beside = together(got, beside)
    first = swap(got[YLINK][:half], XLINK)
    second = swap(got[XLINK][half:], YLINK)
    got[XLINK + CORE] = swap(got[XLINK], CORE)
    got[YLINK + CORE] = swap(got[YLINK], CORE)
    first, second, got, meet = together(first, second, got, meet)
    got[XLINK + YLINK] = jnp.concatenate([first, second])
    got[XLINK + YLINK + CORE] = jnp.concatenate([swap(first, CORE), swap(second, CORE)])
    return got, beside, meet


def add_low(a, b):
    return (a.astype(F32) + b.astype(F32)).astype(BF16)


def chip_sum(parts, a):
    return add_low(parts[a], swap(parts[a ^ CORE], CORE))


def first_hops(chip):
    half = chip[0].shape[0] // 2
    return (
        swap(chip[2][:half], XLINK),
        swap(chip[4][half:], YLINK),
        swap(chip[6][:half], XLINK),
        swap(chip[6][half:], YLINK),
    )


def turned(chip, hops):
    half = chip[4].shape[0] // 2
    return add_low(chip[4][:half], hops[2]), add_low(chip[2][half:], hops[3])


def last_hops(pair):
    return swap(pair[0], YLINK), swap(pair[1], XLINK)


def arrived(chip, hops, lasts):
    half = chip[0].shape[0] // 2
    low = chip[0][:half].astype(F32) + hops[0].astype(F32) + lasts[0].astype(F32)
    high = chip[0][half:].astype(F32) + hops[1].astype(F32) + lasts[1].astype(F32)
    return jnp.concatenate([low, high])


def pick(array, index, axis):
    return lax.dynamic_index_in_dim(array, index, axis, keepdims=False)


def plane_device(
    tokens,
    norm1_gain,
    w_mix_in,
    forget_gap,
    group_gain,
    w_mix_out,
    norm2_gain,
    w_gate_up,
    w_down,
    doc_lengths,
    out_cotangent,
):
    seq_count, mp_count = lax.axis_size("seq"), lax.axis_size("mp")
    seq_index, mp_index = lax.axis_index("seq"), lax.axis_index("mp")
    core, chip = seq_index % 2, seq_index // 2
    chips = seq_count // 2
    span, packs, width = tokens.shape
    rows = span * packs
    run = span * mp_count
    all_heads, head_size, _ = w_mix_out.shape
    heads = all_heads // seq_count
    chans = heads * head_size
    slice_d = width // seq_count

    def pack_major(array):
        return jnp.transpose(array, (1, 0, 2)).reshape(rows, width)

    def token_major(array):
        return jnp.transpose(array.reshape(packs, span, width), (1, 0, 2))

    def gather_shares(part):
        return lax.all_gather(part, "mp", axis=0).reshape((2, 2) + part.shape)

    def both_halves(pairs):
        mine = pick(pairs, core, 0)
        other = swap(pick(pairs, 1 - core, 0), CORE)
        return jnp.where(core == 0, mine, other), jnp.where(core == 0, other, mine)

    in_part = lax.dynamic_slice(
        w_mix_in, (0, 2 * core, chip * head_size), (width, 2, head_size)
    ).reshape(width, 2 * head_size)
    in_pairs = gather_shares(in_part)

    own = pack_major(tokens)
    scale_one = rms_scale(own)
    normed_own = (own * scale_one * norm1_gain).astype(BF16)

    small = pick(jnp.stack([forget_gap, group_gain]), chip, 1)[None]
    for bit in range(2):
        across = 1 << bit
        other = lax.ppermute(small, "mp", [(i, i ^ across) for i in range(mp_count)])
        low = (mp_index >> bit) % 2 == 0
        small = jnp.concatenate([jnp.where(low, small, other), jnp.where(low, other, small)])

    hidden_units = w_gate_up.shape[2]
    share = -(-hidden_units // (chips * TILE)) * TILE
    local_ff = 2 * share
    spare = share * chips - hidden_units
    begin = jnp.minimum(chip * share, hidden_units - share)
    gu_part = lax.dynamic_slice_in_dim(pick(w_gate_up, core, 1), begin, share, 1)
    dn_part = lax.dynamic_slice_in_dim(w_down, begin, share, 0)
    fresh = lax.broadcasted_iota(jnp.int32, (share, 1), 0) >= chip * share - begin
    dn_part = jnp.where(fresh, dn_part, jnp.zeros_like(dn_part))
    dn_part = lax.dynamic_slice_in_dim(dn_part, core * (share // 2), share // 2, 0)
    out_flat = w_mix_out.reshape(-1, width)
    normed, (gu_part, dn_part, small), in_pairs = plane_gather(
        normed_own, (gu_part, dn_part, small), in_pairs
    )
    gu_first, gu_second = gu_part[: width // 2], gu_part[width // 2 :]
    query_forget, value_gate = both_halves(in_pairs)
    w_in = jnp.concatenate(
        [
            part[j, :, k * head_size : (k + 1) * head_size]
            for part, k in ((query_forget, 1), (value_gate, 0), (query_forget, 0), (value_gate, 1))
            for j in range(2)
        ],
        axis=1,
    )

    cot_own = pack_major(lax.dynamic_slice_in_dim(out_cotangent, mp_index * span, span, 0))
    cot_low, gu_first, dn_part, _ = together(cot_own.astype(BF16), gu_first, dn_part, in_pairs)

    dn_pairs = gather_shares(dn_part)
    first_pairs = gather_shares(gu_first)

    small = pick(small.reshape(2, 2, 2, head_size), core, 0)
    gap_row, gain_row = small[:, 0].reshape(1, chans), small[:, 1].reshape(1, chans)

    projected = None
    for a in range(0, seq_count, 2):
        projected = project_call(projected, a, seq_count, normed[a], normed[a + 1], w_in)
    projected = projected.reshape(seq_count, packs, span, 4 * chans)

    halves = span // BLOCK
    steps = seq_count * halves
    where = jnp.stack([seq_index, run, mp_index * span, halves]).astype(jnp.int32)
    block = (1, packs, BLOCK, chans)
    fv_block = (1, packs, BLOCK, 2 * chans)
    wide = (1, packs, BLOCK, 4 * chans)
    pairs = packs * heads
    runs_shape = (packs, seq_count, heads, head_size, head_size)
    run_block = (packs, 1, heads, head_size, head_size)
    tall_shape = (packs, seq_count, heads, head_size + 8, head_size)
    tall_block = (packs, 1, heads, head_size + 8, head_size)
    unit = 2 * BLOCK * head_size * head_size * pairs * steps
    common = [(doc_lengths, "smem", None), (gap_row, "whole", None)]
    call = functools.partial(recur_call, steps=steps, halves=halves, where=where)

    def to_scan(array):
        array = jnp.transpose(array, (0, 2, 1, 3, 4)).astype(BF16)
        array = array.reshape((pairs,) + array.shape[2:])
        return lax.all_to_all(array, "mp", split_axis=0, concat_axis=0, tiled=True)

    def from_scan(array):
        array = lax.all_to_all(array, "mp", split_axis=0, concat_axis=0, tiled=True)
        array = array.reshape((packs, heads) + array.shape[1:])
        return jnp.transpose(array, (0, 2, 1, 3, 4))

    [run_state] = call(
        states_kernel,
        reverse=False,
        ins=common + [(projected, "near", fv_block)],
        outs=[(tall_shape, F32, "run", tall_block)],
        scratch=[],
        flops=27 * unit,
        name="run_states",
    )
    cot, run_state, _ = plane_gather(cot_low, run_state)
    decays = to_scan(run_state)
    entering = from_scan(scan_call(decays, decays, False))
    row_shape = (seq_count, packs, span, chans)
    state_shape = (packs, heads, head_size, head_size)
    heads_out, mixed, kept = call(
        forward_kernel,
        reverse=False,
        ins=common
        + [(gain_row, "whole", None), (projected, "near", wide), (entering, "run", run_block)],
        outs=[
            (row_shape, BF16, "rows", block),
            (row_shape, F32, "rows", block),
            ((steps,) + state_shape, F32, "block", (1,) + state_shape),
        ],
        scratch=[pltpu.VMEM(state_shape, F32)],
        flops=45 * unit,
        name="mix_forward",
    )
    gu_second, dn_pairs, first_pairs, cot, _ = together(
        gu_second, dn_pairs, first_pairs, cot, entering
    )
    second_pairs = gather_shares(gu_second)

    def side_by_side(pairs):
        gate, up = both_halves(pairs)
        return jnp.concatenate([gate[0], gate[1], up[0], up[1]], axis=1)

    w_dn = jnp.concatenate(both_halves(dn_pairs), axis=1).reshape(local_ff, width)
    w_low, w_high = side_by_side(first_pairs), side_by_side(second_pairs)

    split = (chips, 2, rows, 2, head_size)
    heads_by = lax.all_to_all(
        heads_out.reshape(seq_count, rows, chans), "seq", split_axis=0, concat_axis=0, tiled=True
    )
    heads_tok = jnp.transpose(heads_by.reshape(split), (2, 1, 3, 0, 4)).reshape(rows, -1)
    hidden = own + mm(heads_tok, out_flat)
    scale_two = rms_scale(hidden)
    normed_two = (hidden * scale_two * norm2_gain).astype(BF16)

    def ready(parts):
        mine = pick(parts, core, 0)
        other = swap(pick(parts, 1 - core, 0), CORE)
        low = jnp.where(core == 0, mine, other)
        high = jnp.where(core == 0, other, mine)
        return jnp.concatenate([low, high])

    def deliver(terms):
        return lax.psum_scatter(terms, "mp", scatter_dimension=0, tiled=True)[0]

    def handed(piece):
        groups = [list(range(k, seq_count, 2)) for k in range(2)]
        return lax.all_to_all(
            piece, "seq", split_axis=0, concat_axis=0, axis_index_groups=groups, tiled=True
        )

    act, grad_gu, down_parts, back_parts = {}, {}, {}, {}
    order = range(seq_count)

    def feed(a):
        made = feed_call((two[a], two[a + 1]), (cot[a], cot[a + 1]), w_low, w_high, w_dn)
        for k, at in enumerate((a, a + 1)):
            act[at], grad_gu[at], down_parts[at], back_parts[at] = made[4 * k : 4 * k + 4]

    two = {0: normed_two}
    for across in (CORE, XLINK, YLINK):
        two[across] = swap(normed_two, across)
    feed(0)
    two[XLINK], two[YLINK], down_parts[0] = together(two[XLINK], two[YLINK], down_parts[0])
    middle = rows // 2
    far_first = swap(two[YLINK][:middle], XLINK)
    far_second = swap(two[XLINK][middle:], YLINK)
    two[3], two[5] = swap(two[XLINK], CORE), swap(two[YLINK], CORE)
    feed(2)
    two[YLINK], down_parts[2] = together(two[YLINK], down_parts[2])
    feed(4)
    chip_back = {2: chip_sum(back_parts, 2)}
    far_first, far_second, chip_back, down_parts[4] = together(
        far_first, far_second, chip_back, down_parts[4]
    )
    two[6] = jnp.concatenate([far_first, far_second])
    two[7] = jnp.concatenate([swap(far_first, CORE), swap(far_second, CORE)])
    other = swap(back_parts[5], CORE)
    feed(6)
    other, back_parts = together(other, back_parts)
    chip_back[4] = add_low(back_parts[4], other)
    chip_back[6] = chip_sum(back_parts, 6)

    def place_gu(out, total):
        for d in range(seq_count):
            for j in range(2):
                for g in range(2):
                    at = (2 * g + j) * share
                    out[d % 2, j, d // 2, g] = total[
                        d * slice_d : (d + 1) * slice_d, at : at + share
                    ].astype(BF16)

    def place_dn(out, total):
        for d in range(seq_count):
            for j in range(2):
                out[d % 2, j, d // 2] = total[
                    j * share : (j + 1) * share, d * slice_d : (d + 1) * slice_d
                ].astype(BF16)

    chip_back, grad_gu = together(chip_back, grad_gu)
    gu_grad = outer_call(
        [two[a] for a in order],
        [grad_gu[a] for a in order],
        (2, 2, chips, 2, slice_d, share),
        place_gu,
        "gate_up_grad",
    )
    chip_back[0] = chip_sum(back_parts, 0)
    hops, chip_back, gu_grad = together(first_hops(chip_back), chip_back, gu_grad)
    onward, act = together(turned(chip_back, hops), act)
    dn_grad = outer_call(
        [act[a] for a in order],
        [cot[a] for a in order],
        (2, 2, chips, share, slice_d),
        place_dn,
        "down_grad",
    )
    lasts, dn_grad = together(last_hops(onward), dn_grad)
    grad_normed_two = arrived(chip_back, hops, lasts)
    grad_normed_two, down_parts = together(grad_normed_two, down_parts)

    norm2_part = jnp.sum(grad_normed_two * hidden * scale_two, axis=0)
    grad_hidden = cot_own + rms_back(grad_normed_two, hidden, scale_two, norm2_gain)
    grad_mix = grad_hidden.astype(BF16)
    grad_tok = spread_call(grad_mix, w_mix_out.reshape(2, 2, chips, head_size, width))
    grad_tok, dn_grad = together(grad_tok, ready(dn_grad))
    dn_grad = deliver(dn_grad)
    grad_heads = lax.all_to_all(grad_tok, "seq", split_axis=0, concat_axis=0, tiled=True)
    chip_down = {a: chip_sum(down_parts, a) for a in (2, 4, 6, 0)}
    out_grad = heads_grad_call(heads_by, grad_mix, 2, 2)
    grad_heads, chip_down, out_grad = together(
        grad_heads.reshape(row_shape), chip_down, out_grad
    )

    grad_out, grad_gate, group_part, run_grad = call(
        gate_back_kernel,
        reverse=True,
        ins=common
        + [
            (gain_row, "whole", None),
            (projected, "near", wide),
            (mixed, "rows", block),
            (grad_heads, "rows", block),
        ],
        outs=[
            (row_shape, F32, "rows", block),
            (row_shape, BF16, "rows", block),
            ((1, chans), F32, "whole", None),
            (runs_shape, BF16, "run", run_block),
        ],
        scratch=[pltpu.VMEM(state_shape, F32)],
        flops=35 * unit,
        name="gate_back",
    )
    out_grad = out_grad.reshape(seq_count, all_heads, head_size // seq_count, width)
    out_parts = {a: pick(out_grad, seq_index ^ a, 0) for a in range(seq_count)}
    chip_out = {a: chip_sum(out_parts, a) for a in (2, 4, 6, 0)}
    run_grad, chip_out = together(to_scan(run_grad), chip_out)
    entering_back = from_scan(scan_call(decays, run_grad, True))
    hops_down = first_hops(chip_down)
    entering_back, gu_grad = together(entering_back, ready(gu_grad))
    gu_grad = deliver(gu_grad)
    grad_projected, gap_part = call(
        backward_kernel,
        reverse=True,
        ins=common
        + [
            (projected, "near", wide),
            (grad_out, "rows", block),
            (grad_gate, "rows", block),
            (kept, "block", (1,) + state_shape),
            (entering_back, "run", run_block),
        ],
        outs=[
            ((seq_count, packs, span, 4 * chans), BF16, "near", wide),
            ((1, chans), F32, "whole", None),
        ],
        scratch=[pltpu.VMEM(state_shape, F32)],
        flops=69 * unit,
        name="mix_backward",
    )
    grad_projected = grad_projected.reshape(seq_count, rows, 4 * chans)
    grad_projected, dn_grad, hops_down = together(grad_projected, dn_grad, hops_down)
    dn_round = handed(dn_grad)
    lasts_down = last_hops(turned(chip_down, hops_down))
    chip_out = together(chip_out, grad_projected)[0]
    hops_out = first_hops(chip_out)
    def place_in(out, total):
        for d in range(seq_count):
            for j in range(2):
                for k, of in enumerate((2, 0, 1, 3)):
                    at = of * chans + j * head_size
                    out[d % 2, j, d // 2, :, k * head_size : (k + 1) * head_size] = total[
                        d * slice_d : (d + 1) * slice_d, at : at + head_size
                    ].astype(BF16)

    in_grad = outer_call(
        [normed[a] for a in order],
        [grad_projected],
        (2, 2, chips, slice_d, 4 * head_size),
        place_in,
        "mix_in_grad",
    )
    grad_projected, in_grad, lasts_down, dn_round = together(
        grad_projected, in_grad, lasts_down, dn_round
    )
    layer_out = token_major(hidden + arrived(chip_down, hops_down, lasts_down))
    in_parts, chip_in = {}, {}

    def back(a):
        in_parts[a], in_parts[a + 1], part = back_call(
            grad_projected, a, normed[a], normed[a + 1], w_in
        )
        return part

    def from_core(a):
        return swap(in_parts[a + 1], CORE)

    half = rows // 2
    in_mine = pick(in_grad, core, 0)
    in_other = swap(pick(in_grad, 1 - core, 0), CORE)
    norm1_part = back(6)
    grad_projected, in_mine, in_other, hops_out, in_parts = together(
        grad_projected, in_mine, in_other, hops_out, in_parts
    )
    lasts_out = last_hops(turned(chip_out, hops_out))
    in_grad = jnp.concatenate(
        [jnp.where(core == 0, in_mine, in_other), jnp.where(core == 0, in_other, in_mine)]
    )
    other = from_core(6)
    norm1_part = norm1_part + back(2)
    grad_projected, lasts_out, other, in_parts, in_grad, gu_grad = together(
        grad_projected, lasts_out, other, in_parts, in_grad, gu_grad
    )
    in_grad = deliver(in_grad)
    chip_in[6] = add_low(in_parts[6], other)
    far_hops = swap(chip_in[6][:half], XLINK), swap(chip_in[6][half:], YLINK)
    out_grad = arrived(chip_out, hops_out, lasts_out).astype(BF16)
    out_grad = out_grad.reshape((mp_count, all_heads // mp_count) + out_grad.shape[1:])
    other = from_core(2)
    norm1_part = norm1_part + back(4)
    grad_projected, other, in_parts = together(grad_projected, other, in_parts)
    chip_in[2] = add_low(in_parts[2], other)
    mine_x = swap(chip_in[2][:half], XLINK)
    other = from_core(4)
    def set_heads(part):
        row = jnp.zeros((2, 2, chips, head_size), F32)
        mine = part.reshape(1, 2, 1, head_size)
        row = lax.dynamic_update_slice(row, mine, (core, 0, chip, 0))
        row = row.reshape(mp_count, all_heads // mp_count, seq_count, head_size // seq_count)
        return jnp.transpose(row, (2, 0, 1, 3)).reshape(-1)

    grad_projected, far_hops, other, in_parts, chip_in, gu_round, out_grad = together(
        grad_projected, far_hops, other, in_parts, chip_in, handed(gu_grad), out_grad
    )
    out_grad = lax.psum_scatter(out_grad, "mp", scatter_dimension=0, tiled=True)[0]
    chip_in[4] = add_low(in_parts[4], other)
    hops = mine_x, swap(chip_in[4][half:], YLINK)
    lasts = last_hops(turned(chip_in, (None, None) + far_hops))
    norm1_part = norm1_part + back(0)
    gains = jnp.stack(
        [norm1_part[0] / norm1_gain, norm2_part, set_heads(gap_part), set_heads(group_part)]
    )
    gains = jnp.transpose(gains.reshape(4, seq_count, width // seq_count), (1, 0, 2))
    hops, lasts, chip_in, in_parts, layer_out, gains = together(
        hops, lasts, chip_in, in_parts, layer_out, gains
    )
    chip_in[0] = chip_sum(in_parts, 0)
    gains = jnp.sum(lax.all_to_all(gains, "seq", split_axis=0, concat_axis=0, tiled=True), axis=0)
    gains = jnp.transpose(gains.reshape(4, mp_count, -1), (1, 0, 2))
    gains = jnp.sum(lax.all_to_all(gains, "mp", split_axis=0, concat_axis=0, tiled=True), axis=0)
    grad_normed = arrived(chip_in, hops, lasts)
    got = [gu_round[c].astype(F32) for c in range(chips)]
    got[-1] = got[-1][:, :, spare:]
    gate_up_grad = jnp.transpose(jnp.concatenate(got, axis=-1), (1, 0, 2))
    got = [dn_round[c] for c in range(chips)]
    got[-1] = got[-1][spare:]
    down_grad = jnp.concatenate(got, axis=0).astype(F32)
    mix_out_grad = out_grad.astype(F32)
    in_round = handed(in_grad)
    got = [in_round[c].astype(F32).reshape(slice_d, 4, head_size) for c in range(chips)]
    mix_in_grad = jnp.concatenate(got, axis=-1)

    tokens_grad = token_major(
        grad_hidden + rms_back(grad_normed, own, scale_one, norm1_gain)
    )

    small = gains[2:].reshape(2, all_heads // mp_count, head_size // seq_count)
    return (
        layer_out,
        tokens_grad,
        gains[0],
        mix_in_grad,
        small[0],
        small[1],
        mix_out_grad,
        gains[1],
        gate_up_grad,
        down_grad,
    )


def solution(mesh):
    body = plane_device if dict(mesh.shape) == {"seq": 8, "mp": 4} else generic_device
    placed = (
        P(("seq", "mp"), None, None),
        P(),
        P(None, None, "mp"),
        P("mp", None),
        P("mp", None),
        P(),
        P(),
        P(None, None, "mp"),
        P("mp", None),
        P(),
        P("seq", None, None),
    )
    return jax.shard_map(
        body,
        mesh=mesh,
        in_specs=placed,
        out_specs=(
            P(("seq", "mp"), None, None),
            P(("seq", "mp"), None, None),
            P(("seq", "mp")),
            P("seq", None, "mp"),
            P("mp", "seq"),
            P("mp", "seq"),
            P("mp", "seq", None),
            P(("seq", "mp")),
            P("seq", None, "mp"),
            P("mp", "seq"),
        ),
        check_vma=False,
    )
```

```python
import functools

import jax
import jax.numpy as jnp
from jax import lax
from jax.experimental import pallas as pl
from jax.experimental.pallas import tpu as pltpu
from jax.sharding import PartitionSpec as P

BLOCK = 128


EPSILON = 1e-06
PRECISE = lax.Precision.HIGHEST


def entering(x, axis, combine, identity, reverse):
    length, index = (lax.axis_size(axis), lax.axis_index(axis))
    everything = jax.tree.map(
        lambda part, kind: lax.all_gather(part.astype(kind), axis), x, (jnp.bfloat16, jnp.bfloat16)
    )
    start = jax.tree.map(
        lambda part, zero: jnp.broadcast_to(jnp.asarray(zero, part.dtype), part.shape), x, identity
    )

    def turn(k, before):
        at = length - 1 - k if reverse else k
        reached = at > index if reverse else at < index
        new = combine(
            before, jax.tree.map(lambda part, own: part[at].astype(own.dtype), everything, x)
        )
        return jax.tree.map(lambda a, b: jnp.where(reached, a, b), new, before)

    return lax.fori_loop(0, length, turn, start)


def rounded(signal):
    return lax.optimization_barrier(signal.astype(jnp.bfloat16)).astype(jnp.float32)


def rms_scale(signal):
    return lax.rsqrt(jnp.mean(signal * signal, axis=-1, keepdims=True) + EPSILON)


def rms_back(gradient, signal, scaling, gain_vec):
    weighted = gradient * gain_vec
    inner_sum = jnp.mean(weighted * signal, axis=-1, keepdims=True)
    return scaling * weighted - signal * (scaling * scaling * scaling) * inner_sum


def silu_slope(signal):
    sigma_val = jax.nn.sigmoid(signal)
    return sigma_val * (1.0 + signal * (1.0 - sigma_val))


def doc_index(doc_lengths, positions):
    doc_ends = jnp.stack(
        [jnp.sum(doc_lengths[:, : k + 1], axis=1) for k in range(doc_lengths.shape[1])], axis=1
    )
    return jnp.sum((positions[:, None, None] >= doc_ends[None, :, :]).astype(jnp.int32), axis=2)


def chain_combine(earlier, later_part):
    return (earlier[0] * later_part[0], later_part[0][..., None] * earlier[1] + later_part[1])


def block_tables(log_forget, doc_ids, previous):
    length = log_forget.shape[1]
    row_index = lax.broadcasted_iota(jnp.int32, (length, length), 0)
    col_index = lax.broadcasted_iota(jnp.int32, (length, length), 1)
    lower_ones = (row_index >= col_index).astype(jnp.float32)
    cumulated = jnp.einsum("ij,njshk->nishk", lower_ones, log_forget, precision=PRECISE)
    last_sum = cumulated[:, -1]
    same_doc = doc_ids[:, :, None, :] == doc_ids[:, None, :, :]
    visible = jnp.transpose(same_doc & (row_index >= col_index)[None, :, :, None], (0, 3, 1, 2))[
        :, :, None
    ]
    enters = (doc_ids == previous[:, None, :]).astype(jnp.float32)[..., None, None]
    at_end = (doc_ids == doc_ids[:, -1:, :]).astype(jnp.float32)[..., None, None]
    alive_end = (doc_ids[:, -1] == previous).astype(jnp.float32)[..., None, None]
    decays = jnp.exp(last_sum) * alive_end
    return (lower_ones, cumulated, last_sum, visible, enters, at_end, decays)


def block_factors(queries, key_vec, cumulated, last_sum, at_end):
    q_tilde = queries * jnp.exp(cumulated)
    k_tilde = key_vec * jnp.exp(-cumulated)
    k_hat = key_vec * jnp.exp(last_sum[:, None] - cumulated) * at_end
    return (q_tilde, k_tilde, k_hat)


def recur_forward(queries, key_vec, values_in, log_forget, doc_ids, previous):
    lower_ones, cumulated, last_sum, visible, enters, at_end, decays = block_tables(
        log_forget, doc_ids, previous
    )
    q_tilde, k_tilde, k_hat = block_factors(queries, key_vec, cumulated, last_sum, at_end)
    scores = jnp.einsum("nishk,njshk->nshij", q_tilde, k_tilde, precision=PRECISE)
    mixing = jnp.where(visible, scores, 0.0)
    inside = jnp.einsum("nshij,njshv->nishv", mixing, values_in, precision=PRECISE)
    local_sum = jnp.einsum("njshk,njshv->nshkv", k_hat, values_in, precision=PRECISE)

    def advance(carried, element):
        state_now, product = carried
        factor, addend = element
        return ((factor[..., None] * state_now + addend, product * factor), (state_now, product))

    zero_state = jnp.zeros(local_sum.shape[1:], jnp.float32)
    unit_decay = jnp.ones(decays.shape[1:], jnp.float32)
    (run_state, run_decay), (prefix_state, prefix_decay) = lax.scan(
        advance, (zero_state, unit_decay), (decays, local_sum)
    )
    incoming = entering(
        (run_decay, run_state), "seq", chain_combine, (unit_decay, zero_state), False
    )[1]
    start_state = prefix_state + prefix_decay[..., None] * incoming[None]
    carried_in = jnp.einsum("nishk,nshkv->nishv", q_tilde * enters, start_state, precision=PRECISE)
    return (inside + carried_in, start_state)


def recur_backward(
    queries, key_vec, values_in, log_forget, doc_ids, previous, start_state, grad_out
):
    lower_ones, cumulated, last_sum, visible, enters, at_end, decays = block_tables(
        log_forget, doc_ids, previous
    )
    q_tilde, k_tilde, k_hat = block_factors(queries, key_vec, cumulated, last_sum, at_end)
    scores = jnp.einsum("nishk,njshk->nshij", q_tilde, k_tilde, precision=PRECISE)
    mixing = jnp.where(visible, scores, 0.0)
    own_term = jnp.einsum("nishk,nishv->nshkv", q_tilde * enters, grad_out, precision=PRECISE)

    def retreat(carried, element):
        running, product = carried
        factor, addend = element
        return ((addend + factor[..., None] * running, product * factor), (running, product))

    zero_state = jnp.zeros(own_term.shape[1:], jnp.float32)
    unit_decay = jnp.ones(decays.shape[1:], jnp.float32)
    (run_grad, run_decay), (after_sum, after_decay) = lax.scan(
        retreat, (zero_state, unit_decay), (decays, own_term), reverse=True
    )
    outgoing = entering(
        (run_decay, run_grad), "seq", chain_combine, (unit_decay, zero_state), True
    )[1]
    next_grad = after_sum + after_decay[..., None] * outgoing[None]
    grad_mixing = jnp.where(
        visible, jnp.einsum("nishv,njshv->nshij", grad_out, values_in, precision=PRECISE), 0.0
    )
    grad_qt = jnp.einsum("nshij,njshk->nishk", grad_mixing, k_tilde, precision=PRECISE)
    grad_qt = grad_qt + jnp.einsum(
        "nishv,nshkv->nishk", grad_out * enters, start_state, precision=PRECISE
    )
    grad_kt = jnp.einsum("nshij,nishk->njshk", grad_mixing, q_tilde, precision=PRECISE)
    grad_values = jnp.einsum("nshij,nishv->njshv", mixing, grad_out, precision=PRECISE)
    grad_values = grad_values + jnp.einsum(
        "njshk,nshkv->njshv", k_hat, next_grad, precision=PRECISE
    )
    grad_khat = jnp.einsum("njshv,nshkv->njshk", values_in, next_grad, precision=PRECISE) * at_end
    grad_decay = jnp.sum(next_grad * start_state, axis=-1)
    grad_queries = grad_qt * jnp.exp(cumulated)
    grad_keys = grad_kt * jnp.exp(-cumulated) + grad_khat * jnp.exp(last_sum[:, None] - cumulated)
    grad_cum = grad_qt * q_tilde - grad_kt * k_tilde - grad_khat * k_hat
    grad_last = jnp.sum(grad_khat * k_hat, axis=1) + grad_decay * decays
    grad_log = (
        jnp.einsum("it,nishk->ntshk", lower_ones, grad_cum, precision=PRECISE) + grad_last[:, None]
    )
    return (grad_queries, grad_keys, grad_values, grad_log)


def generic_device(
    tokens,
    norm1_gain,
    w_mix_in,
    forget_gap,
    group_gain,
    w_mix_out,
    norm2_gain,
    w_gate_up,
    w_down,
    doc_lengths,
    out_cotangent,
):
    mp_count = lax.axis_size("mp")
    rows_dev, pack_count, model_width = tokens.shape
    run_length = rows_dev * mp_count
    blocks = run_length // BLOCK
    local_heads, head_size = forget_gap.shape
    local_chans = local_heads * head_size
    local_ff = w_gate_up.shape[2]
    mp_index = lax.axis_index("mp")
    run_start = lax.axis_index("seq") * run_length
    positions = run_start - 1 + jnp.arange(run_length + 1, dtype=jnp.int32)
    all_ids = doc_index(doc_lengths, positions)
    doc_ids = all_ids[1:].reshape(blocks, BLOCK, pack_count)
    previous = all_ids[0:run_length:BLOCK]
    shape_blocks = (blocks, BLOCK, pack_count, local_heads, head_size)
    shape_heads = (run_length, pack_count, local_heads, head_size)
    shape_flat = (run_length, pack_count, local_chans)
    scale_one = rms_scale(tokens)
    normed = (tokens * scale_one * norm1_gain).astype(jnp.bfloat16)
    in_flat = w_mix_in.reshape(model_width, 4 * local_chans)
    shard_rows = lax.all_gather(normed, "mp", axis=0, tiled=True)
    normed_all = shard_rows
    projected = jnp.einsum("tsd,dc->tsc", shard_rows, in_flat, preferred_element_type=jnp.float32)
    pre_query = projected[..., :local_chans]
    pre_forget = projected[..., local_chans : 2 * local_chans]
    pre_value = projected[..., 2 * local_chans : 3 * local_chans]
    pre_gate = projected[..., 3 * local_chans :]
    open_gate = jax.nn.sigmoid(-pre_forget)
    gap_gate = forget_gap.reshape(local_chans) * open_gate
    queries = rounded(pre_query).reshape(shape_blocks)
    key_vec = rounded(gap_gate).reshape(shape_blocks)
    values_in = rounded(pre_value).reshape(shape_blocks)
    log_forget = jnp.log1p(-gap_gate).reshape(shape_blocks)
    mixed, start_state = recur_forward(queries, key_vec, values_in, log_forget, doc_ids, previous)
    mixed = mixed.reshape(shape_flat)
    gate_act = jax.nn.silu(pre_gate)
    gated_four = (mixed * gate_act).reshape(shape_heads)
    scale_group = rms_scale(gated_four)
    heads_out = (gated_four * scale_group * group_gain).astype(jnp.bfloat16).reshape(shape_flat)
    heads_tok = lax.all_to_all(heads_out, "mp", split_axis=0, concat_axis=2, tiled=True)
    out_flat = w_mix_out.reshape(-1, model_width)
    hidden = tokens + jnp.einsum(
        "tsc,cd->tsd", heads_tok, out_flat, preferred_element_type=jnp.float32
    )
    scale_two = rms_scale(hidden)
    normed_two = (hidden * scale_two * norm2_gain).astype(jnp.bfloat16)
    ffn_flat = w_gate_up.reshape(model_width, 2 * local_ff)
    shard_rows = lax.all_gather(normed_two, "mp", axis=0, tiled=True)
    gate_up = jnp.einsum("tsd,dc->tsc", shard_rows, ffn_flat, preferred_element_type=jnp.float32)
    pre_gate_two = gate_up[..., :local_ff]
    pre_up = gate_up[..., local_ff:]
    silu_two = jax.nn.silu(pre_gate_two)
    activation = (silu_two * pre_up).astype(jnp.bfloat16)
    partial_value = activation
    ffn_sum = lax.psum_scatter(
        jnp.einsum("tsf,fd->tsd", partial_value, w_down, preferred_element_type=jnp.float32).astype(
            jnp.bfloat16
        ),
        "mp",
        scatter_dimension=0,
        tiled=True,
    ).astype(jnp.float32)
    layer_out = hidden + ffn_sum
    cot_low = out_cotangent.astype(jnp.bfloat16)
    cot_own = lax.dynamic_slice_in_dim(out_cotangent, mp_index * rows_dev, rows_dev, 0)
    down_part = jnp.einsum("tsf,tsd->fd", activation, cot_low, preferred_element_type=jnp.float32)
    grad_act = jnp.einsum("tsd,fd->tsf", cot_low, w_down, preferred_element_type=jnp.float32)
    grad_gate_two = grad_act * pre_up * silu_slope(pre_gate_two)
    grad_up = grad_act * silu_two
    grad_gate_up = jnp.concatenate([grad_gate_two, grad_up], axis=-1).astype(jnp.bfloat16)
    gate_up_part = jnp.einsum(
        "tsd,tsc->dc", shard_rows, grad_gate_up, preferred_element_type=jnp.float32
    )
    gate_up_part = gate_up_part.reshape(model_width, 2, local_ff)
    partial_value = grad_gate_up
    grad_normed_two = lax.psum_scatter(
        jnp.einsum(
            "tsc,dc->tsd", partial_value, ffn_flat, preferred_element_type=jnp.float32
        ).astype(jnp.bfloat16),
        "mp",
        scatter_dimension=0,
        tiled=True,
    ).astype(jnp.float32)
    norm2_part = jnp.sum(grad_normed_two * hidden * scale_two, axis=(0, 1))
    grad_hidden = cot_own + rms_back(grad_normed_two, hidden, scale_two, norm2_gain)
    grad_mix = grad_hidden.astype(jnp.bfloat16)
    out_part = jnp.einsum("tsc,tsd->cd", heads_tok, grad_mix, preferred_element_type=jnp.float32)
    grad_tok = jnp.einsum(
        "tsd,cd->tsc", grad_mix, out_flat, preferred_element_type=jnp.float32
    ).astype(jnp.bfloat16)
    grad_heads = lax.all_to_all(grad_tok, "mp", split_axis=2, concat_axis=0, tiled=True).astype(
        jnp.float32
    )
    grad_four = grad_heads.reshape(shape_heads)
    group_part = jnp.sum(grad_four * gated_four * scale_group, axis=(0, 1))
    grad_gated = rms_back(grad_four, gated_four, scale_group, group_gain).reshape(shape_flat)
    grad_mixed = grad_gated * gate_act
    grad_gate_in = grad_gated * mixed * silu_slope(pre_gate)
    grad_queries, grad_keys, grad_values, grad_log = recur_backward(
        queries,
        key_vec,
        values_in,
        log_forget,
        doc_ids,
        previous,
        start_state,
        grad_mixed.reshape(shape_blocks),
    )
    grad_gap = grad_keys.reshape(shape_flat) - grad_log.reshape(shape_flat) / (1.0 - gap_gate)
    gap_part = jnp.sum(grad_gap * open_gate, axis=(0, 1)).reshape(local_heads, head_size)
    grad_forget_in = -grad_gap * gap_gate * (1.0 - open_gate)
    grad_projected = jnp.concatenate(
        [
            grad_queries.reshape(shape_flat),
            grad_forget_in,
            grad_values.reshape(shape_flat),
            grad_gate_in,
        ],
        axis=-1,
    ).astype(jnp.bfloat16)
    mix_in_part = jnp.einsum(
        "tsd,tsc->dc", normed_all, grad_projected, preferred_element_type=jnp.float32
    )
    mix_in_part = mix_in_part.reshape(model_width, 4, local_chans)
    partial_value = grad_projected
    grad_normed = lax.psum_scatter(
        jnp.einsum(
            "tsc,dc->tsd", partial_value, in_flat, preferred_element_type=jnp.float32
        ).astype(jnp.bfloat16),
        "mp",
        scatter_dimension=0,
        tiled=True,
    ).astype(jnp.float32)
    norm1_part = jnp.sum(grad_normed * tokens * scale_one, axis=(0, 1))
    tokens_grad = grad_hidden + rms_back(grad_normed, tokens, scale_one, norm1_gain)
    seq_count = lax.axis_size("seq")
    arranged = out_part.reshape(
        mp_count, local_heads, seq_count, head_size // seq_count, model_width
    )
    arranged = jnp.transpose(arranged, (2, 0, 1, 3, 4)).reshape(
        seq_count * mp_count * local_heads, head_size // seq_count, model_width
    )
    mix_in_grad, gate_up_grad, down_grad, group_grad, gap_grad = (
        lax.psum_scatter(
            mix_in_part.astype(jnp.bfloat16), "seq", scatter_dimension=0, tiled=True
        ).astype(jnp.float32),
        lax.psum_scatter(
            gate_up_part.astype(jnp.bfloat16), "seq", scatter_dimension=0, tiled=True
        ).astype(jnp.float32),
        lax.psum_scatter(
            down_part.astype(jnp.bfloat16), "seq", scatter_dimension=1, tiled=True
        ).astype(jnp.float32),
        lax.psum_scatter(
            group_part.astype(jnp.bfloat16), "seq", scatter_dimension=1, tiled=True
        ).astype(jnp.float32),
        lax.psum_scatter(
            gap_part.astype(jnp.bfloat16), "seq", scatter_dimension=1, tiled=True
        ).astype(jnp.float32),
    )
    mix_out_grad, norm1_grad, norm2_grad = (
        lax.psum_scatter(arranged, ("seq", "mp"), scatter_dimension=0, tiled=True),
        lax.psum_scatter(norm1_part, ("seq", "mp"), scatter_dimension=0, tiled=True),
        lax.psum_scatter(norm2_part, ("seq", "mp"), scatter_dimension=0, tiled=True),
    )
    return (
        layer_out,
        tokens_grad,
        norm1_grad,
        mix_in_grad,
        gap_grad,
        group_grad,
        mix_out_grad,
        norm2_grad,
        gate_up_grad,
        down_grad,
    )


F32 = jnp.float32
BF16 = jnp.bfloat16


def mm(a, b, dims=((1,), (0,))):
    return lax.dot_general(a, b, (dims, ((), ())), preferred_element_type=F32)


NN, NT, TN = ((1,), (0,)), ((1,), (1,)), ((0,), (0,))


def split_two(value):
    high = value.astype(BF16)
    return high, (value - high.astype(F32)).astype(BF16)


def triangle(length, upper):
    row = lax.broadcasted_iota(jnp.int32, (length, length), 0)
    col = lax.broadcasted_iota(jnp.int32, (length, length), 1)
    return jnp.where((row <= col) if upper else (row >= col), 1.0, 0.0).astype(BF16)


def ids_of(lens, pack, positions):
    total, ids = 0, jnp.zeros_like(positions)
    for k in range(lens.shape[1]):
        total = total + lens[pack, k]
        ids = ids + jnp.where(positions >= total, 1, 0)
    return ids


def block_docs(lens, pack, base, length):
    col = ids_of(lens, pack, base + lax.broadcasted_iota(jnp.int32, (length, 1), 0))
    row = ids_of(lens, pack, base + lax.broadcasted_iota(jnp.int32, (1, length), 1))
    last = ids_of(lens, pack, base + length - 1 + jnp.zeros((1, 1), jnp.int32))
    before = ids_of(lens, pack, base - 1 + jnp.zeros((1, 1), jnp.int32))
    return col, row, last, before


def gates(pre_forget, gap):
    open_gate = jax.nn.sigmoid(-pre_forget)
    gap_gate = gap * open_gate
    return open_gate, gap_gate, gap_gate.astype(BF16).astype(F32), jnp.log1p(-gap_gate)


def mm_split(a, b, dims=((1,), (0,))):
    (a_high, a_low), (b_high, b_low) = split_two(a), split_two(b)
    return mm(a_high, b_high, dims) + mm(a_high, b_low, dims) + mm(a_low, b_high, dims)


def running_sum(ones, value):
    high, low = split_two(value)
    return mm(ones, high) + mm(ones, low)


def states_kernel(where, lens, gap, proj, state_out):
    step = pl.program_id(0)
    length = proj.shape[2]
    heads = state_out.shape[2]
    width = heads * 128
    first = lax.rem(step, where[3]) == 0
    base = position(where, step, length)
    ones = triangle(length, False)
    for p in range(proj.shape[1]):
        col, _, last_id, before = block_docs(lens, p, base, length)
        _, _, key, log_forget = gates(proj[0, p, :, :width], gap[...])
        cum = running_sum(ones, log_forget)
        last = cum[length - 1 :]
        khat = (key * jnp.where(col == last_id, jnp.exp(last - cum), 0.0)).astype(BF16)
        decay = jnp.where(last_id == before, jnp.exp(last), 0.0)
        for h in range(heads):
            at = slice(h * 128, h * 128 + 128)
            values = proj[0, p, :, width + h * 128 : width + h * 128 + 128].astype(BF16)
            made = mm(values, khat[:, at], TN)
            older = jnp.where(first, 0.0, state_out[p, 0, h, :128] * decay[:, at])
            state_out[p, 0, h, :128] = older + made
            kept = jnp.where(first, 1.0, state_out[p, 0, h, 128:])
            state_out[p, 0, h, 128:] = kept * decay[:, at]


def position(where, step, length):
    sub_run, part = lax.div(step, where[3]), lax.rem(step, where[3])
    return sub_run * where[1] + where[2] + part * length


def scan_kernel(reverse, count, steps, decays, states, out):
    now = jnp.zeros(out.shape[2:], F32)
    planes = states.shape[0]
    order = [(s, m) for s in range(steps) for m in range(planes)]
    for s, m in reversed(order) if reverse else order:
        out[m, s] = now.astype(BF16)
        kept = decays[m, s, 128:].astype(F32)[:1]
        now = now * kept + states[m, s, :128].astype(F32)


def forward_kernel(where, lens, gap, gain, proj, entering, heads_out, mixed_out, kept, state):
    step = pl.program_id(0)
    length = proj.shape[2]
    heads = state.shape[1]
    width = heads * 128

    @pl.when(lax.rem(step, where[3]) == 0)
    def _():
        state[...] = entering[:, 0].astype(F32)

    base = position(where, step, length)
    ones = triangle(length, False)
    row_index = lax.broadcasted_iota(jnp.int32, (length, length), 0)
    col_index = lax.broadcasted_iota(jnp.int32, (length, length), 1)
    for p in range(proj.shape[1]):
        col, row, last_id, before = block_docs(lens, p, base, length)
        _, _, key, log_forget = gates(proj[0, p, :, :width], gap[...])
        cum = running_sum(ones, log_forget)
        last = cum[length - 1 :]
        khat = (key * jnp.where(col == last_id, jnp.exp(last - cum), 0.0)).astype(BF16)
        decay = jnp.where(last_id == before, jnp.exp(last), 0.0)
        qt = proj[0, p, :, 2 * width : 3 * width].astype(BF16).astype(F32) * jnp.exp(cum)
        qe = jnp.where(col == before, qt, 0.0)
        kt = key * jnp.exp(-cum)
        visible = (col == row) & (row_index >= col_index)
        for h in range(heads):
            at = slice(h * 128, h * 128 + 128)
            values = proj[0, p, :, width + h * 128 : width + h * 128 + 128].astype(BF16)
            gate = proj[0, p, :, 3 * width + h * 128 : 3 * width + h * 128 + 128]
            now = state[p, h]
            kept[0, p, h] = now
            mixing = jnp.where(visible, mm_split(qt[:, at], kt[:, at], NT), 0.0).astype(BF16)
            mixed = mm(mixing, values) + mm_split(qe[:, at], now, NT)
            state[p, h] = now * decay[:, at] + mm(values, khat[:, at], TN)
            mixed_out[0, p, :, at] = mixed
            gated = mixed * (gate * jax.nn.sigmoid(gate))
            scale = lax.rsqrt(jnp.mean(gated * gated, axis=-1, keepdims=True) + EPSILON)
            heads_out[0, p, :, at] = (gated * scale * gain[:, at]).astype(BF16)


def gate_back_kernel(
    where, lens, gap, gain, proj, mixed_in, grad_heads, grad_out, grad_gate, group_part, run_out, state
):
    turn = pl.program_id(0)
    step = pl.num_programs(0) - 1 - turn
    length = proj.shape[2]
    heads = state.shape[1]
    width = heads * 128

    @pl.when(turn == 0)
    def _():
        group_part[...] = jnp.zeros_like(group_part)

    @pl.when(lax.rem(turn, where[3]) == 0)
    def _():
        state[...] = jnp.zeros_like(state)

    base = position(where, step, length)
    ones = triangle(length, False)
    for p in range(proj.shape[1]):
        col, _, last_id, before = block_docs(lens, p, base, length)
        _, _, _, log_forget = gates(proj[0, p, :, :width], gap[...])
        cum = running_sum(ones, log_forget)
        decay = jnp.where(last_id == before, jnp.exp(cum[length - 1 :]), 0.0)
        qt = proj[0, p, :, 2 * width : 3 * width].astype(BF16).astype(F32) * jnp.exp(cum)
        qe = jnp.where(col == before, qt, 0.0).astype(BF16)
        for h in range(heads):
            at = slice(h * 128, h * 128 + 128)
            gate = proj[0, p, :, 3 * width + h * 128 : 3 * width + h * 128 + 128]
            mixed = mixed_in[0, p, :, at]
            incoming = grad_heads[0, p, :, at].astype(F32)
            sigma = jax.nn.sigmoid(gate)
            act = gate * sigma
            gated = mixed * act
            scale = lax.rsqrt(jnp.mean(gated * gated, axis=-1, keepdims=True) + EPSILON)
            group_part[:, at] += jnp.sum(incoming * gated * scale, axis=0, keepdims=True)
            weighted = incoming * gain[:, at]
            inner = jnp.mean(weighted * gated, axis=-1, keepdims=True)
            grad_gated = scale * weighted - gated * (scale * scale * scale) * inner
            grad = grad_gated * act
            grad_out[0, p, :, at] = grad
            slope = sigma * (1.0 + gate * (1.0 - sigma))
            grad_gate[0, p, :, at] = (grad_gated * mixed * slope).astype(BF16)
            high, low = split_two(grad)
            own = mm(high, qe[:, at], TN) + mm(low, qe[:, at], TN)
            state[p, h] = state[p, h] * decay[:, at] + own
            run_out[p, 0, h] = state[p, h].astype(BF16)


def backward_kernel(
    where, lens, gap, proj, grad_out, grad_gate, kept, entering, grad_proj, gap_part, state
):
    turn = pl.program_id(0)
    step = pl.num_programs(0) - 1 - turn
    length = proj.shape[2]
    heads = state.shape[1]
    width = heads * 128

    @pl.when(turn == 0)
    def _():
        gap_part[...] = jnp.zeros_like(gap_part)

    @pl.when(lax.rem(turn, where[3]) == 0)
    def _():
        state[...] = entering[:, 0].astype(F32)

    base = position(where, step, length)
    ones = triangle(length, False)
    ones_up = triangle(length, True)
    row_index = lax.broadcasted_iota(jnp.int32, (length, length), 0)
    col_index = lax.broadcasted_iota(jnp.int32, (length, length), 1)
    for p in range(proj.shape[1]):
        col, row, last_id, before = block_docs(lens, p, base, length)
        open_gate, gap_gate, key, log_forget = gates(proj[0, p, :, :width], gap[...])
        cum = running_sum(ones, log_forget)
        last = cum[length - 1 :]
        ecum = jnp.exp(cum)
        encum = jnp.exp(-cum)
        tail = jnp.where(col == last_id, jnp.exp(last - cum), 0.0)
        khat = (key * tail).astype(BF16)
        decay = jnp.where(last_id == before, jnp.exp(last), 0.0)
        qt = proj[0, p, :, 2 * width : 3 * width].astype(BF16).astype(F32) * ecum
        enters = col == before
        qe = jnp.where(enters, qt, 0.0).astype(BF16)
        qt = qt.astype(BF16)
        kt = (key * encum).astype(BF16)
        visible = (col == row) & (row_index >= col_index)
        for h in range(heads):
            at = slice(h * 128, h * 128 + 128)
            values = proj[0, p, :, width + h * 128 : width + h * 128 + 128].astype(BF16)
            grad = grad_out[0, p, :, at]
            grad_enter = jnp.where(enters, grad, 0.0)
            grad, grad_low = split_two(grad)
            after = state[p, h]
            after_high, after_low = split_two(after)
            now = kept[0, p, h]
            mixing = jnp.where(visible, mm(qt[:, at], kt[:, at], NT), 0.0).astype(BF16)
            grad_mixing = mm(grad, values, NT) + mm(grad_low, values, NT)
            grad_mixing = jnp.where(visible, grad_mixing, 0.0).astype(BF16)
            grad_qt = mm(grad_mixing, kt[:, at]) + mm_split(grad_enter, now)
            grad_kt = mm(grad_mixing, qt[:, at], TN)
            grad_values = mm(mixing, grad, TN) + mm(khat[:, at], after_high, NT)
            grad_khat = mm(values, after_high) + mm(values, after_low)
            grad_decay = jnp.sum(after * now, axis=0, keepdims=True)
            own = mm(grad, qe[:, at], TN) + mm(grad_low, qe[:, at], TN)
            state[p, h] = after * decay[:, at] + own
            through = grad_khat * khat[:, at].astype(F32)
            grad_cum = (
                grad_qt * qt[:, at].astype(F32) - grad_kt * kt[:, at].astype(F32) - through
            )
            grad_last = jnp.sum(through, axis=0, keepdims=True) + grad_decay * decay[:, at]
            grad_log = running_sum(ones_up, grad_cum) + grad_last
            grad_keys = grad_kt * encum[:, at] + grad_khat * tail[:, at]
            grad_gap = grad_keys - grad_log / (1.0 - gap_gate[:, at])
            gap_part[:, at] += jnp.sum(grad_gap * open_gate[:, at], axis=0, keepdims=True)
            grad_forget = -grad_gap * gap_gate[:, at] * (1.0 - open_gate[:, at])
            made = (grad_forget, grad_values, grad_qt * ecum[:, at])
            for k, part in enumerate(made):
                start = k * width + h * 128
                grad_proj[0, p, :, start : start + 128] = part.astype(BF16)
        grad_proj[0, p, :, 3 * width :] = grad_gate[0, p]


def recur_call(kernel, steps, halves, reverse, where, ins, outs, scratch, flops, name):
    def index(kind, ndim):
        def place(turn, where_ref):
            step = steps - 1 - turn if reverse else turn
            run, half = lax.div(step, halves), lax.rem(step, halves)
            if kind == "near":
                return (lax.bitwise_xor(run, where_ref[0]), 0, half, 0)
            if kind == "rows":
                return (run, 0, half, 0)
            if kind == "block":
                return (step,) + (0,) * (ndim - 1)
            if kind == "run":
                return (0, run) + (0,) * (ndim - 2)
            return (0,) * ndim

        return place

    def spec(kind, block):
        if kind == "smem":
            return pl.BlockSpec(memory_space=pltpu.SMEM)
        return pl.BlockSpec(block, index(kind, len(block)))

    arrays = [array for array, _, _ in ins]
    moved = sum(a.size * a.dtype.itemsize for a in arrays)
    return pl.pallas_call(
        kernel,
        grid_spec=pltpu.PrefetchScalarGridSpec(
            num_scalar_prefetch=1,
            grid=(steps,),
            in_specs=[spec(kind, block or array.shape) for array, kind, block in ins],
            out_specs=[spec(kind, block or shape) for shape, _, kind, block in outs],
            scratch_shapes=scratch,
        ),
        out_shape=[jax.ShapeDtypeStruct(shape, dtype) for shape, dtype, _, _ in outs],
        compiler_params=pltpu.CompilerParams(
            dimension_semantics=("arbitrary",), vmem_limit_bytes=48 << 20
        ),
        cost_estimate=pl.CostEstimate(flops=flops, bytes_accessed=moved // 20, transcendentals=0),
        name=name,
    )(where, *arrays)


def scan_call(decays, states, reverse):
    return pl.pallas_call(
        functools.partial(scan_kernel, reverse, states.shape[0], states.shape[1]),
        out_shape=jax.ShapeDtypeStruct(states.shape[:2] + (128, 128), BF16),
        name="scan_back" if reverse else "scan",
    )(decays, states)


def project_kernel(tiles, left, right, weights, *rest):
    out = rest[-1]
    step = pl.program_id(0)

    @pl.when(step < tiles)
    def _():
        out[0] = mm(left[...], weights[...])

    @pl.when(step >= tiles)
    def _():
        out[0] = mm(right[...], weights[...])


def project_call(made, first, count, left, right, weights):
    rows, width = left.shape
    columns = weights.shape[1]
    tile = min(256, rows)
    tiles = rows // tile
    shape = (count, rows, columns)
    in_specs = [
        pl.BlockSpec((tile, width), lambda i: (jnp.minimum(i, tiles - 1), 0)),
        pl.BlockSpec((tile, width), lambda i: (jnp.maximum(i - tiles, 0), 0)),
        pl.BlockSpec(weights.shape, lambda i: (0, 0), pipeline_mode=pl.Buffered(1)),
    ]
    arrays = [left, right, weights]
    if made is not None:
        in_specs.append(pl.BlockSpec(memory_space=pl.ANY))
        arrays.append(made)
    return pl.pallas_call(
        functools.partial(project_kernel, tiles),
        grid=(2 * tiles,),
        in_specs=in_specs,
        out_specs=pl.BlockSpec(
            (1, tile, columns), lambda i: (first + lax.div(i, tiles), lax.rem(i, tiles), 0)
        ),
        out_shape=jax.ShapeDtypeStruct(shape, F32),
        input_output_aliases={} if made is None else {3: 0},
        compiler_params=pltpu.CompilerParams(
            dimension_semantics=("arbitrary",), vmem_limit_bytes=40 << 20
        ),
        cost_estimate=pl.CostEstimate(
            flops=rows * width * columns * 150 // 100, bytes_accessed=rows * width, transcendentals=0
        ),
        name="project",
    )(*arrays)


def back_kernel(tiles, left, right, grads, weights, out_left, out_right, part):
    step = pl.program_id(0)
    made = mm(grads[0], weights[...], NT)

    @pl.when(step == 0)
    def _():
        part[...] = jnp.zeros_like(part)

    @pl.when(step < tiles)
    def _():
        out_left[...] = made.astype(BF16)
        part[...] += jnp.sum(made * left[...].astype(F32), axis=0, keepdims=True)

    @pl.when(step >= tiles)
    def _():
        out_right[...] = made.astype(BF16)
        part[...] += jnp.sum(made * right[...].astype(F32), axis=0, keepdims=True)


def back_call(grads, first, left, right, weights):
    rows, width = left.shape
    columns = weights.shape[1]
    tile = min(256, rows)
    tiles = rows // tile

    def one(i):
        return (jnp.minimum(i, tiles - 1), 0)

    def two(i):
        return (jnp.maximum(i - tiles, 0), 0)

    return pl.pallas_call(
        functools.partial(back_kernel, tiles),
        grid=(2 * tiles,),
        in_specs=[
            pl.BlockSpec((tile, width), one),
            pl.BlockSpec((tile, width), two),
            pl.BlockSpec(
                (1, tile, columns), lambda i: (first + lax.div(i, tiles), lax.rem(i, tiles), 0)
            ),
            pl.BlockSpec(weights.shape, lambda i: (0, 0), pipeline_mode=pl.Buffered(1)),
        ],
        out_specs=[
            pl.BlockSpec((tile, width), one),
            pl.BlockSpec((tile, width), two),
            pl.BlockSpec((1, width), lambda i: (0, 0)),
        ],
        out_shape=[jax.ShapeDtypeStruct((rows, width), BF16)] * 2
        + [jax.ShapeDtypeStruct((1, width), F32)],
        compiler_params=pltpu.CompilerParams(
            dimension_semantics=("arbitrary",), vmem_limit_bytes=40 << 20
        ),
        cost_estimate=pl.CostEstimate(
            flops=rows * width * columns * 150 // 100, bytes_accessed=rows * width, transcendentals=0
        ),
        name="project_back",
    )(left, right, grads, weights)


def feed_kernel(*refs):
    two_refs, cot_refs, (w_low, w_high, w_dn), outs = refs[0:2], refs[2:4], refs[4:7], refs[7:]
    units = w_dn.shape[0]
    half = w_low.shape[0]
    for k in range(2):
        act_out, grad_out, down_out, back_out = outs[4 * k : 4 * k + 4]
        pre = mm(two_refs[k][:, :half], w_low[...]) + mm(two_refs[k][:, half:], w_high[...])
        gate, up = pre[:, :units], pre[:, units:]
        sigma = jax.nn.sigmoid(gate)
        silu = gate * sigma
        act = (silu * up).astype(BF16)
        act_out[...] = act
        down_out[...] = mm(act, w_dn[...]).astype(BF16)
        grad_act = mm(cot_refs[k][...], w_dn[...], NT)
        grad_out[:, :units] = (grad_act * up * (sigma * (1.0 + gate * (1.0 - sigma)))).astype(BF16)
        grad_out[:, units:] = (grad_act * silu).astype(BF16)
        back_out[:, :half] = mm(grad_out[...], w_low[...], NT).astype(BF16)
        back_out[:, half:] = mm(grad_out[...], w_high[...], NT).astype(BF16)


def feed_call(two, cot, w_low, w_high, w_dn):
    rows, width = two[0].shape
    units = w_dn.shape[0]
    tile = min(256, rows)

    def cut(columns):
        return pl.BlockSpec((tile, columns), lambda i: (i, 0))

    def still(array):
        return pl.BlockSpec(array.shape, lambda i: (0, 0), pipeline_mode=pl.Buffered(1))

    sizes = (units, 2 * units, width, width)
    flops = 2 * 2 * rows * width * 6 * units
    return pl.pallas_call(
        feed_kernel,
        grid=(rows // tile,),
        in_specs=[cut(width)] * 4 + [still(w_low), still(w_high), still(w_dn)],
        out_specs=[cut(s) for s in sizes] * 2,
        out_shape=[jax.ShapeDtypeStruct((rows, s), BF16) for s in sizes] * 2,
        compiler_params=pltpu.CompilerParams(
            dimension_semantics=("arbitrary",), vmem_limit_bytes=58 << 20
        ),
        cost_estimate=pl.CostEstimate(
            flops=flops * 38 // 100, bytes_accessed=rows * width, transcendentals=0
        ),
        name="feed",
    )(*two, *cot, w_low, w_high, w_dn)


def spread_kernel(grads, weights, out):
    units = weights[0, :, 0].reshape(-1, weights.shape[-1])
    out[0] = mm(grads[...], units, NT).astype(BF16)


def spread_call(grads, weights):
    cores, shards, chips, size, width = weights.shape
    rows = grads.shape[0]
    return pl.pallas_call(
        spread_kernel,
        grid=(cores * chips,),
        in_specs=[
            pl.BlockSpec(grads.shape, lambda s: (0, 0)),
            pl.BlockSpec(
                (1, shards, 1, size, width),
                lambda s: (lax.rem(s, cores), 0, lax.div(s, cores), 0, 0),
            ),
        ],
        out_specs=pl.BlockSpec((1, rows, shards * size), lambda s: (s, 0, 0)),
        out_shape=jax.ShapeDtypeStruct((cores * chips, rows, shards * size), BF16),
        compiler_params=pltpu.CompilerParams(
            dimension_semantics=("arbitrary",), vmem_limit_bytes=32 << 20
        ),
        cost_estimate=pl.CostEstimate(
            flops=rows * width * size * 1200 // 100, bytes_accessed=rows * width, transcendentals=0
        ),
        name="spread",
    )(grads, weights)


def heads_grad_kernel(pieces, heads, grads, out):
    made = mm(heads[0], grads[...], TN).astype(BF16)
    tall = made.shape[0] // out.shape[2]
    low = tall // pieces
    for j in range(out.shape[2]):
        for s in range(pieces):
            out[s, 0, j, 0] = made[j * tall + s * low : j * tall + (s + 1) * low]


def heads_grad_call(heads, grads, cores, shards):
    count, rows, chans = heads.shape
    width = grads.shape[1]
    size = chans // shards
    chips = count // cores
    shape = (count, cores, shards, chips, size // count, width)
    return pl.pallas_call(
        functools.partial(heads_grad_kernel, count),
        grid=(count,),
        in_specs=[
            pl.BlockSpec((1, rows, chans), lambda s: (s, 0, 0)),
            pl.BlockSpec(grads.shape, lambda s: (0, 0)),
        ],
        out_specs=pl.BlockSpec(
            (count, 1, shards, 1, size // count, width),
            lambda s: (0, lax.rem(s, cores), 0, lax.div(s, cores), 0, 0),
        ),
        out_shape=jax.ShapeDtypeStruct(shape, BF16),
        compiler_params=pltpu.CompilerParams(
            dimension_semantics=("arbitrary",), vmem_limit_bytes=32 << 20
        ),
        cost_estimate=pl.CostEstimate(
            flops=rows * width * size * 1200 // 100, bytes_accessed=rows * width, transcendentals=0
        ),
        name="mix_out_grad",
    )(heads, grads)


def outer_kernel(count, place, *refs):
    *inputs, out, total, left, right, sems = refs
    lefts, rights = inputs[:count], inputs[count:]
    if len(rights) < count:
        rights = [rights[0].at[k] for k in range(count)]
    step = pl.program_id(0)

    def fetch(block, slot):
        return (
            pltpu.make_async_copy(lefts[block], left.at[slot], sems.at[0, slot]),
            pltpu.make_async_copy(rights[block], right.at[slot], sems.at[1, slot]),
        )

    @pl.when(step == 0)
    def _():
        for copy in fetch(0, 0):
            copy.start()

    slot = lax.rem(step, 2)
    for block in range(1, count):

        @pl.when(step + 1 == block)
        def _(block=block):
            for copy in fetch(block, block % 2):
                copy.start()

    for copy in fetch(0, slot):
        copy.wait()

    @pl.when(step == 0)
    def _():
        total[...] = mm(left[0], right[0], TN)

    @pl.when(step > 0)
    def _():
        total[...] += mm(left[slot], right[slot], TN)

    @pl.when(step == count - 1)
    def _():
        place(out, total)


def outer_call(lefts, rights, shape, place, name):
    count = len(lefts)
    rows, m = lefts[0].shape
    n = rights[0].shape[-1]
    return pl.pallas_call(
        functools.partial(outer_kernel, count, place),
        grid=(count,),
        in_specs=[pl.BlockSpec(memory_space=pl.ANY)] * (count + len(rights)),
        out_specs=pl.BlockSpec(shape, lambda i: (0,) * len(shape), pipeline_mode=pl.Buffered(1)),
        out_shape=jax.ShapeDtypeStruct(shape, BF16),
        scratch_shapes=[
            pltpu.VMEM((m, n), F32),
            pltpu.VMEM((2, rows, m), BF16),
            pltpu.VMEM((2, rows, n), BF16),
            pltpu.SemaphoreType.DMA((2, 2)),
        ],
        compiler_params=pltpu.CompilerParams(
            dimension_semantics=("arbitrary",), vmem_limit_bytes=58 << 20
        ),
        cost_estimate=pl.CostEstimate(
            flops=count * rows * m * n * 75 // 100,
            bytes_accessed=rows * (m + n),
            transcendentals=0,
        ),
        name=name,
    )(*lefts, *rights)


def swap(value, across):
    return lax.ppermute(value, "seq", [(i, i ^ across) for i in range(lax.axis_size("seq"))])


CORE, XLINK, YLINK = 1, 2, 4
TILE = 128


def together(*values):
    return lax.optimization_barrier(values)


def plane_gather(own, beside=None, meet=None):
    half = own.shape[0] // 2
    got = {0: own, XLINK: swap(own, XLINK), YLINK: swap(own, YLINK), CORE: swap(own, CORE)}
    got, beside = together(got, beside)
    first = swap(got[YLINK][:half], XLINK)
    second = swap(got[XLINK][half:], YLINK)
    got[XLINK + CORE] = swap(got[XLINK], CORE)
    got[YLINK + CORE] = swap(got[YLINK], CORE)
    first, second, got, meet = together(first, second, got, meet)
    got[XLINK + YLINK] = jnp.concatenate([first, second])
    got[XLINK + YLINK + CORE] = jnp.concatenate([swap(first, CORE), swap(second, CORE)])
    return got, beside, meet


def add_low(a, b):
    return (a.astype(F32) + b.astype(F32)).astype(BF16)


def chip_sum(parts, a):
    return add_low(parts[a], swap(parts[a ^ CORE], CORE))


def first_hops(chip):
    half = chip[0].shape[0] // 2
    return (
        swap(chip[2][:half], XLINK),
        swap(chip[4][half:], YLINK),
        swap(chip[6][:half], XLINK),
        swap(chip[6][half:], YLINK),
    )


def turned(chip, hops):
    half = chip[4].shape[0] // 2
    return add_low(chip[4][:half], hops[2]), add_low(chip[2][half:], hops[3])


def last_hops(pair):
    return swap(pair[0], YLINK), swap(pair[1], XLINK)


def arrived(chip, hops, lasts):
    half = chip[0].shape[0] // 2
    low = chip[0][:half].astype(F32) + hops[0].astype(F32) + lasts[0].astype(F32)
    high = chip[0][half:].astype(F32) + hops[1].astype(F32) + lasts[1].astype(F32)
    return jnp.concatenate([low, high])


def pick(array, index, axis):
    return lax.dynamic_index_in_dim(array, index, axis, keepdims=False)


def plane_device(
    tokens,
    norm1_gain,
    w_mix_in,
    forget_gap,
    group_gain,
    w_mix_out,
    norm2_gain,
    w_gate_up,
    w_down,
    doc_lengths,
    out_cotangent,
):
    seq_count, mp_count = lax.axis_size("seq"), lax.axis_size("mp")
    seq_index, mp_index = lax.axis_index("seq"), lax.axis_index("mp")
    core, chip = seq_index % 2, seq_index // 2
    chips = seq_count // 2
    span, packs, width = tokens.shape
    rows = span * packs
    run = span * mp_count
    all_heads, head_size, _ = w_mix_out.shape
    heads = all_heads // seq_count
    chans = heads * head_size
    slice_d = width // seq_count

    def pack_major(array):
        return jnp.transpose(array, (1, 0, 2)).reshape(rows, width)

    def token_major(array):
        return jnp.transpose(array.reshape(packs, span, width), (1, 0, 2))

    def gather_shares(part):
        return lax.all_gather(part, "mp", axis=0).reshape((2, 2) + part.shape)

    def both_halves(pairs):
        mine = pick(pairs, core, 0)
        other = swap(pick(pairs, 1 - core, 0), CORE)
        return jnp.where(core == 0, mine, other), jnp.where(core == 0, other, mine)

    in_part = lax.dynamic_slice(
        w_mix_in, (0, 2 * core, chip * head_size), (width, 2, head_size)
    ).reshape(width, 2 * head_size)
    in_pairs = gather_shares(in_part)

    own = pack_major(tokens)
    scale_one = rms_scale(own)
    normed_own = (own * scale_one * norm1_gain).astype(BF16)

    small = pick(jnp.stack([forget_gap, group_gain]), chip, 1)[None]
    for bit in range(2):
        across = 1 << bit
        other = lax.ppermute(small, "mp", [(i, i ^ across) for i in range(mp_count)])
        low = (mp_index >> bit) % 2 == 0
        small = jnp.concatenate([jnp.where(low, small, other), jnp.where(low, other, small)])

    hidden_units = w_gate_up.shape[2]
    share = -(-hidden_units // (chips * TILE)) * TILE
    local_ff = 2 * share
    spare = share * chips - hidden_units
    begin = jnp.minimum(chip * share, hidden_units - share)
    gu_part = lax.dynamic_slice_in_dim(pick(w_gate_up, core, 1), begin, share, 1)
    dn_part = lax.dynamic_slice_in_dim(w_down, begin, share, 0)
    fresh = lax.broadcasted_iota(jnp.int32, (share, 1), 0) >= chip * share - begin
    dn_part = jnp.where(fresh, dn_part, jnp.zeros_like(dn_part))
    dn_part = lax.dynamic_slice_in_dim(dn_part, core * (share // 2), share // 2, 0)
    out_flat = w_mix_out.reshape(-1, width)
    normed, (gu_part, dn_part, small), in_pairs = plane_gather(
        normed_own, (gu_part, dn_part, small), in_pairs
    )
    gu_first, gu_second = gu_part[: width // 2], gu_part[width // 2 :]
    query_forget, value_gate = both_halves(in_pairs)
    w_in = jnp.concatenate(
        [
            part[j, :, k * head_size : (k + 1) * head_size]
            for part, k in ((query_forget, 1), (value_gate, 0), (query_forget, 0), (value_gate, 1))
            for j in range(2)
        ],
        axis=1,
    )

    cot_own = pack_major(lax.dynamic_slice_in_dim(out_cotangent, mp_index * span, span, 0))
    cot_low, gu_first, dn_part, _ = together(cot_own.astype(BF16), gu_first, dn_part, in_pairs)

    dn_pairs = gather_shares(dn_part)
    first_pairs = gather_shares(gu_first)

    small = pick(small.reshape(2, 2, 2, head_size), core, 0)
    gap_row, gain_row = small[:, 0].reshape(1, chans), small[:, 1].reshape(1, chans)

    projected = None
    for a in range(0, seq_count, 2):
        projected = project_call(projected, a, seq_count, normed[a], normed[a + 1], w_in)
    projected = projected.reshape(seq_count, packs, span, 4 * chans)

    halves = span // BLOCK
    steps = seq_count * halves
    where = jnp.stack([seq_index, run, mp_index * span, halves]).astype(jnp.int32)
    block = (1, packs, BLOCK, chans)
    fv_block = (1, packs, BLOCK, 2 * chans)
    wide = (1, packs, BLOCK, 4 * chans)
    pairs = packs * heads
    runs_shape = (packs, seq_count, heads, head_size, head_size)
    run_block = (packs, 1, heads, head_size, head_size)
    tall_shape = (packs, seq_count, heads, head_size + 8, head_size)
    tall_block = (packs, 1, heads, head_size + 8, head_size)
    unit = 2 * BLOCK * head_size * head_size * pairs * steps
    common = [(doc_lengths, "smem", None), (gap_row, "whole", None)]
    call = functools.partial(recur_call, steps=steps, halves=halves, where=where)

    def to_scan(array):
        array = jnp.transpose(array, (0, 2, 1, 3, 4)).astype(BF16)
        array = array.reshape((pairs,) + array.shape[2:])
        return lax.all_to_all(array, "mp", split_axis=0, concat_axis=0, tiled=True)

    def from_scan(array):
        array = lax.all_to_all(array, "mp", split_axis=0, concat_axis=0, tiled=True)
        array = array.reshape((packs, heads) + array.shape[1:])
        return jnp.transpose(array, (0, 2, 1, 3, 4))

    [run_state] = call(
        states_kernel,
        reverse=False,
        ins=common + [(projected, "near", fv_block)],
        outs=[(tall_shape, F32, "run", tall_block)],
        scratch=[],
        flops=17 * unit,
        name="run_states",
    )
    cot, run_state, _ = plane_gather(cot_low, run_state)
    decays = to_scan(run_state)
    entering = from_scan(scan_call(decays, decays, False))
    row_shape = (seq_count, packs, span, chans)
    state_shape = (packs, heads, head_size, head_size)
    heads_out, mixed, kept = call(
        forward_kernel,
        reverse=False,
        ins=common
        + [(gain_row, "whole", None), (projected, "near", wide), (entering, "run", run_block)],
        outs=[
            (row_shape, BF16, "rows", block),
            (row_shape, F32, "rows", block),
            ((steps,) + state_shape, F32, "block", (1,) + state_shape),
        ],
        scratch=[pltpu.VMEM(state_shape, F32)],
        flops=28 * unit,
        name="mix_forward",
    )
    gu_second, dn_pairs, first_pairs, cot, _ = together(
        gu_second, dn_pairs, first_pairs, cot, entering
    )
    second_pairs = gather_shares(gu_second)

    def side_by_side(pairs):
        gate, up = both_halves(pairs)
        return jnp.concatenate([gate[0], gate[1], up[0], up[1]], axis=1)

    w_dn = jnp.concatenate(both_halves(dn_pairs), axis=1).reshape(local_ff, width)
    w_low, w_high = side_by_side(first_pairs), side_by_side(second_pairs)

    split = (chips, 2, rows, 2, head_size)
    heads_by = lax.all_to_all(
        heads_out.reshape(seq_count, rows, chans), "seq", split_axis=0, concat_axis=0, tiled=True
    )
    heads_tok = jnp.transpose(heads_by.reshape(split), (2, 1, 3, 0, 4)).reshape(rows, -1)
    hidden = own + mm(heads_tok, out_flat)
    scale_two = rms_scale(hidden)
    normed_two = (hidden * scale_two * norm2_gain).astype(BF16)

    def ready(parts):
        mine = pick(parts, core, 0)
        other = swap(pick(parts, 1 - core, 0), CORE)
        low = jnp.where(core == 0, mine, other)
        high = jnp.where(core == 0, other, mine)
        return jnp.concatenate([low, high])

    def deliver(terms):
        return lax.psum_scatter(terms, "mp", scatter_dimension=0, tiled=True)[0]

    def handed(piece):
        groups = [list(range(k, seq_count, 2)) for k in range(2)]
        return lax.all_to_all(
            piece, "seq", split_axis=0, concat_axis=0, axis_index_groups=groups, tiled=True
        )

    act, grad_gu, down_parts, back_parts = {}, {}, {}, {}
    order = range(seq_count)

    def feed(a):
        made = feed_call((two[a], two[a + 1]), (cot[a], cot[a + 1]), w_low, w_high, w_dn)
        for k, at in enumerate((a, a + 1)):
            act[at], grad_gu[at], down_parts[at], back_parts[at] = made[4 * k : 4 * k + 4]

    two = {0: normed_two}
    for across in (CORE, XLINK, YLINK):
        two[across] = swap(normed_two, across)
    feed(0)
    two[XLINK], two[YLINK], down_parts[0] = together(two[XLINK], two[YLINK], down_parts[0])
    middle = rows // 2
    far_first = swap(two[YLINK][:middle], XLINK)
    far_second = swap(two[XLINK][middle:], YLINK)
    two[3], two[5] = swap(two[XLINK], CORE), swap(two[YLINK], CORE)
    feed(2)
    two[YLINK], down_parts[2] = together(two[YLINK], down_parts[2])
    feed(4)
    chip_back = {2: chip_sum(back_parts, 2)}
    far_first, far_second, chip_back, down_parts[4] = together(
        far_first, far_second, chip_back, down_parts[4]
    )
    two[6] = jnp.concatenate([far_first, far_second])
    two[7] = jnp.concatenate([swap(far_first, CORE), swap(far_second, CORE)])
    other = swap(back_parts[5], CORE)
    feed(6)
    other, back_parts = together(other, back_parts)
    chip_back[4] = add_low(back_parts[4], other)
    chip_back[6] = chip_sum(back_parts, 6)

    def place_gu(out, total):
        for d in range(seq_count):
            for j in range(2):
                for g in range(2):
                    at = (2 * g + j) * share
                    out[d % 2, j, d // 2, g] = total[
                        d * slice_d : (d + 1) * slice_d, at : at + share
                    ].astype(BF16)

    def place_dn(out, total):
        for d in range(seq_count):
            for j in range(2):
                out[d % 2, j, d // 2] = total[
                    j * share : (j + 1) * share, d * slice_d : (d + 1) * slice_d
                ].astype(BF16)

    chip_back, grad_gu = together(chip_back, grad_gu)
    gu_grad = outer_call(
        [two[a] for a in order],
        [grad_gu[a] for a in order],
        (2, 2, chips, 2, slice_d, share),
        place_gu,
        "gate_up_grad",
    )
    chip_back[0] = chip_sum(back_parts, 0)
    hops, chip_back, gu_grad = together(first_hops(chip_back), chip_back, gu_grad)
    onward, act = together(turned(chip_back, hops), act)
    dn_grad = outer_call(
        [act[a] for a in order],
        [cot[a] for a in order],
        (2, 2, chips, share, slice_d),
        place_dn,
        "down_grad",
    )
    lasts, dn_grad = together(last_hops(onward), dn_grad)
    grad_normed_two = arrived(chip_back, hops, lasts)
    grad_normed_two, down_parts = together(grad_normed_two, down_parts)

    norm2_part = jnp.sum(grad_normed_two * hidden * scale_two, axis=0)
    grad_hidden = cot_own + rms_back(grad_normed_two, hidden, scale_two, norm2_gain)
    grad_mix = grad_hidden.astype(BF16)
    grad_tok = spread_call(grad_mix, w_mix_out.reshape(2, 2, chips, head_size, width))
    grad_tok, dn_grad = together(grad_tok, ready(dn_grad))
    dn_grad = deliver(dn_grad)
    grad_heads = lax.all_to_all(grad_tok, "seq", split_axis=0, concat_axis=0, tiled=True)
    chip_down = {a: chip_sum(down_parts, a) for a in (2, 4, 6, 0)}
    out_grad = heads_grad_call(heads_by, grad_mix, 2, 2)
    grad_heads, chip_down, out_grad = together(
        grad_heads.reshape(row_shape), chip_down, out_grad
    )

    grad_out, grad_gate, group_part, run_grad = call(
        gate_back_kernel,
        reverse=True,
        ins=common
        + [
            (gain_row, "whole", None),
            (projected, "near", wide),
            (mixed, "rows", block),
            (grad_heads, "rows", block),
        ],
        outs=[
            (row_shape, F32, "rows", block),
            (row_shape, BF16, "rows", block),
            ((1, chans), F32, "whole", None),
            (runs_shape, BF16, "run", run_block),
        ],
        scratch=[pltpu.VMEM(state_shape, F32)],
        flops=22 * unit,
        name="gate_back",
    )
    out_grad = out_grad.reshape(seq_count, all_heads, head_size // seq_count, width)
    out_parts = {a: pick(out_grad, seq_index ^ a, 0) for a in range(seq_count)}
    chip_out = {a: chip_sum(out_parts, a) for a in (2, 4, 6, 0)}
    run_grad, chip_out = together(to_scan(run_grad), chip_out)
    entering_back = from_scan(scan_call(decays, run_grad, True))
    hops_down = first_hops(chip_down)
    entering_back, gu_grad = together(entering_back, ready(gu_grad))
    gu_grad = deliver(gu_grad)
    grad_projected, gap_part = call(
        backward_kernel,
        reverse=True,
        ins=common
        + [
            (projected, "near", wide),
            (grad_out, "rows", block),
            (grad_gate, "rows", block),
            (kept, "block", (1,) + state_shape),
            (entering_back, "run", run_block),
        ],
        outs=[
            ((seq_count, packs, span, 4 * chans), BF16, "near", wide),
            ((1, chans), F32, "whole", None),
        ],
        scratch=[pltpu.VMEM(state_shape, F32)],
        flops=43 * unit,
        name="mix_backward",
    )
    grad_projected = grad_projected.reshape(seq_count, rows, 4 * chans)
    grad_projected, dn_grad, hops_down = together(grad_projected, dn_grad, hops_down)
    dn_round = handed(dn_grad)
    lasts_down = last_hops(turned(chip_down, hops_down))
    chip_out = together(chip_out, grad_projected)[0]
    hops_out = first_hops(chip_out)
    def place_in(out, total):
        for d in range(seq_count):
            for j in range(2):
                for k, of in enumerate((2, 0, 1, 3)):
                    at = of * chans + j * head_size
                    out[d % 2, j, d // 2, :, k * head_size : (k + 1) * head_size] = total[
                        d * slice_d : (d + 1) * slice_d, at : at + head_size
                    ].astype(BF16)

    in_grad = outer_call(
        [normed[a] for a in order],
        [grad_projected],
        (2, 2, chips, slice_d, 4 * head_size),
        place_in,
        "mix_in_grad",
    )
    grad_projected, in_grad, lasts_down, dn_round = together(
        grad_projected, in_grad, lasts_down, dn_round
    )
    layer_out = token_major(hidden + arrived(chip_down, hops_down, lasts_down))
    in_parts, chip_in = {}, {}

    def back(a):
        in_parts[a], in_parts[a + 1], part = back_call(
            grad_projected, a, normed[a], normed[a + 1], w_in
        )
        return part

    def from_core(a):
        return swap(in_parts[a + 1], CORE)

    half = rows // 2
    in_mine = pick(in_grad, core, 0)
    in_other = swap(pick(in_grad, 1 - core, 0), CORE)
    norm1_part = back(6)
    grad_projected, in_mine, in_other, hops_out, in_parts = together(
        grad_projected, in_mine, in_other, hops_out, in_parts
    )
    lasts_out = last_hops(turned(chip_out, hops_out))
    in_grad = jnp.concatenate(
        [jnp.where(core == 0, in_mine, in_other), jnp.where(core == 0, in_other, in_mine)]
    )
    other = from_core(6)
    norm1_part = norm1_part + back(2)
    grad_projected, lasts_out, other, in_parts, in_grad, gu_grad = together(
        grad_projected, lasts_out, other, in_parts, in_grad, gu_grad
    )
    in_grad = deliver(in_grad)
    chip_in[6] = add_low(in_parts[6], other)
    far_hops = swap(chip_in[6][:half], XLINK), swap(chip_in[6][half:], YLINK)
    out_grad = arrived(chip_out, hops_out, lasts_out).astype(BF16)
    out_grad = out_grad.reshape((mp_count, all_heads // mp_count) + out_grad.shape[1:])
    other = from_core(2)
    norm1_part = norm1_part + back(4)
    grad_projected, other, in_parts = together(grad_projected, other, in_parts)
    chip_in[2] = add_low(in_parts[2], other)
    mine_x = swap(chip_in[2][:half], XLINK)
    other = from_core(4)
    norm1_part = norm1_part + back(0)
    def set_heads(part):
        row = jnp.zeros((2, 2, chips, head_size), F32)
        mine = part.reshape(1, 2, 1, head_size)
        row = lax.dynamic_update_slice(row, mine, (core, 0, chip, 0))
        row = row.reshape(mp_count, all_heads // mp_count, seq_count, head_size // seq_count)
        return jnp.transpose(row, (2, 0, 1, 3)).reshape(-1)

    gains = jnp.stack(
        [norm1_part[0] / norm1_gain, norm2_part, set_heads(gap_part), set_heads(group_part)]
    )
    gains = jnp.transpose(gains.reshape(4, seq_count, width // seq_count), (1, 0, 2))
    far_hops, other, in_parts, chip_in, gu_round, gains, out_grad = together(
        far_hops, other, in_parts, chip_in, handed(gu_grad), gains, out_grad
    )
    out_grad = lax.psum_scatter(out_grad, "mp", scatter_dimension=0, tiled=True)[0]
    chip_in[4] = add_low(in_parts[4], other)
    hops = mine_x, swap(chip_in[4][half:], YLINK)
    lasts = last_hops(turned(chip_in, (None, None) + far_hops))
    chip_in[0] = chip_sum(in_parts, 0)
    gains = jnp.sum(lax.all_to_all(gains, "seq", split_axis=0, concat_axis=0, tiled=True), axis=0)
    gains = jnp.transpose(gains.reshape(4, mp_count, -1), (1, 0, 2))
    hops, lasts, chip_in, layer_out, gains = together(hops, lasts, chip_in, layer_out, gains)
    gains = jnp.sum(lax.all_to_all(gains, "mp", split_axis=0, concat_axis=0, tiled=True), axis=0)
    grad_normed = arrived(chip_in, hops, lasts)
    got = [gu_round[c].astype(F32) for c in range(chips)]
    got[-1] = got[-1][:, :, spare:]
    gate_up_grad = jnp.transpose(jnp.concatenate(got, axis=-1), (1, 0, 2))
    got = [dn_round[c] for c in range(chips)]
    got[-1] = got[-1][spare:]
    down_grad = jnp.concatenate(got, axis=0).astype(F32)
    mix_out_grad = out_grad.astype(F32)
    in_round = handed(in_grad)
    got = [in_round[c].astype(F32).reshape(slice_d, 4, head_size) for c in range(chips)]
    mix_in_grad = jnp.concatenate(got, axis=-1)

    tokens_grad = token_major(
        grad_hidden + rms_back(grad_normed, own, scale_one, norm1_gain)
    )

    small = gains[2:].reshape(2, all_heads // mp_count, head_size // seq_count)
    return (
        layer_out,
        tokens_grad,
        gains[0],
        mix_in_grad,
        small[0],
        small[1],
        mix_out_grad,
        gains[1],
        gate_up_grad,
        down_grad,
    )


def solution(mesh):
    body = plane_device if dict(mesh.shape) == {"seq": 8, "mp": 4} else generic_device
    placed = (
        P(("seq", "mp"), None, None),
        P(),
        P(None, None, "mp"),
        P("mp", None),
        P("mp", None),
        P(),
        P(),
        P(None, None, "mp"),
        P("mp", None),
        P(),
        P("seq", None, None),
    )
    return jax.shard_map(
        body,
        mesh=mesh,
        in_specs=placed,
        out_specs=(
            P(("seq", "mp"), None, None),
            P(("seq", "mp"), None, None),
            P(("seq", "mp")),
            P("seq", None, "mp"),
            P("mp", "seq"),
            P("mp", "seq"),
            P("mp", "seq", None),
            P(("seq", "mp")),
            P("seq", None, "mp"),
            P("mp", "seq"),
        ),
        check_vma=False,
    )
```
